32 devices in a mesh: row: 8 (over z, x), col: 4 (over y, core).
Axes of the slice: x: 2, y: 2, z: 4, core: 2. Of those that a mesh axis runs over, the one named last changes fastest.
Arguments:
- tokens: bfloat16 [16384, 768], P(('row', 'col')), may hold values from -6 to 6
- cotangent: bfloat16 [16384, 768], P(('row', 'col')), may hold values from -6 to 6
- lengths: int32 [8], P('row'), may hold values from 512 to 2048, as said below
- w_qkv: float32 [768, 2304], P('row', 'col'), may hold values from -0.21875 to 0.21875
- w_out: float32 [768, 768], P('col', 'row'), may hold values from -2.5 to 2.5
- w_gate: float32 [768, 3072], P('row', 'col'), may hold values from -0.21875 to 0.21875
- w_up: float32 [768, 3072], P('row', 'col'), may hold values from -0.21875 to 0.21875
- w_down: float32 [3072, 768], P('col', 'row'), may hold values from -0.109375 to 0.109375
- norm_params: float32 [4, 768], replicated, may hold values from -0.5 to 1.5, as said below
- m_qkv: float32 [768, 2304], P('row', 'col'), may hold values from -32 to 32
- v_qkv: float32 [768, 2304], P('row', 'col'), may hold values from 2.56 to 10.24
- m_out: float32 [768, 768], P('col', 'row'), may hold values from -2 to 2
- v_out: float32 [768, 768], P('col', 'row'), may hold values from 0.0085 to 0.034
- m_gate: float32 [768, 3072], P('row', 'col'), may hold values from -20 to 20
- v_gate: float32 [768, 3072], P('row', 'col'), may hold values from 0.9216 to 3.6864
- m_up: float32 [768, 3072], P('row', 'col'), may hold values from -20 to 20
- v_up: float32 [768, 3072], P('row', 'col'), may hold values from 0.9216 to 3.6864
- m_down: float32 [3072, 768], P('col', 'row'), may hold values from -20 to 20
- v_down: float32 [3072, 768], P('col', 'row'), may hold values from 0.9216 to 3.6864
- m_norm: float32 [4, 768], replicated, may hold values from -56 to 56
- v_norm: float32 [4, 768], replicated, may hold values from 6.5536 to 26.2144
Outputs:
- layer_out: bfloat16 [16384, 768], P(('row', 'col'))
- grad_tokens: float32 [16384, 768], P(('row', 'col'))
- residual_rms: float32 [], replicated
- new_qkv: float32 [768, 2304], P('row', 'col')
- first_qkv: float32 [768, 2304], P('row', 'col')
- second_qkv: float32 [768, 2304], P('row', 'col')
- copy_qkv: bfloat16 [768, 2304], P('row', 'col')
- new_out: float32 [768, 768], P('col', 'row')
- first_out: float32 [768, 768], P('col', 'row')
- second_out: float32 [768, 768], P('col', 'row')
- copy_out: bfloat16 [768, 768], P('col', 'row')
- new_gate: float32 [768, 3072], P('row', 'col')
- first_gate: float32 [768, 3072], P('row', 'col')
- second_gate: float32 [768, 3072], P('row', 'col')
- copy_gate: bfloat16 [768, 3072], P('row', 'col')
- new_up: float32 [768, 3072], P('row', 'col')
- first_up: float32 [768, 3072], P('row', 'col')
- second_up: float32 [768, 3072], P('row', 'col')
- copy_up: bfloat16 [768, 3072], P('row', 'col')
- new_down: float32 [3072, 768], P('col', 'row')
- first_down: float32 [3072, 768], P('col', 'row')
- second_down: float32 [3072, 768], P('col', 'row')
- copy_down: bfloat16 [3072, 768], P('col', 'row')
- new_norm: float32 [4, 768], replicated
- first_norm: float32 [4, 768], replicated
- second_norm: float32 [4, 768], replicated
The draws below stay inside these ranges and needn't reach their ends.
Inputs may be any that keep to these rules, and one draw needn't show every extreme that they name: `lengths`: the first slot holds 512 valid tokens and the last slot 2048. `norm_params`: gains lie in rows 0 and 2 and are positive; biases lie in rows 1 and 3.
All inputs are finite; a program needn't handle non-finite values.
Results may differ from the reference program's by a relative error of at most 0.02.
The reference program's roundings to bfloat16 on the way count: a program that leaves them out, or rounds other values in their place, can miss the bound.
Values may be sent and summed in bfloat16 or wider, within the bound.
No kernel may reach another device: no remote copies, remote signals or barrier semaphores. Data moves between devices by JAX's collectives and lax.ppermute only.
A program may use at most 128 MiB of HBM per device.

```python
import math
import jax
import jax.numpy as jnp
from jax import lax

D = 768
H = 12
HD = 64
FF = 3072
SEQ = 2048
STEP = 10
SLOTS = 8
TOKENS = 16384
N_ROW = 8


def draw_lengths(key, part):
    key = jax.random.fold_in(key, 11)
    lowest = SEQ // 4
    step_draw = jax.random.randint(key, (SLOTS,), 0, 8)
    slot_index = jnp.arange(SLOTS, dtype=jnp.int32)
    raw_length = lowest + (SEQ - lowest) * (slot_index * 8 + step_draw) // (SLOTS * 8)
    raw_length = jnp.where(slot_index == 0, lowest, raw_length)
    return jnp.where(slot_index == SLOTS - 1, SEQ, raw_length).astype(jnp.int32)


def draw_norm_params(key, part):
    key = jax.random.fold_in(key, 23)
    key_gain, key_shift = jax.random.split(key)
    place_frac = jnp.arange(D, dtype=jnp.float32) / D
    trend_line = 0.6 + 0.6 * place_frac
    wobble = jax.random.uniform(key_gain, (2, D), minval=0.8, maxval=1.2)
    gain_rows = trend_line[None, :] * wobble
    shifts = jax.random.uniform(key_shift, (2, D), minval=-0.5, maxval=0.5)
    return jnp.stack([gain_rows[0], shifts[0], gain_rows[1], shifts[1]]).astype(jnp.float32)


def steps_of(own_key, extent, pieces, low, high):
    loudness, own = 1.0, jax.random.fold_in(own_key, 6)
    for dim, parts in pieces:
        steps = jnp.exp(jax.random.uniform(jax.random.fold_in(own, dim), (parts,), jnp.float32, low / len(pieces), high / len(pieces)))
        loudness = loudness * jnp.repeat(steps, extent[dim] // parts).reshape([-1 if axis == dim else 1 for axis in range(len(extent))])
    return loudness


def noise(rng, extent, width, reach, pieces=(), held_as=jnp.bfloat16):
    loudness = steps_of(rng, extent, pieces, -0.22, 0.18) if pieces else 1.0
    values = jax.random.normal(rng, extent, jnp.float32) * width * loudness
    return jnp.minimum(jnp.maximum(values, -reach), reach).astype(held_as)


def setup_inputs(seed: int = 0) -> dict:
    key_list = jax.random.split(jax.random.key(seed), 22)
    return {
        "tokens": noise(key_list[0], (TOKENS, D), 1.0, 6.0, ((0, 32),)),
        "cotangent": noise(key_list[1], (TOKENS, D), 1.0, 6.0, ((0, 32),)),
        "lengths": draw_lengths(jax.random.fold_in(key_list[21], 71), 0),
        "w_qkv": noise(key_list[3], (D, 3 * D), D ** -0.5, 0.21875, ((0, 8), (1, 4)), jnp.float32),
        "w_out": noise(key_list[4], (D, D), (D * 16 // SEQ) ** -0.5, 2.5, ((0, 4), (1, 8)), jnp.float32),
        "w_gate": noise(key_list[5], (D, FF), D ** -0.5, 0.21875, ((0, 8), (1, 4)), jnp.float32),
        "w_up": noise(key_list[6], (D, FF), D ** -0.5, 0.21875, ((0, 8), (1, 4)), jnp.float32),
        "w_down": noise(key_list[7], (FF, D), FF ** -0.5, 0.109375, ((0, 4), (1, 8)), jnp.float32),
        "norm_params": draw_norm_params(jax.random.fold_in(key_list[21], 71), 0),
        "m_qkv": noise(key_list[9], (D, 3 * D), (0.055 * (SEQ * N_ROW * 5 // 8) ** 0.5), 32.0, ((0, 8), (1, 4)), jnp.float32),
        "v_qkv": jnp.clip(jnp.exp(math.log(10.24) - 1.3862944 * jax.random.uniform(key_list[10], (D, 3 * D), jnp.float32) ** steps_of(key_list[10], (D, 3 * D), ((0, 8), (1, 4)), -0.2, 0.2)), 2.56, 10.24),
        "m_out": noise(key_list[11], (D, D), (0.14 * (N_ROW * 5 // 8) ** 0.5), 2.0, ((0, 4), (1, 8)), jnp.float32),
        "v_out": jnp.clip(jnp.exp(math.log(0.034) - 1.3862944 * jax.random.uniform(key_list[12], (D, D), jnp.float32) ** steps_of(key_list[12], (D, D), ((0, 4), (1, 8)), -0.2, 0.2)), 0.0085, 0.034),
        "m_gate": noise(key_list[13], (D, FF), (0.033 * (SEQ * N_ROW * 5 // 8) ** 0.5), 20.0, ((0, 8), (1, 4)), jnp.float32),
        "v_gate": jnp.clip(jnp.exp(math.log(3.6864) - 1.3862944 * jax.random.uniform(key_list[14], (D, FF), jnp.float32) ** steps_of(key_list[14], (D, FF), ((0, 8), (1, 4)), -0.2, 0.2)), 0.9216, 3.6864),
        "m_up": noise(key_list[15], (D, FF), (0.033 * (SEQ * N_ROW * 5 // 8) ** 0.5), 20.0, ((0, 8), (1, 4)), jnp.float32),
        "v_up": jnp.clip(jnp.exp(math.log(3.6864) - 1.3862944 * jax.random.uniform(key_list[16], (D, FF), jnp.float32) ** steps_of(key_list[16], (D, FF), ((0, 8), (1, 4)), -0.2, 0.2)), 0.9216, 3.6864),
        "m_down": noise(key_list[17], (FF, D), (0.033 * (SEQ * N_ROW * 5 // 8) ** 0.5), 20.0, ((0, 4), (1, 8)), jnp.float32),
        "v_down": jnp.clip(jnp.exp(math.log(3.6864) - 1.3862944 * jax.random.uniform(key_list[18], (FF, D), jnp.float32) ** steps_of(key_list[18], (FF, D), ((0, 4), (1, 8)), -0.2, 0.2)), 0.9216, 3.6864),
        "m_norm": noise(key_list[19], (4, D), (0.088 * (SEQ * N_ROW * 5 // 8) ** 0.5), 56.0, (), jnp.float32),
        "v_norm": jnp.clip(jnp.exp(jax.random.uniform(key_list[20], (4, D), jnp.float32, math.log(6.5536), math.log(26.2144))), 6.5536, 26.2144),
    }


FIRST_DECAY = 0.9
SECOND_DECAY = 0.999
ADAM_EPSILON = 1e-08
NORM_EPSILON = 1e-05
ROPE_BASE = 1000.0
MATRIX_DECAY = 0.01
NORM_RATE = 0.4
HIGHEST_PRECISION = lax.Precision.HIGHEST

@jax.custom_vjp
def low(v):
    return lax.optimization_barrier(v.astype(jnp.bfloat16)).astype(jnp.float32)

@jax.custom_vjp
def low_back(v):
    return v

def low_keep(v):
    return (low(v), None)

def low_pass(kept, grad):
    return (grad,)

def back_keep(v):
    return (v, None)

def back_low(kept, grad):
    return (low(grad),)
low.defvjp(low_keep, low_pass)
low_back.defvjp(back_keep, back_low)

def rope_tables(length):
    position = jnp.arange(length, dtype=jnp.float32)
    index_half = jnp.arange(HD // 2, dtype=jnp.float32)
    inverse = jnp.exp(index_half * (-2.0 * math.log(ROPE_BASE) / HD))
    angle_table = position[:, None] * inverse[None, :]
    return (jnp.cos(angle_table), jnp.sin(angle_table))

def rotate(values_in, cosine_table, sine_table):
    half_width = values_in.shape[-1] // 2
    front_half = values_in[..., :half_width]
    behind = values_in[..., half_width:]
    cos_wide = cosine_table[:, None, :]
    sin_wide = sine_table[:, None, :]
    return jnp.concatenate([front_half * cos_wide - behind * sin_wide, behind * cos_wide + front_half * sin_wide], axis=-1)

def layer_norm(hidden_in, gain_row, shift_row):
    centre = lax.optimization_barrier(jnp.mean(hidden_in, axis=-1, keepdims=True))
    spread = lax.optimization_barrier(jnp.mean((hidden_in - centre) ** 2, axis=-1, keepdims=True))
    return (hidden_in - centre) * lax.rsqrt(spread + NORM_EPSILON) * gain_row + shift_row

def layer(tokens_in, w_qkv, w_out, w_gate, w_up, w_down, norm_params, key_mask):
    cosine_table, sine_table = rope_tables(SEQ)
    score_scale = 1.0 / math.sqrt(HD)
    mixed_rows = low_back(jnp.dot(tokens_in, low(w_qkv), precision=HIGHEST_PRECISION))
    mixed_rows = mixed_rows.reshape(SEQ, H, 3, HD)
    query_rows = low(rotate(mixed_rows[:, :, 0], cosine_table, sine_table))
    key_rows = low(rotate(mixed_rows[:, :, 1], cosine_table, sine_table))
    value_rows = low(mixed_rows[:, :, 2])
    block_rows = min(512, SEQ)
    query_blocks = query_rows.reshape(SEQ // block_rows, block_rows, H, HD)

    def attend(query_piece):
        scores = low_back(jnp.einsum('qhe,khe->hqk', query_piece, key_rows, precision=HIGHEST_PRECISION) * score_scale)
        scores = jnp.where(key_mask[None, None, :], scores, -1e+30)
        weights = jax.nn.softmax(scores, axis=-1)
        return jnp.einsum('hqk,khe->qhe', low(weights), value_rows, precision=HIGHEST_PRECISION)
    heads_out = lax.map(jax.checkpoint(attend), query_blocks).reshape(SEQ, D)
    heads_out = low_back(low(heads_out))
    attention = low_back(jnp.dot(heads_out, low(w_out), precision=HIGHEST_PRECISION))
    normed = layer_norm(tokens_in + attention, norm_params[0], norm_params[1])
    normed_low = low(normed)
    gate_act = low_back(jnp.dot(normed_low, low(w_gate), precision=HIGHEST_PRECISION))
    up_act = low_back(jnp.dot(normed_low, low(w_up), precision=HIGHEST_PRECISION))
    hidden = low(jax.nn.silu(gate_act) * up_act)
    branch = low_back(jnp.dot(hidden, low(w_down), precision=HIGHEST_PRECISION))
    return layer_norm(normed + branch, norm_params[2], norm_params[3])

def adamw(weight, gradient, first_state, second_state, step_rate, decay_rate):
    first_new = FIRST_DECAY * first_state + (1.0 - FIRST_DECAY) * gradient
    second_new = SECOND_DECAY * second_state + (1.0 - SECOND_DECAY) * gradient * gradient
    first_hat = first_new / (1.0 - FIRST_DECAY ** STEP)
    second_hat = second_new / (1.0 - SECOND_DECAY ** STEP)
    weight_new = weight - step_rate * (first_hat / (jnp.sqrt(second_hat) + ADAM_EPSILON) + decay_rate * weight)
    return (weight_new, first_new, second_new)

def reference(tokens, cotangent, lengths, w_qkv, w_out, w_gate, w_up, w_down, norm_params, m_qkv, v_qkv, m_out, v_out, m_gate, v_gate, m_up, v_up, m_down, v_down, m_norm, v_norm):
    params = (w_qkv, w_out, w_gate, w_up, w_down, norm_params)
    token_slots = tokens.reshape(SLOTS, SEQ, D)
    back_slots = cotangent.reshape(SLOTS, SEQ, D)
    position = jnp.arange(SEQ, dtype=jnp.int32)

    def one_slot(totals, slot_item):
        token_slot, back_slot, length = slot_item
        key_mask = position < length
        row_weight = key_mask.astype(jnp.float32)[:, None]

        def run_layer(tokens_in, *weights_in):
            return layer(tokens_in, *weights_in, key_mask)
        result, pull = jax.vjp(run_layer, token_slot.astype(jnp.float32), *params)
        grads = pull(back_slot.astype(jnp.float32) * row_weight)
        squares = jnp.sum(result * result * row_weight)
        summed = tuple((running_sum + fresh_grad for running_sum, fresh_grad in zip(totals[:-1], grads[1:])))
        return (summed + (totals[-1] + squares,), (result.astype(jnp.bfloat16), grads[0]))
    start_totals = tuple((jnp.zeros_like(parameter) for parameter in params)) + (jnp.zeros((), jnp.float32),)
    totals, (outputs, token_grads) = lax.scan(one_slot, start_totals, (token_slots, back_slots, lengths))
    residual_rms = jnp.sqrt(totals[-1] / (float(TOKENS) * D))
    rate_main = 2.0 / math.sqrt(D)
    rate_out = 2.0 / math.sqrt(D * 16 // SEQ)
    rate_down = 2.0 / math.sqrt(FF)
    new_qkv, first_qkv, second_qkv = adamw(w_qkv, totals[0], m_qkv, v_qkv, rate_main, MATRIX_DECAY)
    new_out, first_out, second_out = adamw(w_out, totals[1], m_out, v_out, rate_out, MATRIX_DECAY)
    new_gate, first_gate, second_gate = adamw(w_gate, totals[2], m_gate, v_gate, rate_main, MATRIX_DECAY)
    new_up, first_up, second_up = adamw(w_up, totals[3], m_up, v_up, rate_main, MATRIX_DECAY)
    new_down, first_down, second_down = adamw(w_down, totals[4], m_down, v_down, rate_down, MATRIX_DECAY)
    new_norm, first_norm, second_norm = adamw(norm_params, totals[5], m_norm, v_norm, NORM_RATE, 0.0)
    return (outputs.reshape(TOKENS, D), token_grads.reshape(TOKENS, D), residual_rms, new_qkv, first_qkv, second_qkv, new_qkv.astype(jnp.bfloat16), new_out, first_out, second_out, new_out.astype(jnp.bfloat16), new_gate, first_gate, second_gate, new_gate.astype(jnp.bfloat16), new_up, first_up, second_up, new_up.astype(jnp.bfloat16), new_down, first_down, second_down, new_down.astype(jnp.bfloat16), new_norm, first_norm, second_norm)
```

```python
import functools
import math

import jax
import jax.numpy as jnp
import numpy as np
from jax import lax
from jax.experimental import pallas as pl
from jax.experimental.pallas import tpu as pltpu
from jax.sharding import PartitionSpec as P

D = 768
HD = 64
FF = 3072
SEQ = 2048
STEP = 10

FIRST_DECAY = 0.9
SECOND_DECAY = 0.999
ADAM_EPSILON = 1e-08
NORM_EPSILON = 1e-05
ROPE_BASE = 1000.0
MATRIX_DECAY = 0.01
NORM_RATE = 0.4
SCALE = 1.0 / math.sqrt(HD)
MASKED = -1e30
SAFE_SCORE = 60.0

BF = jnp.bfloat16
F32 = jnp.float32
NN = (((1,), (0,)), ((), ()))
NT = (((1,), (1,)), ((), ()))
VMEM_LIMIT = 60 << 20
VAUG = 80
ROWS = 8
BLOCK = D // ROWS

LINKS = {"c": ("col", 1), "y": ("col", 2), "x": ("row", 1), "0": ("row", 2), "1": ("row", 4)}
ORDER_QA, ORDER_QB = "1x0", "10x"
ORDER_A, ORDER_B = "1x0", "10x"
OUT_AT = 640


def mm(a, b, dims):
    return lax.dot_general(a, b, dims, preferred_element_type=F32)


def params(n=1):
    return pltpu.CompilerParams(
        vmem_limit_bytes=VMEM_LIMIT, dimension_semantics=("arbitrary",) * n
    )


def cost(flops, nbytes, trans=0):
    return pl.CostEstimate(flops=int(flops), bytes_accessed=int(nbytes), transcendentals=int(trans))


def swap(value, step):
    axis, bit = LINKS[step]
    return lax.ppermute(value, axis, [(i, i ^ bit) for i in range(lax.axis_size(axis))])


def tie(*values):
    return lax.optimization_barrier(values)


def row_mask(order, j):
    return sum(LINKS[s][1] for k, s in enumerate(order) if (j >> k) & 1)


def doubled(held, step):
    return jnp.concatenate([held, swap(held, step)], axis=0)


def halved(keep, send, step):
    total = keep.astype(F32) + swap(send, step).astype(F32)
    half = total.shape[0] // 2
    return total[:half].astype(BF), total[half:].astype(BF)


def gather_plain(shard, order, start, rows):
    full = lax.all_gather(shard, "row", axis=0, tiled=True)
    places = [row_mask(order, j) * BLOCK + start for j in range(ROWS)]
    return jnp.stack([full[at : at + rows] for at in places])


def ungather_plain(pieces):
    rows = []
    for r in range(ROWS):
        parts = []
        for order, blocks in pieces:
            j = [row_mask(order, i) for i in range(ROWS)].index(r)
            parts.append(blocks[j])
        rows.append(jnp.concatenate(parts, axis=0))
    return lax.psum_scatter(
        jnp.concatenate(rows, axis=0).astype(F32), "row", scatter_dimension=0, tiled=True
    )


def fill(dst, src, pos, start, rows, at, lanes, to, cols=slice(None)):
    for j in range(ROWS):
        place = pl.multiple_of(pos[j] * BLOCK + start, 16)
        dst[pl.ds(place, rows), to : to + lanes] = src[j, at : at + rows, cols]


def spill(src, keep, send, pos, start, rows, at, lanes, to, column=0):
    half = keep.shape[0]
    for j in range(ROWS):
        place = pl.multiple_of(pos[j] * BLOCK + start, 16)
        piece = src[pl.ds(place, rows), to : to + lanes].astype(BF)
        if j < half:
            keep[j, at : at + rows, column : column + lanes] = piece
        else:
            send[j - half, at : at + rows, column : column + lanes] = piece


def fill_qkv(w, wa, wb, pos_a, pos_b):
    width = w.shape[1]
    for part, (src, pos) in enumerate(((wa, pos_a), (wb, pos_b))):
        fill(w, src, pos, part * BLOCK // 2, BLOCK // 2, 0, width, 0, slice(0, width))


def project_kernel(col, pos_a, pos_b, lens, x, wa, wb, cos, sin, q_t, k_t, v_t, k_n, v_n, qn, kn, w, w_t):
    i = pl.program_id(0)
    heads = q_t.shape[0]
    rows = x.shape[0]

    @pl.when(i == 0)
    def _():
        fill_qkv(w, wa, wb, pos_a, pos_b)
        w_t[...] = w[...].T

    mixed = mm(w_t[...], x[...], NT)
    c, s = cos[...], sin[...]
    position = (i ^ col[0]) * rows + lax.broadcasted_iota(jnp.int32, (16, rows), 1)
    line = lax.broadcasted_iota(jnp.int32, (16, rows), 0)
    ones_q = jnp.where(line == 0, 1.0, 0.0).astype(BF)
    bias = jnp.where(position < lens[0], 0.0, MASKED)
    tail_k = jnp.where(line == 0, bias, jnp.where(line < 4, 1.0, 0.0)).astype(BF)
    tail_v = jnp.where(line < 3, 1.0, 0.0).astype(BF)
    blank = jnp.zeros((48, rows), BF)

    def turned(block):
        a, b = block[: HD // 2], block[HD // 2 :]
        return jnp.concatenate([a * c - b * s, b * c + a * s], axis=0).astype(BF)

    for h in range(heads):
        at = h * 3 * HD
        q = turned(mixed[at : at + HD]).astype(F32) * SCALE
        k = turned(mixed[at + HD : at + 2 * HD])
        v = mixed[at + 2 * HD : at + 3 * HD].astype(BF)
        kf = k.astype(F32)
        q_t[h] = jnp.concatenate([q.astype(BF), ones_q, blank], axis=0)
        k_t[h] = k
        v_t[h] = jnp.concatenate([v, ones_q], axis=0)
        k_n[h] = jnp.concatenate([k, tail_k, blank], axis=0).T
        v_n[h] = jnp.concatenate([v, tail_v, blank], axis=0).T
        qn[h] = jnp.broadcast_to(jnp.sum(q * q, axis=0, keepdims=True), (8, rows))
        kn[h] = jnp.broadcast_to(jnp.sum(kf * kf, axis=0, keepdims=True), (8, rows))


def project(col, pos_a, pos_b, lengths, x, wa, wb, cos, sin, width):
    t = x.shape[0]
    rows = t // 4
    heads = width // (3 * HD)
    lane = lambda n: pl.BlockSpec((heads, n, rows), lambda i, *_: (0, 0, i))
    line = pl.BlockSpec((heads, rows, 128), lambda i, *_: (0, i, 0))
    whole = lambda a: pl.BlockSpec(a.shape, lambda i, *_: (0,) * a.ndim)
    table = pl.BlockSpec((HD // 2, rows), lambda i, col, *_: (0, i ^ col[0]))
    made = lambda n, dt=BF: jax.ShapeDtypeStruct((heads, n, t), dt)
    natural = jax.ShapeDtypeStruct((heads, t, 128), BF)
    return pl.pallas_call(
        project_kernel,
        grid_spec=pltpu.PrefetchScalarGridSpec(
            num_scalar_prefetch=4,
            grid=(4,),
            in_specs=[pl.BlockSpec((rows, D), lambda i, *_: (i, 0)), whole(wa), whole(wb), table, table],
            out_specs=[lane(128), lane(HD), lane(VAUG), line, line, lane(8), lane(8)],
            scratch_shapes=[pltpu.VMEM((D, width), BF), pltpu.VMEM((width, D), BF)],
        ),
        out_shape=[made(128), made(HD), made(VAUG), natural, natural, made(8, F32), made(8, F32)],
        compiler_params=params(),
        cost_estimate=cost(2 * t * D * width * 2, t * D * 2 + 12 * t * 128 * 2),
        name="project",
    )(col, pos_a, pos_b, lengths, x, wa, wb, cos, sin)


def attend_kernel(q_t, k_n, v_t, qn, kn, out, lse, q_s, top):
    n = k_n.shape[1]
    chunk = min(1024, n)
    bq = q_t.shape[2]
    q_s[...] = q_t[0]
    top[...] = jnp.zeros_like(top)

    @pl.when(jnp.max(qn[0]) * jnp.max(kn[0]) > SAFE_SCORE * SAFE_SCORE)
    def _():
        best = jnp.full((1, bq), -jnp.inf, F32)
        for i in range(n // 256):
            s = mm(k_n[0, i * 256 : (i + 1) * 256, :], q_t[0], NN)
            best = jnp.maximum(best, jnp.max(s, axis=0, keepdims=True))
        high = best.astype(BF).astype(F32)
        low = (best - high).astype(BF).astype(F32)
        top[...] = jnp.broadcast_to(high + low, top.shape)
        line = lax.broadcasted_iota(jnp.int32, (16, bq), 0)
        tail = jnp.where(line == 0, 1.0, jnp.where(line == 1, -high, jnp.where(line == 2, -low, 0.0)))
        q_s[HD : HD + 16, :] = tail.astype(BF)

    q = q_s[...]
    total = None
    for i in range(n // chunk):
        at = slice(i * chunk, (i + 1) * chunk)
        p = jnp.exp(mm(k_n[0, at, :], q, NN)).astype(BF)
        part = mm(v_t[0, :, at], p, NN)
        total = part if total is None else total + part
    weight = total[HD : HD + 1]
    out[0] = (total[:HD] / weight).astype(BF)
    lse[0] = top[...] + jnp.log(jnp.broadcast_to(weight, top.shape))


def attend(q_t, k_n, v_t, qn, kn, half):
    heads, _, t = q_t.shape
    bq = t // 2
    lane = lambda rows, at=half: pl.BlockSpec((1, rows, bq), lambda h: (h, 0, at))
    return pl.pallas_call(
        attend_kernel,
        grid=(heads,),
        in_specs=[
            lane(128),
            pl.BlockSpec((1, t, 128), lambda h: (h, 0, 0)),
            pl.BlockSpec((1, VAUG, t), lambda h: (h, 0, 0)),
            lane(8),
            pl.BlockSpec((1, 8, t), lambda h: (h, 0, 0)),
        ],
        out_specs=[lane(HD, 0), lane(8, 0)],
        out_shape=[
            jax.ShapeDtypeStruct((heads, HD, bq), BF),
            jax.ShapeDtypeStruct((heads, 8, bq), F32),
        ],
        scratch_shapes=[pltpu.VMEM((128, bq), BF), pltpu.VMEM((8, bq), F32)],
        compiler_params=params(),
        cost_estimate=cost(heads * 2 * 2 * bq * t * 256, heads * t * 512),
        name="attend",
    )(q_t, k_n, v_t, qn, kn)


def split3(value):
    a = value.astype(BF).astype(F32)
    b = (value - a).astype(BF).astype(F32)
    return a, b, value - a - b


def turn_back(grad, c, s):
    a, b = grad[: HD // 2], grad[HD // 2 :]
    return jnp.concatenate([a * c + b * s, b * c - a * s], axis=0)


def attend_back_kernel(first, q_t, lse, o_t, do_t, k_n, k_t, v_n, cos, sin, *refs):
    if first:
        dq, dk, dv, q_s, do_s = refs
    else:
        cos_all, sin_all, dk_in, dv_in, dq, dk, dv, q_s, do_s, dk_s = refs
    n = k_n.shape[1]
    chunk = min(512, n)
    bq = q_t.shape[2]
    line = lax.broadcasted_iota(jnp.int32, (16, bq), 0)
    a, b, c = split3(-lse[0][:1])
    tail = jnp.where(line == 0, 1.0, jnp.where(line == 1, a, jnp.where(line == 2, b, jnp.where(line == 3, c, 0.0))))
    q_s[:HD, :] = q_t[0, :HD, :]
    q_s[HD : HD + 16, :] = tail.astype(BF)
    q_s[HD + 16 :, :] = jnp.zeros((48, bq), BF)
    delta = jnp.sum(do_t[0].astype(F32) * o_t[0].astype(F32), axis=0, keepdims=True)
    a, b, c = split3(-delta)
    tail = jnp.where(line == 0, a, jnp.where(line == 1, b, jnp.where(line == 2, c, 0.0)))
    do_s[:HD, :] = do_t[0]
    do_s[HD : HD + 16, :] = tail.astype(BF)
    do_s[HD + 16 :, :] = jnp.zeros((48, bq), BF)
    q, do = q_s[...], do_s[...]
    q64, do64 = q_s[:HD, :], do_s[:HD, :]
    total = None
    for i in range(n // chunk):
        at = slice(i * chunk, (i + 1) * chunk)
        p = jnp.exp(mm(k_n[0, at, :], q, NN))
        gp = mm(v_n[0, at, :], do, NN)
        gs = (p * gp).astype(BF)
        p = p.astype(BF)
        part = mm(k_t[0, :, at], gs, NN)
        total = part if total is None else total + part
        gv = mm(do64, p, NT)
        gk = mm(q64, gs, NT)
        if first:
            dv[0, :, at] = gv
            dk[0, :, at] = gk
        else:
            dv[0, :, at] = (gv + dv_in[0, :, at]).astype(BF)
            dk_s[:, at] = gk + dk_in[0, :, at]
    dq[0] = turn_back(total * SCALE, cos[...], sin[...]).astype(BF)
    if not first:
        dk[0] = turn_back(dk_s[...], cos_all[...], sin_all[...]).astype(BF)


def attend_back(q_t, lse, o_t, do_t, k_n, k_t, v_n, cos, sin, half, sums=None):
    heads, _, t = q_t.shape
    bq = t // 2
    first = sums is None
    lane = lambda rows, at=0: pl.BlockSpec((1, rows, bq), lambda h: (h, 0, at))
    full = lambda rows: pl.BlockSpec((1, rows, t), lambda h: (h, 0, 0))
    natural = pl.BlockSpec((1, t, 128), lambda h: (h, 0, 0))
    table = pl.BlockSpec((HD // 2, bq), lambda h: (0, half))
    table_all = pl.BlockSpec((HD // 2, t), lambda h: (0, 0))
    made = F32 if first else BF
    more = () if first else (cos, sin) + tuple(sums)
    return pl.pallas_call(
        functools.partial(attend_back_kernel, first),
        grid=(heads,),
        in_specs=[lane(128, half), lane(8), lane(HD), lane(HD), natural, full(HD), natural, table, table]
        + ([] if first else [table_all, table_all, full(HD), full(HD)]),
        out_specs=[lane(HD), full(HD), full(HD)],
        out_shape=[
            jax.ShapeDtypeStruct((heads, HD, bq), BF),
            jax.ShapeDtypeStruct((heads, HD, t), made),
            jax.ShapeDtypeStruct((heads, HD, t), made),
        ],
        scratch_shapes=[pltpu.VMEM((128, bq), BF), pltpu.VMEM((128, bq), BF)]
        + ([] if first else [pltpu.VMEM((HD, t), F32)]),
        compiler_params=params(),
        cost_estimate=cost(heads * 5 * 2 * bq * t * 256, heads * t * 2048),
        name="attend_back",
    )(q_t, lse, o_t, do_t, k_n, k_t, v_n, cos, sin, *more)


def fill_out(w, wa, wb, other, pos_a, pos_b):
    width = w.shape[2]
    half = BLOCK // 2
    for part, (src, pos) in enumerate(((wa, pos_a), (wb, pos_b))):
        fill(w.at[0], src, pos, part * half, half, 0, width, 0, slice(OUT_AT, OUT_AT + width))
        fill(w.at[1], other.at[pl.ds(part * ROWS, ROWS)], pos, part * half, half, 0, width, 0)


def out_kernel(pos_a, pos_b, h_own, h_other, wa, wb, other, keep, send, w):
    fill_out(w, wa, wb, other, pos_a, pos_b)
    rows = keep.shape[0]
    for part, out in ((1, send), (0, keep)):
        at = slice(part * rows, (part + 1) * rows)
        total = mm(h_own[:, at].T, w[0], NT) + mm(h_other[:, at].T, w[1], NT)
        out[...] = total.astype(out.dtype)


def out_back_kernel(pos_a, pos_b, ga_own, ga_near, h_own, h_other, wa, wb, other, gh_own, gh_other, keep, send, w, ga):
    fill_out(w, wa, wb, other, pos_a, pos_b)
    rows = ga_own.shape[0]
    ga[:rows] = ga_own[...]
    ga[rows:] = ga_near[...]
    for half, (h, gh, g) in enumerate(((h_own, gh_own, keep), (h_other, gh_other, send))):
        gh[...] = mm(w[half].T, ga[...], NT).astype(BF)
        g[...] = mm(h[...], ga[...], NN).astype(BF)


def vmem_call(kernel, out_shape, scratch, work, name, scalars, *args):
    whole = lambda a: pl.BlockSpec(a.shape, lambda i, *_: (0,) * len(a.shape))
    nbytes = sum(math.prod(a.shape) * a.dtype.itemsize for a in list(args) + list(out_shape))
    return pl.pallas_call(
        kernel,
        grid_spec=pltpu.PrefetchScalarGridSpec(
            num_scalar_prefetch=len(scalars),
            grid=(1,),
            in_specs=[whole(a) for a in args],
            out_specs=[whole(a) for a in out_shape],
            scratch_shapes=scratch,
        ),
        out_shape=out_shape,
        compiler_params=params(),
        cost_estimate=cost(work, nbytes),
        name=name,
    )(*scalars, *args)


def out_project(pos_a, pos_b, h_own, h_other, wa, wb, other):
    rows = h_own.shape[1] // 2
    width = h_own.shape[0]
    return vmem_call(
        out_kernel,
        [jax.ShapeDtypeStruct((rows, D), F32), jax.ShapeDtypeStruct((rows, D), BF)],
        [pltpu.VMEM((2, D, width), BF)],
        2 * 2 * rows * D * 2 * width,
        "out_project",
        (pos_a, pos_b),
        h_own, h_other, wa, wb, other,
    )


def out_back(pos_a, pos_b, ga_own, ga_near, h_own, h_other, wa, wb, other):
    t = 2 * ga_own.shape[0]
    width = h_own.shape[0]
    gh = jax.ShapeDtypeStruct((width, t), BF)
    grad = jax.ShapeDtypeStruct((width, D), BF)
    return vmem_call(
        out_back_kernel,
        [gh, gh, grad, grad],
        [pltpu.VMEM((2, D, width), BF), pltpu.VMEM((t, D), BF)],
        2 * 2 * t * D * 2 * width,
        "out_back",
        (pos_a, pos_b),
        ga_own, ga_near, h_own, h_other, wa, wb, other,
    )


FF_STEPS = 3


def fill_ffn(pos, a0, a1, b0, b1, g_s, u_s, d_s):
    lanes = a0.shape[2]
    half = BLOCK // 2
    for k, (a, b) in enumerate(((a0, b0), (a1, b1))):
        fill(g_s, a, pos.at[0], 0, BLOCK, 0, lanes, k * lanes)
        fill(u_s, b, pos.at[1], 0, BLOCK, 0, lanes, k * lanes)
        fill(d_s, a, pos.at[0], 0, half, BLOCK, lanes, k * lanes)
        fill(d_s, b, pos.at[1], half, half, BLOCK, lanes, k * lanes)


def add_up(total, part, keep, send):
    i = pl.program_id(0)

    @pl.when(i == 0)
    def _():
        total[...] = part

    @pl.when(i > 0)
    def _():
        total[...] += part

    @pl.when(i == pl.num_programs(0) - 1)
    def _():
        rows = keep.shape[0]
        keep[...] = total[:rows]
        send[...] = total[rows:].astype(BF)


def ffn_kernel(pos, x_own, x_far, a0, a1, b0, b1, gate, up, keep, send, x, g_s, u_s, d_s, total):
    rows = x_own.shape[0]

    @pl.when(pl.program_id(0) == 0)
    def _():
        x[:rows] = x_own[...]
        x[rows:] = x_far[...]

    fill_ffn(pos, a0, a1, b0, b1, g_s, u_s, d_s)
    g = mm(x[...], g_s[...], NN)
    u = mm(x[...], u_s[...], NN)
    gate[...] = g
    up[...] = u
    hidden = (g * jax.nn.sigmoid(g) * u).astype(BF)
    add_up(total, mm(hidden, d_s[...], NT), keep, send)


def ffn_back_kernel(
    pos, gb_own, gb_far, a0, a1, b0, b1, gate, up, hid, ggate, gup, keep, send, gb, g_s, u_s, d_s, total
):
    rows = gb_own.shape[0]

    @pl.when(pl.program_id(0) == 0)
    def _():
        gb[:rows] = gb_own[...]
        gb[rows:] = gb_far[...]

    fill_ffn(pos, a0, a1, b0, b1, g_s, u_s, d_s)
    gh = mm(gb[...], d_s[...], NN)
    g, u = gate[...], up[...]
    sig = jax.nn.sigmoid(g)
    silu = g * sig
    hid[...] = (silu * u).astype(BF)
    gga = (gh * u * sig * (1.0 + g * (1.0 - sig))).astype(BF)
    gua = (gh * silu).astype(BF)
    ggate[...] = gga
    gup[...] = gua
    add_up(total, mm(gga, g_s[...], NT) + mm(gua, u_s[...], NT), keep, send)


def ffn_grad_kernel(n, pos, *refs):
    xs, gbs, acts = refs[: 2 * n], refs[2 * n : 4 * n], refs[4 * n : 7 * n]
    ak, as_, bk, bs, x_t, gb_t, grad = refs[7 * n :]
    rows = xs[0].shape[0]

    @pl.when(pl.program_id(0) == 0)
    def _():
        for k in range(2 * n):
            x_t[:, k * rows : (k + 1) * rows] = xs[k][...].T
            gb_t[:, k * rows : (k + 1) * rows] = gbs[k][...].T

    lanes = ak.shape[2]
    half = BLOCK // 2

    def product(left, right):
        total = None
        for k in range(n):
            part = mm(left[:, 2 * k * rows : 2 * (k + 1) * rows], right[k][...], NN)
            total = part if total is None else total + part
        grad[...] = total

    def out(src_pos, keep, send, start, count, at):
        for dst, to in ((keep, 0), (send, lanes)):
            for j in range(ROWS):
                place = pl.multiple_of(src_pos[j] * BLOCK + start, 16)
                dst[j, at : at + count, :] = grad[pl.ds(place, count), to : to + lanes].astype(BF)

    product(gb_t, acts[:n])
    out(pos.at[0], ak, as_, 0, half, BLOCK)
    out(pos.at[1], bk, bs, half, half, BLOCK)
    product(x_t, acts[n : 2 * n])
    out(pos.at[0], ak, as_, 0, BLOCK, 0)
    product(x_t, acts[2 * n :])
    out(pos.at[1], bk, bs, 0, BLOCK, 0)


def const_spec(a):
    return pl.BlockSpec(a.shape, lambda i, *_: (0,) * len(a.shape))


def ffn_parts(x, a0):
    width = a0.shape[2] // FF_STEPS
    t = 2 * x.shape[0]
    weight = pl.BlockSpec((ROWS, a0.shape[1], width), lambda i, *_: (0, 0, i))
    act = pl.BlockSpec((t, 2 * width), lambda i, *_: (0, i))
    scratch = [pltpu.VMEM((t, D), BF)] + [pltpu.VMEM((D, 2 * width), BF)] * 3 + [pltpu.VMEM((t, D), F32)]
    return width, t, weight, act, scratch, 2 * a0.shape[2]


def ffn(pos, x_own, x_far, weights):
    width, t, weight, act, scratch, units = ffn_parts(x_own, weights[0])
    acts = jax.ShapeDtypeStruct((t, units), F32)
    ends = [jax.ShapeDtypeStruct((t // 2, D), F32), jax.ShapeDtypeStruct((t // 2, D), BF)]
    return pl.pallas_call(
        ffn_kernel,
        grid_spec=pltpu.PrefetchScalarGridSpec(
            num_scalar_prefetch=1,
            grid=(FF_STEPS,),
            in_specs=[const_spec(x_own), const_spec(x_far)] + [weight] * 4,
            out_specs=[act, act] + [const_spec(e) for e in ends],
            scratch_shapes=scratch,
        ),
        out_shape=[acts, acts] + ends,
        compiler_params=params(),
        cost_estimate=cost(6 * t * D * units, 8 * t * units + 6 * D * units),
        name="ffn",
    )(pos, x_own, x_far, *weights)


def ffn_back(pos, gb_own, gb_far, weights, gate, up):
    width, t, weight, act, scratch, units = ffn_parts(gb_own, weights[0])
    acts = jax.ShapeDtypeStruct((t, units), BF)
    ends = [jax.ShapeDtypeStruct((t // 2, D), F32), jax.ShapeDtypeStruct((t // 2, D), BF)]
    return pl.pallas_call(
        ffn_back_kernel,
        grid_spec=pltpu.PrefetchScalarGridSpec(
            num_scalar_prefetch=1,
            grid=(FF_STEPS,),
            in_specs=[const_spec(gb_own), const_spec(gb_far)] + [weight] * 4 + [act, act],
            out_specs=[act] * 3 + [const_spec(e) for e in ends],
            scratch_shapes=scratch,
        ),
        out_shape=[acts] * 3 + ends,
        compiler_params=params(),
        cost_estimate=cost(6 * t * D * units, 14 * t * units + 6 * D * units),
        name="ffn_back",
    )(pos, gb_own, gb_far, *weights, gate, up)


def ffn_grad(pos, xs, gbs, acts, units):
    n = len(xs) // 2
    rows = xs[0].shape[0]
    width = units // 2 // FF_STEPS
    act = pl.BlockSpec((2 * rows, 2 * width), lambda i, *_: (0, i))
    blocks = jax.ShapeDtypeStruct((ROWS, BLOCK * 3 // 2, units // 2), BF)
    grads = pl.BlockSpec((ROWS, BLOCK * 3 // 2, width), lambda i, *_: (0, 0, i))
    t = 2 * n * rows
    return pl.pallas_call(
        functools.partial(ffn_grad_kernel, n),
        grid_spec=pltpu.PrefetchScalarGridSpec(
            num_scalar_prefetch=1,
            grid=(FF_STEPS,),
            in_specs=[const_spec(a) for a in xs + gbs] + [act] * len(acts),
            out_specs=[grads] * 4,
            scratch_shapes=[pltpu.VMEM((D, t), BF)] * 2 + [pltpu.VMEM((D, 2 * width), F32)],
        ),
        out_shape=[blocks] * 4,
        compiler_params=params(),
        cost_estimate=cost(6 * t * D * units, 6 * t * units + 6 * D * units),
        name="ffn_grad",
    )(pos, *xs, *gbs, *acts)


def units_of(h):
    centre = jnp.mean(h, axis=1, keepdims=True)
    away = h - centre
    scale = lax.rsqrt(jnp.mean(away * away, axis=1, keepdims=True) + NORM_EPSILON)
    return away * scale, scale


def back_through(grad, unit, scale, gain):
    scaled = grad * gain
    mean = jnp.mean(scaled, axis=1, keepdims=True)
    crossed = jnp.mean(scaled * unit, axis=1, keepdims=True)
    return scale * (scaled - mean - unit * crossed)


def columns(value):
    return jnp.sum(value, axis=0, keepdims=True)


def first_kernel(tokens, keep, came, norm, first, *lows):
    h = tokens[...].astype(F32) + keep[...] + came[...].astype(F32)
    first[...] = h
    unit, _ = units_of(h)
    normed = (unit * norm[0:1] + norm[1:2]).astype(BF)
    rows = lows[0].shape[0]
    for k, low in enumerate(lows):
        low[...] = normed[k * rows : (k + 1) * rows]


def norm_one(tokens, keep, came, norm, chunks):
    rows = tokens.shape[0]
    return vmem_call(
        first_kernel,
        [jax.ShapeDtypeStruct((rows, D), F32)] + [jax.ShapeDtypeStruct((rows // chunks, D), BF)] * chunks,
        [], 12 * rows * D, "first_norm", (), tokens, keep, came, norm,
    )


def second_kernel(place, first, keep, came, cotangent, norm, result, grad, low, sums):
    rows = result.shape[0]
    unit, _ = units_of(first[...])
    normed = unit * norm[0:1] + norm[1:2]
    unit, scale = units_of(normed + keep[...] + came[...].astype(F32))
    out = unit * norm[2:3] + norm[3:4]
    result[...] = out.astype(BF)
    position = place[0] + lax.broadcasted_iota(jnp.int32, (rows, 1), 0)
    weight = (position < place[1]).astype(F32)
    g = cotangent[...].astype(F32) * weight
    back = back_through(g, unit, scale, norm[2:3])
    grad[...] = back
    low[...] = back.astype(BF)
    sums[...] = jnp.concatenate(
        [jnp.zeros((2, D), F32), columns(g * unit), columns(g), columns(out * out * weight), jnp.zeros((3, D), F32)],
        axis=0,
    )


def chunk_call(kernel, k, scalars, chunked, whole, out_shape, name, work):
    rows = out_shape[0].shape[0]
    part = pl.BlockSpec((rows, D), lambda i, *_: (k, 0))
    return pl.pallas_call(
        kernel,
        grid_spec=pltpu.PrefetchScalarGridSpec(
            num_scalar_prefetch=len(scalars),
            grid=(1,),
            in_specs=[part] * len(chunked) + [const_spec(a) for a in whole],
            out_specs=[const_spec(a) for a in out_shape],
        ),
        out_shape=out_shape,
        compiler_params=params(),
        cost_estimate=cost(work, 20 * rows * D),
        name=name,
    )(*scalars, *chunked, *whole)


def norm_two(k, place, first, keep, came, cotangent, norm):
    rows = keep.shape[0]
    made = lambda kind: jax.ShapeDtypeStruct((rows, D), kind)
    kernel = lambda place, first, cot, keep, came, *rest: second_kernel(place, first, keep, came, cot, *rest)
    return chunk_call(
        kernel, k, (place,), (first, cotangent), (keep, came, norm),
        [made(BF), made(F32), made(BF), jax.ShapeDtypeStruct((8, D), F32)], "second_norm", 30 * rows * D,
    )


def first_back_kernel(first, second, keep, came, norm, grad, low, sums):
    unit, scale = units_of(first[...])
    g = second[...] + keep[...] + came[...].astype(F32)
    back = back_through(g, unit, scale, norm[0:1])
    grad[...] = back
    low[...] = back.astype(BF)
    sums[...] = jnp.concatenate([columns(g * unit), columns(g), jnp.zeros((6, D), F32)], axis=0)


def norm_one_back(k, first, second, keep, came, norm):
    rows = keep.shape[0]
    made = lambda kind: jax.ShapeDtypeStruct((rows, D), kind)
    return chunk_call(
        first_back_kernel, k, (), (first,), (second, keep, came, norm),
        [made(F32), made(BF), jax.ShapeDtypeStruct((8, D), F32)], "first_norm_back", 20 * rows * D,
    )


def token_kernel(pos_a, pos_b, dq, dk, dv, wa, wb, near, far, w):
    fill_qkv(w, wa, wb, pos_a, pos_b)
    rows = near.shape[0]
    for part, out in ((0, near), (1, far)):
        at = slice(part * rows, (part + 1) * rows)
        mixed = jnp.concatenate([ref[h, :, at] for h in range(dq.shape[0]) for ref in (dq, dk, dv)], axis=0)
        out[...] = mm(mixed.T, w[...], NT).astype(out.dtype)


def token_terms(pos_a, pos_b, dq, dk, dv, wa, wb, half, kinds):
    heads, _, bq = dq.shape
    width = heads * 3 * HD
    whole = lambda a: pl.BlockSpec(a.shape, lambda i, *_: (0,) * len(a.shape))
    lane = lambda at: pl.BlockSpec((heads, HD, bq), lambda i, *_: (0, 0, at))
    out = [jax.ShapeDtypeStruct((bq // 2, D), kind) for kind in kinds]
    return pl.pallas_call(
        token_kernel,
        grid_spec=pltpu.PrefetchScalarGridSpec(
            num_scalar_prefetch=2,
            grid=(1,),
            in_specs=[lane(0), lane(half), lane(half), whole(wa), whole(wb)],
            out_specs=[whole(a) for a in out],
            scratch_shapes=[pltpu.VMEM((D, width), BF)],
        ),
        out_shape=out,
        compiler_params=params(),
        cost_estimate=cost(2 * bq * D * width, bq * (D + width) * 4),
        name="token_terms",
    )(pos_a, pos_b, dq, dk, dv, wa, wb)


def qkv_grad_kernel(pos_a, pos_b, dq0, dq1, dk, dv, x, out_own, out_came, a_k, a_s, b_k, b_s, g, go):
    bq = dq0.shape[2]
    total = None
    for half, dq in enumerate((dq0, dq1)):
        at = slice(half * bq, (half + 1) * bq)
        mixed = jnp.concatenate(
            [p for h in range(dq.shape[0]) for p in (dq[h], dk[h, :, at], dv[h, :, at])], axis=0
        )
        part = mm(mixed, x[at, :], NN)
        total = part if total is None else total + part
    g[...] = total.T
    go[...] = (out_own[...].astype(F32) + out_came[...].astype(F32)).T
    half = BLOCK // 2
    width, out_width = g.shape[1], go.shape[1]
    for part, (k, s, pos) in enumerate(((a_k, a_s, pos_a), (b_k, b_s, pos_b))):
        k[:, :, width:OUT_AT] = jnp.zeros((ROWS // 2, half, OUT_AT - width), BF)
        s[:, :, width:OUT_AT] = jnp.zeros((ROWS // 2, half, OUT_AT - width), BF)
        spill(g, k, s, pos, part * half, half, 0, width, 0)
        spill(go, k, s, pos, part * half, half, 0, out_width, 0, OUT_AT)


def qkv_grad(pos_a, pos_b, dq0, dq1, dk, dv, x, out_own, out_came):
    out_width = out_own.shape[0]
    blocks = jax.ShapeDtypeStruct((ROWS // 2, BLOCK // 2, OUT_AT + out_width), BF)
    width = 3 * dq0.shape[0] * HD
    return vmem_call(
        qkv_grad_kernel,
        [blocks] * 4,
        [pltpu.VMEM((D, width), F32), pltpu.VMEM((D, out_width), F32)],
        2 * x.shape[0] * D * width,
        "qkv_grad",
        (pos_a, pos_b),
        dq0, dq1, dk, dv, x, out_own, out_came,
    )


def adamw(weight, gradient, first_state, second_state, step_rate, decay_rate):
    first_new = FIRST_DECAY * first_state + (1.0 - FIRST_DECAY) * gradient
    second_new = SECOND_DECAY * second_state + (1.0 - SECOND_DECAY) * gradient * gradient
    first_hat = first_new / (1.0 - FIRST_DECAY**STEP)
    second_hat = second_new / (1.0 - SECOND_DECAY**STEP)
    weight_new = weight - step_rate * (
        first_hat / (jnp.sqrt(second_hat) + ADAM_EPSILON) + decay_rate * weight
    )
    return (weight_new, first_new, second_new)


def rope_tables(length):
    position = np.arange(length, dtype=np.float32)
    inverse = np.exp(np.arange(HD // 2, dtype=np.float32) * np.float32(-2.0 * math.log(ROPE_BASE) / HD))
    angle = (inverse.astype(np.float32)[:, None] * position[None, :]).astype(np.float64)
    return np.cos(angle).astype(np.float32), np.sin(angle).astype(np.float32)


def on_device(
    tokens, cotangent, lengths, w_qkv, w_out, w_gate, w_up, w_down, norm_params,
    m_qkv, v_qkv, m_out, v_out, m_gate, v_gate, m_up, v_up, m_down, v_down, m_norm, v_norm,
):
    own_rows = tokens.shape[0]
    seq_rows = own_rows * lax.axis_size("col")
    col = lax.axis_index("col").astype(jnp.int32)
    row = lax.axis_index("row").astype(jnp.int32)
    small = lax.axis_size("row") == ROWS
    me = row if small else row * 0
    qkv_width = w_qkv.shape[1]
    head_width = qkv_width // 3
    heads = head_width // HD
    half = BLOCK // 2
    chunks = 2

    places = lambda order: jnp.stack([me ^ row_mask(order, j) for j in range(ROWS)])
    pos_a, pos_b = places(ORDER_QA), places(ORDER_QB)
    pos_f = jnp.stack([places(ORDER_A), places(ORDER_B)])

    gap = jnp.zeros((w_qkv.shape[0], OUT_AT - qkv_width), BF)
    pack = jnp.concatenate([w_qkv.astype(BF), gap, w_out.T.astype(BF)], axis=1)
    low_down = w_down.T.astype(BF)
    low_gate, low_up = w_gate.astype(BF), w_up.astype(BF)

    near = swap(tokens, "c")
    far = swap(tokens, "y")
    if small:
        qa, qb = doubled(pack[None, :half], "1"), doubled(pack[None, half:], "1")
        fa = jnp.concatenate([low_gate, low_down[:half]], axis=0)[None]
        fb = jnp.concatenate([low_up, low_down[half:]], axis=0)[None]
        fa, fb, qa, qb = tie(fa, fb, qa, qb)
        qa, qb = doubled(qa, "x"), doubled(qb, "0")
        wa, wb = doubled(qa, "0"), doubled(qb, "x")
        fa, fb = doubled(fa, "1"), doubled(fb, "1")
    else:
        wa = gather_plain(pack, ORDER_QA, 0, half)
        wb = gather_plain(pack, ORDER_QB, half, half)
        join = lambda w, order, start: jnp.concatenate(
            [gather_plain(w, order, 0, BLOCK), gather_plain(low_down, order, start, half)], axis=1
        )
        fa, fb = join(low_gate, ORDER_A, 0), join(low_up, ORDER_B, half)
    far_near = swap(far, "c")
    tokens_all = jnp.concatenate([tokens, near, far, far_near], axis=0)

    cos_np, sin_np = rope_tables(seq_rows)
    cos, sin = jnp.asarray(cos_np), jnp.asarray(sin_np)
    q_t, k_t, v_t, k_n, v_n, qn, kn = project(
        col[None], pos_a, pos_b, lengths, tokens_all, wa, wb, cos, sin, qkv_width
    )
    wo_far = swap(jnp.concatenate([wa, wb], axis=0)[:, :, OUT_AT:], "y")
    if small:
        fa, fb, q_t = tie(fa, fb, q_t)
        fa, fb = doubled(fa, "x"), doubled(fb, "0")
    far_heads, far_lse = attend(q_t, k_n, v_t, qn, kn, 1)
    if small:
        fa, fb, far_heads, far_lse, q_t = tie(fa, fb, far_heads, far_lse, q_t)
        fa, fb = doubled(fa, "0"), doubled(fb, "x")
    other_heads = swap(far_heads.reshape(head_width, seq_rows // 2), "y")
    own_heads, own_lse = attend(q_t, k_n, v_t, qn, kn, 0)
    flat_heads = own_heads.reshape(head_width, seq_rows // 2)
    if small:
        fa, fb, flat_heads, other_heads = tie(fa, fb, flat_heads, other_heads)
    weights = (fa, swap(fa, "c"), fb, swap(fb, "c"))

    keep, send = out_project(pos_a, pos_b, flat_heads, other_heads, wa, wb, wo_far)
    first, *normed = norm_one(tokens, keep, swap(send, "c"), norm_params, chunks)
    normed_far = [swap(n, "y") for n in normed]
    place = lambda k: jnp.stack([col * own_rows + k * (own_rows // chunks), lengths[0]])
    fwd, sums, results, seconds, lows = [], [], [], [], []
    for k in range(chunks):
        fwd.append(ffn(pos_f, normed[k], normed_far[k], weights))
    came = [swap(f[3], "y") for f in fwd]
    for k in range(chunks):
        result, second, low, part = norm_two(
            k, place(k), first, fwd[k][2], came[k], cotangent, norm_params
        )
        results.append(result)
        seconds.append(second)
        lows.append(low)
        sums.append(part)
    lows_far = [swap(low, "y") for low in lows]
    back = [ffn_back(pos_f, lows[k], lows_far[k], weights, fwd[k][0], fwd[k][1]) for k in range(chunks)]
    came = [swap(b[4], "y") for b in back]
    pairs = lambda a, b: [v for ab in zip(a, b) for v in ab]
    ak, as_, bk, bs = ffn_grad(
        pos_f, pairs(normed, normed_far), pairs(lows, lows_far),
        [back[k][t] for t in range(3) for k in range(chunks)], 2 * w_gate.shape[1],
    )
    firsts, ga = [], []
    for k in range(chunks):
        grad, low, part = norm_one_back(k, first, seconds[k], back[k][3], came[k], norm_params)
        firsts.append(grad)
        ga.append(low)
        sums.append(part)
    grad_first = jnp.concatenate(firsts, axis=0)
    ga = jnp.concatenate(ga, axis=0)
    gh_own, gh_other, go_own, go_other = out_back(
        pos_a, pos_b, ga, swap(ga, "c"), flat_heads, other_heads, wa, wb, wo_far
    )
    gh_far = swap(gh_other, "y")
    go_came = swap(go_other, "y")
    grad_a = (ak.astype(F32) + swap(as_, "c").astype(F32)).astype(BF)
    grad_b = (bk.astype(F32) + swap(bs, "c").astype(F32)).astype(BF)

    turn = lambda table: jnp.concatenate(
        [lax.dynamic_slice_in_dim(table, (col ^ j) * own_rows, own_rows, 1) for j in range(4)], axis=1
    )
    cos_rel, sin_rel = turn(cos), turn(sin)
    shaped = lambda a: a.reshape(heads, HD, seq_rows // 2)
    if small:
        a = halved(grad_a[:4], grad_a[4:], "0")
        b = halved(grad_b[:4], grad_b[4:], "x")
    dq0, dk, dv = attend_back(
        q_t, own_lse, own_heads, shaped(gh_own), k_n, k_t, v_n, cos_rel, sin_rel, 0
    )
    if small:
        *a, dq0, dk, dv = tie(*a, dq0, dk, dv)
        *b, dq0, dk, dv = tie(*b, dq0, dk, dv)
        a = halved(*a, "x")
        b = halved(*b, "0")
    dq1, dk, dv = attend_back(
        q_t, far_lse, far_heads, shaped(gh_far), k_n, k_t, v_n, cos_rel, sin_rel, 1, (dk, dv)
    )
    if small:
        *a, dq1, dk, dv = tie(*a, dq1, dk, dv)
        *b, dq1, dk, dv = tie(*b, dq1, dk, dv)
        own_a = (a[0].astype(F32) + swap(a[1], "1").astype(F32))[0]
        own_b = (b[0].astype(F32) + swap(b[1], "1").astype(F32))[0]
        own_gate, own_up = own_a[:BLOCK], own_b[:BLOCK]
        own_down = jnp.concatenate([own_a[BLOCK:], own_b[BLOCK:]], axis=0)
    else:
        own_gate = ungather_plain([(ORDER_A, grad_a[:, :BLOCK])])
        own_up = ungather_plain([(ORDER_B, grad_b[:, :BLOCK])])
        own_down = ungather_plain([(ORDER_A, grad_a[:, BLOCK:]), (ORDER_B, grad_b[:, BLOCK:])])
    f_keep, f_send = token_terms(pos_a, pos_b, dq1, dk, dv, wa, wb, 1, (F32, BF))
    f_send = (f_keep + swap(f_send, "c").astype(F32)).astype(BF)
    from_far = swap(f_send, "y")
    qa_k, qa_s, qb_k, qb_s = qkv_grad(pos_a, pos_b, dq0, dq1, dk, dv, tokens_all, go_own, go_came)
    n_keep, n_send = token_terms(pos_a, pos_b, dq0, dk, dv, wa, wb, 0, (F32, BF))
    grad_tokens = grad_first + n_keep + swap(n_send, "c").astype(F32) + from_far.astype(F32)
    if small:
        a, b = halved(qa_k, qa_s, "0"), halved(qb_k, qb_s, "x")
        a, b = halved(*a, "x"), halved(*b, "0")
        own_a = (a[0].astype(F32) + swap(a[1], "1").astype(F32))[0]
        own_b = (b[0].astype(F32) + swap(b[1], "1").astype(F32))[0]
        own_pack = jnp.concatenate([own_a, own_b], axis=0)
    else:
        own_pack = ungather_plain(
            [(ORDER_QA, jnp.concatenate([qa_k, qa_s])), (ORDER_QB, jnp.concatenate([qb_k, qb_s]))]
        )
    own_qkv, own_out = own_pack[:, :qkv_width], own_pack[:, OUT_AT:]

    sums = sum(sums)
    if small:
        for step in "cyx01":
            sums = sums + swap(sums, step)
    else:
        sums = lax.psum(sums, ("row", "col"))
    summed_norm = sums[:4]
    all_cells = float(own_rows * lax.axis_size("row") * lax.axis_size("col") * D)
    residual_rms = jnp.sqrt(jnp.sum(sums[4]) / all_cells)
    result = jnp.concatenate(results, axis=0)

    rate_main = 2.0 / math.sqrt(D)
    rate_out = 2.0 / math.sqrt(D * 16 // SEQ)
    rate_down = 2.0 / math.sqrt(FF)
    new_qkv, first_qkv, second_qkv = adamw(w_qkv, own_qkv, m_qkv, v_qkv, rate_main, MATRIX_DECAY)
    new_out, first_out, second_out = adamw(w_out, own_out.T, m_out, v_out, rate_out, MATRIX_DECAY)
    new_gate, first_gate, second_gate = adamw(w_gate, own_gate, m_gate, v_gate, rate_main, MATRIX_DECAY)
    new_up, first_up, second_up = adamw(w_up, own_up, m_up, v_up, rate_main, MATRIX_DECAY)
    new_down, first_down, second_down = adamw(w_down, own_down.T, m_down, v_down, rate_down, MATRIX_DECAY)
    new_norm, first_norm, second_norm = adamw(norm_params, summed_norm, m_norm, v_norm, NORM_RATE, 0.0)
    return (
        result, grad_tokens, residual_rms,
        new_qkv, first_qkv, second_qkv, new_qkv.astype(BF),
        new_out, first_out, second_out, new_out.astype(BF),
        new_gate, first_gate, second_gate, new_gate.astype(BF),
        new_up, first_up, second_up, new_up.astype(BF),
        new_down, first_down, second_down, new_down.astype(BF),
        new_norm, first_norm, second_norm,
    )


def solution(mesh):
    tokens, wide, tall, full = P(("row", "col"), None), P("row", "col"), P("col", "row"), P()
    return jax.shard_map(
        on_device,
        mesh=mesh,
        in_specs=(tokens, tokens, P("row"), wide, tall, wide, wide, tall, full)
        + (wide, wide, tall, tall, wide, wide, wide, wide, tall, tall, full, full),
        out_specs=(tokens, tokens, full)
        + (wide,) * 4 + (tall,) * 4 + (wide,) * 8 + (tall,) * 4 + (full,) * 3,
        check_vma=False,
    )
```

```python
import functools
import math

import jax
import jax.numpy as jnp
import numpy as np
from jax import lax
from jax.experimental import pallas as pl
from jax.experimental.pallas import tpu as pltpu
from jax.sharding import PartitionSpec as P

D = 768
HD = 64
FF = 3072
SEQ = 2048
STEP = 10

FIRST_DECAY = 0.9
SECOND_DECAY = 0.999
ADAM_EPSILON = 1e-08
NORM_EPSILON = 1e-05
ROPE_BASE = 1000.0
MATRIX_DECAY = 0.01
NORM_RATE = 0.4
SCALE = 1.0 / math.sqrt(HD)
MASKED = -1e30
SAFE_SCORE = 60.0

BF = jnp.bfloat16
F32 = jnp.float32
NN = (((1,), (0,)), ((), ()))
NT = (((1,), (1,)), ((), ()))
VAUG = 80
ROWS = 8
BLOCK = D // ROWS

LINKS = {"c": ("col", 1), "y": ("col", 2), "x": ("row", 1), "0": ("row", 2), "1": ("row", 4)}
ORDER_QA, ORDER_QB = "1x0", "10x"
ORDER_A, ORDER_B = "1x0", "01x"
OUT_AT = 640


def mm(a, b, dims):
    return lax.dot_general(a, b, dims, preferred_element_type=F32)


def params(mib=10):
    return pltpu.CompilerParams(vmem_limit_bytes=mib << 20)


def cost(flops, nbytes, trans=0):
    return pl.CostEstimate(flops=int(flops) // 10, bytes_accessed=int(nbytes) // 10, transcendentals=int(trans))


def swap(value, step):
    axis, bit = LINKS[step]
    return lax.ppermute(value, axis, [(i, i ^ bit) for i in range(lax.axis_size(axis))])


def tie(*values):
    return lax.optimization_barrier(values)


def row_mask(order, j):
    return sum(LINKS[s][1] for k, s in enumerate(order) if (j >> k) & 1)


def doubled(held, step):
    return jnp.concatenate([held, swap(held, step)], axis=0)


RIDE = 16


def ride(sums):
    return jnp.concatenate([*split3(sums[:5]), jnp.zeros((1, D), F32)], axis=0).astype(BF)


def unride(rows):
    rows = rows.astype(F32)
    return jnp.concatenate([rows[:5] + rows[5:10] + rows[10:15], jnp.zeros((3, D), F32)], axis=0)


def fold_sums_kernel(a, b, a_came, b_came, sums, a_keep, b_keep, a_send, b_send, sums_out):
    half, rows = a_keep.shape[0], a_keep.shape[1]
    n = 2 * half
    total = sums[...] + unride(a_came[n * rows :, :D])
    sums_out[...] = total
    for j in range(n):
        ta = (a[j].astype(F32) + a_came[j * rows : (j + 1) * rows].astype(F32)).astype(BF)
        tb = (b[j].astype(F32) + b_came[j].astype(F32)).astype(BF)
        if j < half:
            a_keep[j] = ta
            b_keep[j] = tb
        else:
            a_send[(j - half) * rows : (j - half + 1) * rows, :] = ta
            b_send[j - half] = tb
    a_send[half * rows :, :D] = ride(total)
    a_send[half * rows :, D:] = jnp.zeros((RIDE, a_send.shape[1] - D), BF)


def fold_sums(a, b, a_came, b_came, sums):
    half = jax.ShapeDtypeStruct((a.shape[0] // 2,) + a.shape[1:], BF)
    send = jax.ShapeDtypeStruct((half.shape[0] * a.shape[1] + RIDE, a.shape[2]), BF)
    sums_out = jax.ShapeDtypeStruct(sums.shape, F32)
    outs = [half, half, send, half, sums_out]
    return vmem_call(fold_sums_kernel, outs, [], 2 * math.prod(a.shape), "fold_sums", (), a, b, a_came, b_came, sums)


def fold_kernel(*refs):
    n = len(refs) // 4
    for keep, came, out_keep, out_send in zip(refs[:n], refs[n : 2 * n], refs[2 * n : 3 * n], refs[3 * n :]):
        half = out_keep.shape[0]
        for j in range(2 * half):
            total = (keep[j].astype(F32) + came[j].astype(F32)).astype(BF)
            if j < half:
                out_keep[j] = total
            else:
                out_send[j - half] = total


def fold(keeps, cames):
    halves = [jax.ShapeDtypeStruct((k.shape[0] // 2,) + k.shape[1:], BF) for k in keeps]
    size = sum(math.prod(k.shape) for k in keeps)
    out = vmem_call(fold_kernel, halves * 2, [], size, "fold", (), *keeps, *cames)
    return out[: len(keeps)], out[len(keeps) :]


def gather_plain(shard, order, start, rows):
    full = lax.all_gather(shard, "row", axis=0, tiled=True)
    places = [row_mask(order, j) * BLOCK + start for j in range(ROWS)]
    return jnp.stack([full[at : at + rows] for at in places])


def ungather_plain(pieces):
    rows = []
    for r in range(ROWS):
        parts = []
        for order, blocks in pieces:
            j = [row_mask(order, i) for i in range(ROWS)].index(r)
            parts.append(blocks[j])
        rows.append(jnp.concatenate(parts, axis=0))
    return lax.psum_scatter(
        jnp.concatenate(rows, axis=0).astype(F32), "row", scatter_dimension=0, tiled=True
    )


def pack_kernel(w_qkv, w_out, w_gate, w_up, w_down, out, ffn_a, ffn_b):
    width = w_qkv.shape[1]
    gap = jnp.zeros((out.shape[0], OUT_AT - width), F32)
    out[...] = jnp.concatenate([w_qkv[...], gap, w_out[...].T], axis=1).astype(BF)
    half = BLOCK // 2
    ffn_a[:BLOCK] = w_gate[...].astype(BF)
    ffn_a[BLOCK:] = w_down[:half].astype(BF)
    ffn_b[:BLOCK] = w_up[...].astype(BF)
    ffn_b[BLOCK:] = w_down[half:].astype(BF)


def fill(dst, src, pos, start, rows, at, lanes, to, cols=slice(None), first=0):
    for j in range(src.shape[0]):
        place = pl.multiple_of(pos[first + j] * BLOCK + start, 16)
        dst[pl.ds(place, rows), to : to + lanes] = src[j, at : at + rows, cols]


def spill(src, keep, send, pos, start, rows, at, lanes, to, column=0):
    half = keep.shape[0]
    for j in range(ROWS):
        place = pl.multiple_of(pos[j] * BLOCK + start, 16)
        piece = src[pl.ds(place, rows), to : to + lanes].astype(BF)
        if j < half:
            keep[j, at : at + rows, column : column + lanes] = piece
        else:
            send[j - half, at : at + rows, column : column + lanes] = piece


def fill_qkv(w, packs, pos_a, pos_b):
    width = w.shape[1]
    for k, src in enumerate(packs):
        part, pos = k // 2, (pos_a, pos_b)[k // 2]
        fill(w, src, pos, part * BLOCK // 2, BLOCK // 2, 0, width, 0, slice(0, width), k % 2 * (ROWS // 2))


def project_kernel(col, pos_a, pos_b, lens, *refs):
    xs, packs, (cos, sin, q_t, k_t, v_t, k_n, v_n, qn, kn, w, w_t) = refs[:4], refs[4:8], refs[8:]
    heads = q_t.shape[0]
    rows = xs[0].shape[0]
    fill_qkv(w, packs, pos_a, pos_b)
    w_t[...] = w[...].T
    line = lax.broadcasted_iota(jnp.int32, (16, rows), 0)
    ones_q = jnp.where(line == 0, 1.0, 0.0).astype(BF)
    tail_v = jnp.where(line < 3, 1.0, 0.0).astype(BF)
    blank = jnp.zeros((48, rows), BF)
    for i, x in enumerate(xs):
        at = slice(i * rows, (i + 1) * rows)
        start = pl.multiple_of((i ^ col[0]) * rows, 128)
        c, s = cos[:, pl.ds(start, rows)], sin[:, pl.ds(start, rows)]
        mixed = mm(w_t[...], x[...], NT)
        position = start + lax.broadcasted_iota(jnp.int32, (16, rows), 1)
        bias = jnp.where(position < lens[0], 0.0, MASKED)
        tail_k = jnp.where(line == 0, bias, jnp.where(line < 4, 1.0, 0.0)).astype(BF)

        def turned(block):
            a, b = block[: HD // 2], block[HD // 2 :]
            return jnp.concatenate([a * c - b * s, b * c + a * s], axis=0).astype(BF)

        for h in range(heads):
            top = h * 3 * HD
            q = turned(mixed[top : top + HD]).astype(F32) * SCALE
            k = turned(mixed[top + HD : top + 2 * HD])
            v = mixed[top + 2 * HD : top + 3 * HD].astype(BF)
            kf = k.astype(F32)
            q_t[h, :, at] = jnp.concatenate([q.astype(BF), ones_q, blank], axis=0)
            k_t[h, :, at] = k
            v_t[h, :, at] = jnp.concatenate([v, ones_q], axis=0)
            k_n[h, at, :] = jnp.concatenate([k, tail_k, blank], axis=0).T
            v_n[h, at, :] = jnp.concatenate([v, tail_v, blank], axis=0).T
            qn[h, :, at] = jnp.broadcast_to(jnp.sum(q * q, axis=0, keepdims=True), (8, rows))
            kn[h, :, at] = jnp.broadcast_to(jnp.sum(kf * kf, axis=0, keepdims=True), (8, rows))


def project(col, pos_a, pos_b, lengths, xs, packs, cos, sin, width):
    t = 4 * xs[0].shape[0]
    heads = width // (3 * HD)
    made = lambda n, dt=BF: jax.ShapeDtypeStruct((heads, n, t), dt)
    natural = jax.ShapeDtypeStruct((heads, t, 128), BF)
    return vmem_call(
        project_kernel,
        [made(128), made(HD), made(VAUG), natural, natural, made(8, F32), made(8, F32)],
        [pltpu.VMEM((D, width), BF), pltpu.VMEM((width, D), BF)],
        4 * t * D * width,
        "project",
        (col, pos_a, pos_b, lengths),
        *xs, *packs, in_hbm(cos), in_hbm(sin),
        mib=14,
    )


def attend_kernel(q_t, k_n, v_t, qn, kn, out, inverse, kept, q_s):
    n = k_n.shape[1]
    chunk = min(1024, n)
    bq = q_t.shape[2]
    q_s[...] = q_t[0]

    @pl.when(jnp.max(qn[0]) * jnp.max(kn[0]) > SAFE_SCORE * SAFE_SCORE)
    def _():
        best = jnp.full((1, bq), -jnp.inf, F32)
        for i in range(n // 256):
            s = mm(k_n[0, i * 256 : (i + 1) * 256, :], q_t[0], NN)
            best = jnp.maximum(best, jnp.max(s, axis=0, keepdims=True))
        high = best.astype(BF).astype(F32)
        low = (best - high).astype(BF).astype(F32)
        line = lax.broadcasted_iota(jnp.int32, (16, bq), 0)
        tail = jnp.where(line == 0, 1.0, jnp.where(line == 1, -high, jnp.where(line == 2, -low, 0.0)))
        q_s[HD : HD + 16, :] = tail.astype(BF)

    q = q_s[...]
    total = None
    for i in range(n // chunk):
        at = slice(i * chunk, (i + 1) * chunk)
        p = jnp.exp(mm(k_n[0, at, :], q, NN)).astype(BF)
        kept[0, at, :] = p
        part = mm(v_t[0, :, at], p, NN)
        total = part if total is None else total + part
    scale = 1.0 / total[HD : HD + 1]
    out[0] = (total[:HD] * scale).astype(BF)
    inverse[0] = jnp.broadcast_to(scale, inverse.shape[1:])


def attend(q_t, k_n, v_t, qn, kn, half):
    heads, _, t = q_t.shape
    bq = t // 2
    lane = lambda rows, at=half: pl.BlockSpec((1, rows, bq), lambda h: (h, 0, at))
    return pl.pallas_call(
        attend_kernel,
        grid=(heads,),
        in_specs=[
            lane(128),
            pl.BlockSpec((1, t, 128), lambda h: (h, 0, 0)),
            pl.BlockSpec((1, VAUG, t), lambda h: (h, 0, 0)),
            lane(8),
            pl.BlockSpec((1, 8, t), lambda h: (h, 0, 0)),
        ],
        out_specs=[lane(HD, 0), lane(8, 0), pl.BlockSpec((1, t, bq), lambda h: (h, 0, 0))],
        out_shape=[
            jax.ShapeDtypeStruct((heads, HD, bq), BF),
            jax.ShapeDtypeStruct((heads, 8, bq), F32),
            pltpu.HBM((heads, t, bq), BF),
        ],
        scratch_shapes=[pltpu.VMEM((128, bq), BF)],
        compiler_params=params(24),
        cost_estimate=cost(heads * 2 * 2 * bq * t * 256, heads * t * 512),
        name="attend",
    )(q_t, k_n, v_t, qn, kn)


def split3(value):
    a = value.astype(BF).astype(F32)
    b = (value - a).astype(BF).astype(F32)
    return a, b, value - a - b


def turn_back(grad, c, s):
    a, b = grad[: HD // 2], grad[HD // 2 :]
    return jnp.concatenate([a * c + b * s, b * c - a * s], axis=0)


def relative(table, col, first, count):
    rows = table.shape[1] // 4
    starts = [pl.multiple_of((i ^ col[0]) * rows, 128) for i in range(first, first + count)]
    return jnp.concatenate([table[:, pl.ds(at, rows)] for at in starts], axis=1)


def attend_back_kernel(first, col, kept, inverse, q_t, o_t, do_t, k_t, v_n, cos, sin, *refs):
    if first:
        dq, dk, dv, do_s = refs
    else:
        dk_in, dv_in, dq, dk, dv, do_s, dk_s = refs
    n = v_n.shape[1]
    chunk = min(512, n)
    bq = q_t.shape[2]
    line = lax.broadcasted_iota(jnp.int32, (16, bq), 0)
    do = do_t[0].astype(F32) * inverse[0, :1]
    a, b, c = split3(-jnp.sum(do * o_t[0].astype(F32), axis=0, keepdims=True))
    tail = jnp.where(line == 0, a, jnp.where(line == 1, b, jnp.where(line == 2, c, 0.0)))
    do_s[:HD, :] = do.astype(BF)
    do_s[HD : HD + 16, :] = tail.astype(BF)
    do_s[HD + 16 :, :] = jnp.zeros((48, bq), BF)
    do = do_s[...]
    do64, q64 = do_s[:HD, :], q_t[0, :HD, :]
    total = None
    for i in range(n // chunk):
        at = slice(i * chunk, (i + 1) * chunk)
        p = kept[0, at, :]
        gs = (p.astype(F32) * mm(v_n[0, at, :], do, NN)).astype(BF)
        part = mm(k_t[0, :, at], gs, NN)
        total = part if total is None else total + part
        gv = mm(do64, p, NT)
        gk = mm(q64, gs, NT)
        if first:
            dv[0, :, at] = gv
            dk[0, :, at] = gk
        else:
            dv[0, :, at] = (gv + dv_in[0, :, at]).astype(BF)
            dk_s[:, at] = gk + dk_in[0, :, at]
    near = 0 if first else 2
    dq[0] = turn_back(total * SCALE, relative(cos, col, near, 2), relative(sin, col, near, 2)).astype(BF)
    if not first:
        dk[0] = turn_back(dk_s[...], relative(cos, col, 0, 4), relative(sin, col, 0, 4)).astype(BF)


def attend_back(col, q_t, kept, inverse, o_t, do_t, k_t, v_n, cos, sin, half, sums=None):
    heads, _, t = q_t.shape
    bq = t // 2
    first = sums is None
    lane = lambda rows, at=0: pl.BlockSpec((1, rows, bq), lambda h, *_: (h, 0, at))
    full = lambda rows: pl.BlockSpec((1, rows, t), lambda h, *_: (h, 0, 0))
    tall = lambda lanes: pl.BlockSpec((1, t, lanes), lambda h, *_: (h, 0, 0))
    table = const_spec(cos)
    made = F32 if first else BF
    more = () if first else tuple(sums)
    return pl.pallas_call(
        functools.partial(attend_back_kernel, first),
        grid_spec=pltpu.PrefetchScalarGridSpec(
            num_scalar_prefetch=1,
            grid=(heads,),
            in_specs=[tall(bq), lane(8), lane(128, half), lane(HD), lane(HD), full(HD), tall(128), table, table]
            + ([] if first else [full(HD), full(HD)]),
            out_specs=[lane(HD), full(HD), full(HD)],
            scratch_shapes=[pltpu.VMEM((128, bq), BF)]
            + ([] if first else [pltpu.VMEM((HD, t), F32)]),
        ),
        out_shape=[
            jax.ShapeDtypeStruct((heads, HD, bq), BF),
            jax.ShapeDtypeStruct((heads, HD, t), made),
            jax.ShapeDtypeStruct((heads, HD, t), made),
        ],
        compiler_params=params(28),
        cost_estimate=cost(heads * 4 * 2 * bq * t * 256, heads * t * 2048),
        name="attend_back",
    )(col, in_hbm(kept), inverse, q_t, o_t, do_t, k_t, v_n, in_hbm(cos), in_hbm(sin), *more)


def fill_out(w, packs, other, pos_a, pos_b):
    width = w.shape[2]
    half = BLOCK // 2
    for k, src in enumerate(packs):
        part, pos, first = k // 2, (pos_a, pos_b)[k // 2], k % 2 * (ROWS // 2)
        fill(w.at[0], src, pos, part * half, half, 0, width, 0, slice(OUT_AT, OUT_AT + width), first)
        fill(w.at[1], other.at[pl.ds(part * ROWS + first, ROWS // 2)], pos, part * half, half, 0, width, 0, first=first)


def out_kernel(pos_a, pos_b, h_own, h_other, wa, wa2, wb, wb2, other, keep, send, w):
    fill_out(w, (wa, wa2, wb, wb2), other, pos_a, pos_b)
    rows = keep.shape[0]
    for part, out in ((1, send), (0, keep)):
        at = slice(part * rows, (part + 1) * rows)
        total = mm(h_own[:, at].T, w[0], NT) + mm(h_other[:, at].T, w[1], NT)
        out[...] = total.astype(out.dtype)


def out_back_kernel(
    pos_a, pos_b, ga_own, ga_own2, ga_near, ga_near2, sums, h_own, h_other, wa, wa2, wb, wb2, other,
    gh_own, gh_other, keep, send, sums_out, w, ga,
):
    fill_out(w, (wa, wa2, wb, wb2), other, pos_a, pos_b)
    rows = ga_own.shape[0]
    for k, ref in enumerate((ga_own, ga_own2, ga_near, ga_near2)):
        ga[k * rows : (k + 1) * rows] = ref[:rows]
    total = sums[...] + unride(ga_near2[rows:])
    sums_out[...] = total
    send[h_own.shape[0] :, :] = ride(total)
    for half, (h, gh, g) in enumerate(((h_own, gh_own, keep), (h_other, gh_other, send))):
        gh[...] = mm(w[half].T, ga[...], NT).astype(BF)
        g[: h.shape[0], :] = mm(h[...], ga[...], NN).astype(BF)


def const_spec(a):
    return pl.BlockSpec(a.shape, lambda i, *_: (0,) * len(a.shape))


def in_hbm(x):
    return pltpu.with_memory_space_constraint(x, pltpu.HBM)


def vmem_call(kernel, out_shape, scratch, work, name, scalars, *args, mib=10, hbm_out=()):
    out_shape = [pltpu.HBM(o.shape, o.dtype) if k in hbm_out else o for k, o in enumerate(out_shape)]
    nbytes = sum(math.prod(a.shape) * a.dtype.itemsize for a in list(args) + list(out_shape))
    return pl.pallas_call(
        kernel,
        grid_spec=pltpu.PrefetchScalarGridSpec(
            num_scalar_prefetch=len(scalars),
            grid=(1,),
            in_specs=[const_spec(a) for a in args],
            out_specs=[const_spec(a) for a in out_shape],
            scratch_shapes=scratch,
        ),
        out_shape=out_shape,
        compiler_params=params(mib),
        cost_estimate=cost(work, nbytes),
        name=name,
    )(*scalars, *args)


def out_project(pos_a, pos_b, h_own, h_other, packs, other):
    rows = h_own.shape[1] // 2
    width = h_own.shape[0]
    return vmem_call(
        out_kernel,
        [jax.ShapeDtypeStruct((rows, D), F32), jax.ShapeDtypeStruct((rows, D), BF)],
        [pltpu.VMEM((2, D, width), BF)],
        2 * 2 * rows * D * 2 * width,
        "out_project",
        (pos_a, pos_b),
        h_own, h_other, *packs, other,
    )


def out_back(pos_a, pos_b, gas, sums, h_own, h_other, packs, other):
    t = 4 * gas[0].shape[0]
    width = h_own.shape[0]
    gh = jax.ShapeDtypeStruct((width, t), BF)
    grad = jax.ShapeDtypeStruct((width, D), BF)
    return vmem_call(
        out_back_kernel,
        [gh, gh, grad, jax.ShapeDtypeStruct((width + RIDE, D), BF), jax.ShapeDtypeStruct((8, D), F32)],
        [pltpu.VMEM((2, D, width), BF), pltpu.VMEM((t, D), BF)],
        2 * 2 * t * D * 2 * width,
        "out_back",
        (pos_a, pos_b),
        *gas, sums, h_own, h_other, *packs, other,
    )


FF_STEPS = 3


def assemble_kernel(pos, *refs):
    a, b, (g, u, d) = refs[:4], refs[4:8], refs[8:]
    lanes = a[0].shape[2]
    half = BLOCK // 2
    for k in range(4):
        to, first = k // 2 * lanes, k % 2 * (ROWS // 2)
        fill(g, a[k], pos.at[0], 0, BLOCK, 0, lanes, to, first=first)
        fill(u, b[k], pos.at[1], 0, BLOCK, 0, lanes, to, first=first)
        fill(d, a[k], pos.at[0], 0, half, BLOCK, lanes, to, first=first)
        fill(d, b[k], pos.at[1], half, half, BLOCK, lanes, to, first=first)


def assemble(pos, a_own, a_near, b_own, b_near):
    made = jax.ShapeDtypeStruct((D, 2 * a_own[0].shape[2]), BF)
    refs = [in_hbm(x) for x in (*a_own, *a_near, *b_own, *b_near)]
    return vmem_call(
        assemble_kernel, [made] * 3, [], 6 * D * made.shape[1], "assemble", (pos,), *refs, mib=24
    )


def place_call(kernel, pos, given, base, outs, scratch, work, name):
    in_vmem = pl.BlockSpec(memory_space=pltpu.VMEM)
    nbytes = sum(math.prod(o.shape) * 4 for o in outs)
    return list(pl.pallas_call(
        kernel,
        in_specs=[pl.BlockSpec(memory_space=pltpu.SMEM)] + [in_vmem] * (len(given) + len(base)),
        out_specs=[in_vmem] * len(outs),
        out_shape=outs,
        scratch_shapes=scratch,
        input_output_aliases={1 + len(given) + k: k for k in range(len(base))},
        compiler_params=params(),
        cost_estimate=cost(work, nbytes),
        name=name,
    )(pos, *given, *base))


def steps(units):
    width = units // FF_STEPS
    return [slice(k * width, (k + 1) * width) for k in range(FF_STEPS)]


def ffn_kernel(x_own, x_far, wg, wu, wd, gate, up, keep, send, x):
    rows = x_own.shape[0]
    x[:rows] = x_own[...]
    x[rows:] = x_far[...]
    total = None
    for at in steps(wg.shape[1]):
        g = mm(x[...], wg[:, at], NN)
        u = mm(x[...], wu[:, at], NN)
        gate[:, at] = g.astype(BF)
        up[:, at] = u.astype(BF)
        part = mm((g * jax.nn.sigmoid(g) * u).astype(BF), wd[:, at], NT)
        total = part if total is None else total + part
    keep[...] = total[:rows]
    send[...] = total[rows:].astype(BF)


def ffn_back_kernel(gb_own, gb_far, wg, wu, wd, gate, up, hid, ggate, gup, keep, send, gb):
    rows = gb_own.shape[0]
    gb[:rows] = gb_own[...]
    gb[rows:] = gb_far[...]
    total = None
    for at in steps(wg.shape[1]):
        gh = mm(gb[...], wd[:, at], NN)
        g, u = gate[:, at].astype(F32), up[:, at].astype(F32)
        sig = jax.nn.sigmoid(g)
        silu = g * sig
        hid[:, at] = (silu * u).astype(BF)
        gga = (gh * u * sig * (1.0 + g * (1.0 - sig))).astype(BF)
        gua = (gh * silu).astype(BF)
        ggate[:, at] = gga
        gup[:, at] = gua
        part = mm(gga, wg[:, at], NT) + mm(gua, wu[:, at], NT)
        total = part if total is None else total + part
    keep[...] = total[:rows]
    send[...] = total[rows:].astype(BF)


def ffn_grad_kernel(n, which, pos, *refs):
    xs, acts = refs[: 2 * n], refs[2 * n : 3 * n]
    outs, (x_t, grad) = refs[-6 if which is None else -4 : -2], refs[-2:]
    rows = xs[0].shape[0]
    for k in range(2 * n):
        x_t[:, k * rows : (k + 1) * rows] = xs[k][...].T
    lanes = outs[0].shape[2]
    half = BLOCK // 2
    wide = grad.shape[1]

    def product(right, at):
        total = None
        for k in range(n):
            part = mm(x_t[:, 2 * k * rows : 2 * (k + 1) * rows], right[k][:, at], NN)
            total = part if total is None else total + part
        grad[...] = total

    def out(src_pos, dst, start, count, to, cols):
        for j in range(ROWS):
            place = pl.multiple_of(src_pos[j] * BLOCK + start, 16)
            dst[j, to : to + count, cols] = grad[pl.ds(place, count), :].astype(BF)

    for part in range(2):
        for lo in range(0, lanes, wide):
            cols, at = slice(lo, lo + wide), slice(part * lanes + lo, part * lanes + lo + wide)
            product(acts, at)
            if which is None:
                out(pos.at[0], outs[2 * part], 0, half, BLOCK, cols)
                out(pos.at[1], outs[2 * part + 1], half, half, BLOCK, cols)
            else:
                out(pos.at[which], outs[part], 0, BLOCK, 0, cols)


def ffn_grad(pos, xs, acts, which, lanes, base=()):
    n = len(acts)
    rows = xs[0].shape[0]
    blocks = jax.ShapeDtypeStruct((ROWS, BLOCK * 3 // 2, lanes), BF)
    kernel = functools.partial(ffn_grad_kernel, n, which)
    scratch = [pltpu.VMEM((D, 2 * n * rows), BF), pltpu.VMEM((D, lanes // 3), F32)]
    work = n * rows * D * lanes
    outs = [blocks] * (4 if which is None else 2)
    return place_call(kernel, pos, list(xs) + acts, base, outs, scratch, work, "ffn_grad")


def ffn(x_own, x_far, weights):
    rows = x_own.shape[0]
    units = weights[0].shape[1]
    acts = jax.ShapeDtypeStruct((2 * rows, units), BF)
    ends = [jax.ShapeDtypeStruct((rows, D), F32), jax.ShapeDtypeStruct((rows, D), BF)]
    scratch = [pltpu.VMEM((2 * rows, D), BF)]
    work = 12 * rows * D * units
    return vmem_call(
        ffn_kernel, [acts, acts] + ends, scratch, work, "ffn", (), x_own, x_far, *weights,
        hbm_out=(0, 1),
    )


def ffn_back(gb_own, gb_far, weights, gate, up):
    rows = gb_own.shape[0]
    units = weights[0].shape[1]
    acts = jax.ShapeDtypeStruct((2 * rows, units), BF)
    ends = [jax.ShapeDtypeStruct((rows, D), F32), jax.ShapeDtypeStruct((rows, D), BF)]
    scratch = [pltpu.VMEM((2 * rows, D), BF)]
    work = 12 * rows * D * units
    return vmem_call(
        ffn_back_kernel, [acts] * 3 + ends, scratch, work, "ffn_back", (), gb_own, gb_far, *weights, in_hbm(gate), in_hbm(up),
        mib=20,
    )


def units_of(h):
    centre = jnp.mean(h, axis=1, keepdims=True)
    away = h - centre
    scale = lax.rsqrt(jnp.mean(away * away, axis=1, keepdims=True) + NORM_EPSILON)
    return away * scale, scale


def back_through(grad, unit, scale, gain):
    scaled = grad * gain
    mean = jnp.mean(scaled, axis=1, keepdims=True)
    crossed = jnp.mean(scaled * unit, axis=1, keepdims=True)
    return scale * (scaled - mean - unit * crossed)


def columns(value):
    return jnp.sum(value, axis=0, keepdims=True)


def first_kernel(tokens, keep, came, norm, first, *refs):
    h = tokens[...].astype(F32) + keep[...] + came[...].astype(F32)
    first[...] = h
    unit, _ = units_of(h)
    normed = (unit * norm[0:1] + norm[1:2]).astype(BF)
    rows = refs[0].shape[0]
    for k, low in enumerate(refs):
        k = k % (len(refs) // 2)
        low[...] = normed[k * rows : (k + 1) * rows]


def norm_one(tokens, keep, came, norm, chunks):
    rows = tokens.shape[0]
    return vmem_call(
        first_kernel,
        [jax.ShapeDtypeStruct((rows, D), F32)] + [jax.ShapeDtypeStruct((rows // chunks, D), BF)] * 2 * chunks,
        [], 12 * rows * D, "first_norm", (), tokens, keep, came, norm, hbm_out=[0, *range(1 + chunks, 1 + 2 * chunks)],
    )


def second_kernel(place, first, keep, came, cotangent, norm, result, grad, low, low_too, sums):
    rows = result.shape[0]
    unit, _ = units_of(first[...])
    normed = unit * norm[0:1] + norm[1:2]
    unit, scale = units_of(normed + keep[...] + came[...].astype(F32))
    out = unit * norm[2:3] + norm[3:4]
    result[...] = out.astype(BF)
    position = place[0] + lax.broadcasted_iota(jnp.int32, (rows, 1), 0)
    weight = (position < place[1]).astype(F32)
    g = cotangent[...].astype(F32) * weight
    back = back_through(g, unit, scale, norm[2:3])
    grad[...] = back
    low[...] = back.astype(BF)
    low_too[...] = back.astype(BF)
    sums[...] = jnp.concatenate(
        [jnp.zeros((2, D), F32), columns(g * unit), columns(g), columns(out * out * weight), jnp.zeros((3, D), F32)],
        axis=0,
    )


def chunk_call(kernel, k, scalars, chunked, whole, out_shape, name, work):
    rows = out_shape[0].shape[0]
    part = pl.BlockSpec((rows, D), lambda i, *_: (k, 0))
    return pl.pallas_call(
        kernel,
        grid_spec=pltpu.PrefetchScalarGridSpec(
            num_scalar_prefetch=len(scalars),
            grid=(1,),
            in_specs=[part] * len(chunked) + [const_spec(a) for a in whole],
            out_specs=[const_spec(a) for a in out_shape],
        ),
        out_shape=out_shape,
        compiler_params=params(),
        cost_estimate=cost(work, 20 * rows * D),
        name=name,
    )(*scalars, *chunked, *whole)


def norm_two(k, place, first, keep, came, cotangent, norm):
    rows = keep.shape[0]
    made = lambda kind: pltpu.HBM((rows, D), kind)
    send = jax.ShapeDtypeStruct((rows, D), BF)
    kernel = lambda place, first, cot, keep, came, *rest: second_kernel(place, first, keep, came, cot, *rest)
    return chunk_call(
        kernel, k, (place,), (first, cotangent), (keep, came, norm),
        [made(BF), made(F32), send, made(BF), jax.ShapeDtypeStruct((8, D), F32)], "second_norm", 30 * rows * D,
    )


def first_back_kernel(n, first, second, keep, came, norm, *refs):
    prior, (grad, low, sums) = refs[:n], refs[n:]
    rows = grad.shape[0]
    unit, scale = units_of(first[...])
    g = second[...] + keep[...] + came[...].astype(F32)
    back = back_through(g, unit, scale, norm[0:1])
    grad[...] = back
    low[:rows] = back.astype(BF)
    total = jnp.concatenate([columns(g * unit), columns(g), jnp.zeros((6, D), F32)], axis=0)
    for ref in prior:
        total = total + ref[...]
    sums[...] = total
    if n:
        low[rows:] = ride(total)


def norm_one_back(k, first, second, keep, came, norm, prior=()):
    rows = keep.shape[0]
    more = RIDE if prior else 0
    outs = [
        jax.ShapeDtypeStruct((rows, D), F32),
        jax.ShapeDtypeStruct((rows + more, D), BF),
        jax.ShapeDtypeStruct((8, D), F32),
    ]
    return chunk_call(
        functools.partial(first_back_kernel, len(prior)), k, (), (first,), (second, keep, came, norm, *prior),
        outs, "first_norm_back", 20 * rows * D,
    )


def token_kernel(n, pos_a, pos_b, *refs):
    groups, refs = [refs[3 * k : 3 * k + 3] for k in range(n)], refs[3 * n :]
    packs, base, (near, far, w) = refs[:4], refs[4:-3], refs[-3:]
    fill_qkv(w, packs, pos_a, pos_b)
    rows = near.shape[0]
    for part, out in ((1, far), (0, near)):
        at = slice(part * rows, (part + 1) * rows)
        mixed = [ref[h, :, at] for group in groups for h in range(group[0].shape[0]) for ref in group]
        total = mm(jnp.concatenate(mixed, axis=0).T, w[...], NT)
        if part == 0 and base:
            total = total + jnp.concatenate([ref[...] for ref in base], axis=0)
        out[...] = total.astype(out.dtype)


def token_terms(pos_a, pos_b, groups, packs, half, base=()):
    bq = groups[0][0].shape[2]
    width = sum(g[0].shape[0] for g in groups) * 3 * HD
    lane = lambda a, at: pl.BlockSpec((a.shape[0], HD, bq), lambda i, *_: (0, 0, at))
    flat = [a for g in groups for a in g]
    out = [jax.ShapeDtypeStruct((bq // 2, D), kind) for kind in (F32, BF)]
    return pl.pallas_call(
        functools.partial(token_kernel, len(groups)),
        grid_spec=pltpu.PrefetchScalarGridSpec(
            num_scalar_prefetch=2,
            grid=(1,),
            in_specs=[lane(a, half if k % 3 else 0) for k, a in enumerate(flat)]
            + [const_spec(a) for a in (*packs, *base)],
            out_specs=[const_spec(a) for a in out],
            scratch_shapes=[pltpu.VMEM((D, width), BF)],
        ),
        out_shape=out,
        compiler_params=params(),
        cost_estimate=cost(2 * bq * D * width, bq * (D + width) * 4),
        name="token_terms",
    )(pos_a, pos_b, *flat, *packs, *base)


def total_kernel(keep, near, far, out):
    out[...] = keep[...] + near[...].astype(F32) + far[...].astype(F32)


def total_grad(keep, near, far):
    rows = keep.shape[0]
    part = pl.BlockSpec((rows // 4, D), lambda i: (i, 0))
    return pl.pallas_call(
        total_kernel,
        grid=(4,),
        in_specs=[part] * 3,
        out_specs=part,
        out_shape=jax.ShapeDtypeStruct((rows, D), F32),
        compiler_params=params(),
        cost_estimate=cost(2 * rows * D, 12 * rows * D),
        name="total_grad",
    )(keep, near, far)


def qkv_grad_kernel(n, pos_a, pos_b, *refs):
    groups, refs = [refs[4 * k : 4 * k + 4] for k in range(n)], refs[4 * n :]
    x0, x1, x2, x3, out_own, out_came, sums, a_k, b_k, a_s, b_s, sums_out, g, go = refs
    rows = x0.shape[0]
    total = None
    for k, x in enumerate((x0, x1, x2, x3)):
        at, to = slice(k * rows, (k + 1) * rows), slice(k % 2 * rows, (k % 2 + 1) * rows)
        mixed = []
        for *dqs, dk, dv in groups:
            for h in range(dk.shape[0]):
                mixed += [dqs[k // 2][h, :, to], dk[h, :, at], dv[h, :, at]]
        part = mm(jnp.concatenate(mixed, axis=0), x[...], NN)
        total = part if total is None else total + part
    g[...] = total.T
    half = BLOCK // 2
    width, out_width = g.shape[1], go.shape[1]
    go[...] = (out_own[...].astype(F32) + out_came[:out_width].astype(F32)).T
    total = sums[...] + unride(out_came[out_width:])
    sums_out[...] = total
    gap = jnp.zeros((half, OUT_AT - width), BF)
    for part, (pos, k, s) in enumerate(((pos_a, a_k, a_s), (pos_b, b_k, b_s))):
        for j in range(ROWS):
            at = pl.ds(pl.multiple_of(pos[j] * BLOCK + part * half, 16), half)
            piece = jnp.concatenate([g[at, :].astype(BF), gap, go[at, :].astype(BF)], axis=1)
            if j < ROWS // 2:
                k[j] = piece
            elif part:
                s[j - ROWS // 2] = piece
            else:
                s[(j - ROWS // 2) * half : (j - ROWS // 2 + 1) * half, :] = piece
    a_s[ROWS // 2 * half :, :D] = ride(total)
    a_s[ROWS // 2 * half :, D:] = jnp.zeros((RIDE, a_s.shape[1] - D), BF)


def qkv_grad(pos_a, pos_b, groups, xs, out_own, out_came, sums):
    out_width = out_own.shape[0]
    blocks = jax.ShapeDtypeStruct((ROWS // 2, BLOCK // 2, OUT_AT + out_width), BF)
    send = jax.ShapeDtypeStruct((ROWS // 2 * (BLOCK // 2) + RIDE, OUT_AT + out_width), BF)
    width = 3 * HD * sum(g[0].shape[0] for g in groups)
    return vmem_call(
        functools.partial(qkv_grad_kernel, len(groups)),
        [blocks, blocks, send, blocks, jax.ShapeDtypeStruct((8, D), F32)],
        [pltpu.VMEM((D, width), F32), pltpu.VMEM((D, out_width), F32)],
        8 * xs[0].shape[0] * D * width,
        "qkv_grad",
        (pos_a, pos_b),
        *[a for g in groups for a in g], *xs, out_own, out_came, sums,
    )


def adamw(weight, gradient, first_state, second_state, step_rate, decay_rate):
    first_new = FIRST_DECAY * first_state + (1.0 - FIRST_DECAY) * gradient
    second_new = SECOND_DECAY * second_state + (1.0 - SECOND_DECAY) * gradient * gradient
    first_hat = first_new / (1.0 - FIRST_DECAY**STEP)
    second_hat = second_new / (1.0 - SECOND_DECAY**STEP)
    weight_new = weight - step_rate * (
        first_hat / (jnp.sqrt(second_hat) + ADAM_EPSILON) + decay_rate * weight
    )
    return (weight_new, first_new, second_new)


RATE_MAIN = 2.0 / math.sqrt(D)
RATE_OUT = 2.0 / math.sqrt(D * 16 // SEQ)
RATE_DOWN = 2.0 / math.sqrt(FF)


def update(grad, states, outs, rate):
    w, m, v = (ref[...] for ref in states)
    new, first, second = adamw(w, grad, m, v, rate, MATRIX_DECAY)
    for ref, value in zip(outs, (new, first, second, new.astype(BF))):
        ref[...] = value


def ffn_update_kernel(a, b, a_came, b_came, *refs):
    states, outs = refs[:9], refs[9:]
    ga = a[0].astype(F32) + a_came[0].astype(F32)
    gb = b[0].astype(F32) + b_came[0].astype(F32)
    rows = states[0].shape[0]
    update(ga[:rows], states[:3], outs[:4], RATE_MAIN)
    update(gb[:rows], states[3:6], outs[4:8], RATE_MAIN)
    update(jnp.concatenate([ga[rows:], gb[rows:]], axis=0), states[6:], outs[8:], RATE_DOWN)


def pack_update_kernel(a, b, came, sums, *refs):
    states, outs = refs[:9], refs[9:]
    rows = a.shape[1]
    ga = a[0].astype(F32) + came[:rows].astype(F32)
    gb = b[0].astype(F32) + came[rows + RIDE :].astype(F32)
    grad = jnp.concatenate([ga, gb], axis=0)
    width = states[0].shape[1]
    update(grad[:, :width], states[:3], outs[:4], RATE_MAIN)
    update(grad[:, OUT_AT:].T, states[3:6], outs[4:8], RATE_OUT)
    total = sums[...] + unride(came[rows : rows + RIDE, :D])
    w, m, v = (ref[...] for ref in states[6:])
    for ref, value in zip(outs[8:], adamw(w, total[:4], m, v, NORM_RATE, 0.0)):
        ref[...] = value
    outs[11][...] = jnp.broadcast_to(jnp.sum(total[4:5], axis=1, keepdims=True), outs[11].shape)


def updated(kernel, given, states, name, more=()):
    outs = []
    for w, _, _ in states:
        outs += [pltpu.HBM(w.shape, F32)] * 3 + [pltpu.HBM(w.shape, BF)]
    flat = [pltpu.with_memory_space_constraint(x, pltpu.HBM) for state in states for x in state]
    work = sum(20 * math.prod(w.shape) for w, _, _ in states)
    rest = [x for state in more for x in state]
    for w, _, _ in more:
        outs += [jax.ShapeDtypeStruct(w.shape, F32)] * 3 + [jax.ShapeDtypeStruct((8, 128), F32)]
    return vmem_call(kernel, outs, [], work, name, (), *given, *flat, *rest)


def rope_tables(length):
    position = np.arange(length, dtype=np.float32)
    inverse = np.exp(np.arange(HD // 2, dtype=np.float32) * np.float32(-2.0 * math.log(ROPE_BASE) / HD))
    angle = (inverse.astype(np.float32)[:, None] * position[None, :]).astype(np.float64)
    return np.cos(angle).astype(np.float32), np.sin(angle).astype(np.float32)


def on_device(
    tokens, cotangent, lengths, w_qkv, w_out, w_gate, w_up, w_down, norm_params,
    m_qkv, v_qkv, m_out, v_out, m_gate, v_gate, m_up, v_up, m_down, v_down, m_norm, v_norm,
):
    own_rows = tokens.shape[0]
    seq_rows = own_rows * lax.axis_size("col")
    col = lax.axis_index("col").astype(jnp.int32)
    row = lax.axis_index("row").astype(jnp.int32)
    small = lax.axis_size("row") == ROWS
    me = row if small else row * 0
    qkv_width = w_qkv.shape[1]
    head_width = qkv_width // 3
    heads = head_width // HD
    half = BLOCK // 2
    chunks = 2

    places = lambda order: jnp.stack([me ^ row_mask(order, j) for j in range(ROWS)])
    pos_a, pos_b = places(ORDER_QA), places(ORDER_QB)
    pos_f = jnp.stack([places(ORDER_A), places(ORDER_B)])

    near = swap(tokens, "c")
    far = swap(tokens, "y")
    if small:
        part = (BLOCK + half, w_gate.shape[1])
        shapes = [jax.ShapeDtypeStruct(n, BF) for n in ((BLOCK, OUT_AT + head_width), part, part)]
        given = [in_hbm(w) for w in (w_qkv, w_out, w_gate, w_up, w_down.T)]
        pack, fa, fb = vmem_call(pack_kernel, shapes, [], 0, "pack", (), *given)
        pack, fa, fb = pack[None], fa[None], fb[None]
        pack_came, fa, fb = tie(swap(pack, "1"), fa, fb)
        ff_came = swap(fa, "1"), swap(fb, "0")
        both = jnp.concatenate([pack, pack_came], axis=0)
        qa, qb = both[:, :half], both[:, half:]
        came = swap(qa, "x"), swap(qb, "0")
        *ff_came, qa_came, qb_came = tie(*ff_came, *came)
        qa, qb = jnp.concatenate([qa, qa_came], axis=0), jnp.concatenate([qb, qb_came], axis=0)
        came = swap(qa, "0"), swap(qb, "x")
        fa, fb = jnp.concatenate([fa, ff_came[0]], axis=0), jnp.concatenate([fb, ff_came[1]], axis=0)
        packs = (qa, came[0], qb, came[1])
        ff_came = swap(fa, "x"), swap(fb, "1")
    else:
        gap = jnp.zeros((w_qkv.shape[0], OUT_AT - qkv_width), BF)
        pack = jnp.concatenate([w_qkv.astype(BF), gap, w_out.T.astype(BF)], axis=1)
        low_down = w_down.T.astype(BF)
        low_gate, low_up = w_gate.astype(BF), w_up.astype(BF)
        wa = gather_plain(pack, ORDER_QA, 0, half)
        wb = gather_plain(pack, ORDER_QB, half, half)
        packs = (wa[: ROWS // 2], wa[ROWS // 2 :], wb[: ROWS // 2], wb[ROWS // 2 :])
        join = lambda w, order, start: jnp.concatenate(
            [gather_plain(w, order, 0, BLOCK), gather_plain(low_down, order, start, half)], axis=1
        )
        fa, fb = join(low_gate, ORDER_A, 0), join(low_up, ORDER_B, half)
        fa, fb, fa2, fb2 = fa[: ROWS // 2], fb[: ROWS // 2], fa[ROWS // 2 :], fb[ROWS // 2 :]
    far_near = swap(far, "c")
    blocks = (tokens, near, far, far_near)

    cos_np, sin_np = rope_tables(seq_rows)
    cos, sin = jnp.asarray(cos_np), jnp.asarray(sin_np)
    q_t, k_t, v_t, k_n, v_n, qn, kn = project(
        col[None], pos_a, pos_b, lengths, blocks, packs, cos, sin, qkv_width
    )
    wo_far = swap(jnp.concatenate([p[:, :, OUT_AT:] for p in packs], axis=0), "y")
    if small:
        fa_came, q_t = tie(ff_came[0], q_t)
        fa, q_t = tie(jnp.concatenate([fa, fa_came], axis=0), q_t)
        fa2 = swap(fa, "0")
    far_heads, far_inv, far_kept = attend(q_t, k_n, v_t, qn, kn, 1)
    if small:
        fb_came, far_heads, q_t = tie(ff_came[1], far_heads, q_t)
        fb, q_t = tie(jnp.concatenate([fb, fb_came], axis=0), q_t)
        fb2 = swap(fb, "x")
    fa_c, fb_c = swap(fa, "c"), swap(fb, "c")
    if small:
        far_heads, wo_far = tie(far_heads, wo_far)
    other_heads = swap(far_heads.reshape(head_width, seq_rows // 2), "y")
    own_heads, own_inv, own_kept = attend(q_t, k_n, v_t, qn, kn, 0)
    flat_heads = own_heads.reshape(head_width, seq_rows // 2)
    if small:
        flat_heads, other_heads = tie(flat_heads, other_heads)

    keep, send = out_project(pos_a, pos_b, flat_heads, other_heads, packs, wo_far)
    if small:
        fa2, fb2, keep = tie(fa2, fb2, keep)
    fa2_c, fb2_c = swap(fa2, "c"), swap(fb2, "c")
    first, *normed = norm_one(tokens, keep, swap(send, "c"), norm_params, chunks)
    normed_far = [swap(n, "y") for n in normed[:chunks]]
    normed = normed[chunks:]
    weights = assemble(pos_f, (fa, fa2), (fa_c, fa2_c), (fb, fb2), (fb_c, fb2_c))
    place = lambda k: jnp.stack([col * own_rows + k * (own_rows // chunks), lengths[0]])
    fwd, sums, results, seconds, lows, lows_far = [], [], [], [], [], []
    for k in range(chunks):
        fwd.append(ffn(normed[k], normed_far[k], weights))
    came = [swap(f[3], "y") for f in fwd]
    for k in range(chunks):
        result, second, low_send, low, part = norm_two(
            k, place(k), first, fwd[k][2], came[k], cotangent, norm_params
        )
        results.append(result)
        seconds.append(second)
        lows.append(low)
        lows_far.append(swap(low_send, "y"))
        sums.append(part)
    back = [ffn_back(lows[k], lows_far[k], weights, fwd[k][0], fwd[k][1]) for k in range(chunks)]
    came = [swap(b[4], "y") for b in back]
    pairs = lambda a, b: [v for ab in zip(a, b) for v in ab]
    spread = lambda t: [back[k][t] for k in range(chunks)]
    down = ffn_grad(pos_f, pairs(lows, lows_far), spread(0), None, w_gate.shape[1])
    xs = pairs(normed, normed_far)
    if small:
        came[0], xs[0] = tie(came[0], xs[0])
    gate_grad = ffn_grad(pos_f, xs, spread(1), 0, w_gate.shape[1], down[::2])
    if small:
        came[1], xs[0] = tie(came[1], xs[0])
    up_grad = ffn_grad(pos_f, xs, spread(2), 1, w_gate.shape[1], down[1::2])
    (ak, as_), (bk, bs) = gate_grad, up_grad
    firsts, ga = [], []
    (ak, bk), (as_, bs) = fold((ak, bk), (swap(as_, "c"), swap(bs, "c")))
    for k in range(chunks):
        if small and k == chunks - 1:
            ak, bk, as_, bs, came[k] = tie(ak, bk, as_, bs, came[k])
        prior = sums if k == chunks - 1 else ()
        grad, low, part = norm_one_back(k, first, seconds[k], back[k][3], came[k], norm_params, prior)
        firsts.append(grad)
        ga.append(low)
        sums = sums + [part]
    own_sums = sums[-1]
    ga += [swap(low, "c") for low in ga]
    gh_own, gh_other, go_own, go_other, sums = out_back(
        pos_a, pos_b, ga, own_sums, flat_heads, other_heads, packs, wo_far
    )
    gh_far = swap(gh_other, "y")
    go_came = swap(go_other, "y")
    shaped = lambda a: a.reshape(heads, HD, seq_rows // 2)
    back = lambda rows, half, sums=None: attend_back(col[None], q_t, *rows, k_t, v_n, cos, sin, half, sums)
    if small:
        came = swap(as_, "0"), swap(bs, "x")
    dq0, dk, dv = back((own_kept, own_inv, own_heads, shaped(gh_own)), 0)
    if small:
        *came, dq0 = tie(*came, dq0)
        (ak, bk), (as_, bs) = fold((ak, bk), came)
        as_, bs, dk = tie(as_, bs, dk)
        ff_came = swap(as_, "x"), swap(bs, "1")
    dq0, dk, go_came, gh_far = tie(dq0, dk, go_came, gh_far)
    dq1, dk, dv = back((far_kept, far_inv, far_heads, shaped(gh_far)), 1, (dk, dv))
    groups = ((dq0, dq1, dk, dv),)
    qa, qb, qa_s, qb_s, sums = qkv_grad(pos_a, pos_b, groups, blocks, go_own, go_came, sums)
    qa_s, qb_s, dq1 = tie(qa_s, qb_s, dq1)
    if small:
        came = swap(qa_s, "0"), swap(qb_s, "x")
        *ff_came, dq1 = tie(*ff_came, dq1)
        (ak, bk), (as_, bs) = fold((ak, bk), ff_came)
        as_, bs, dq1 = tie(as_, bs, dq1)
        ff_came = swap(as_, "1"), swap(bs, "0")
    f_keep, f_send = token_terms(pos_a, pos_b, ((dq1, dk, dv),), packs, 1)
    f_came = swap(f_send, "c")
    from_far = swap((f_keep + f_came.astype(F32)).astype(BF), "y")
    n_keep, n_send = token_terms(pos_a, pos_b, ((dq0, dk, dv),), packs, 0, firsts)
    near_came = swap(n_send, "c")
    turned = lambda *arrays: tuple(x.T for x in arrays)
    ff_states = ((w_gate, m_gate, v_gate), (w_up, m_up, v_up), turned(w_down, m_down, v_down))
    pack_states = ((w_qkv, m_qkv, v_qkv), (w_out, m_out, v_out))
    norm_states = (norm_params, m_norm, v_norm)
    all_cells = float(own_rows * lax.axis_size("row") * lax.axis_size("col") * D)
    if small:
        qa, qb, qa_s, qb_s, sums = fold_sums(qa, qb, *came, sums)
        came = swap(qa_s, "x"), swap(qb_s, "0")
        *ff_came, qa_came, qb_came = tie(*ff_came, *came)
        came = qa_came, qb_came
        qa, qb, qa_s, qb_s, sums = fold_sums(qa, qb, *came, sums)
        came = swap(jnp.concatenate([qa_s, qb_s[0]], axis=0), "1")
        ff_new = updated(ffn_update_kernel, (ak, bk, *ff_came), ff_states, "ffn_update")
        *pack_new, squares = updated(
            pack_update_kernel, (qa, qb, came, sums), pack_states, "pack_update", (norm_states,)
        )
        pack_new, new_norm = pack_new[:8], pack_new[8:]
        squares = squares[0, 0]
    else:
        sums = lax.psum(own_sums, ("row", "col"))
        new_norm = adamw(norm_params, sums[:4], m_norm, v_norm, NORM_RATE, 0.0)
        squares = jnp.sum(sums[4])
        ga, gb = jnp.concatenate([ak, as_]), jnp.concatenate([bk, bs])
        own_down = ungather_plain([(ORDER_A, ga[:, BLOCK:]), (ORDER_B, gb[:, BLOCK:])])
        own_pack = ungather_plain([
            (ORDER_QA, jnp.concatenate([qa, qa_s[: ROWS // 2 * half].reshape(qa.shape)])),
            (ORDER_QB, jnp.concatenate([qb, qb_s])),
        ])
        ff_new, pack_new = [], []
        for new, grad, state, rate in (
            (ff_new, ungather_plain([(ORDER_A, ga[:, :BLOCK])]), ff_states[0], RATE_MAIN),
            (ff_new, ungather_plain([(ORDER_B, gb[:, :BLOCK])]), ff_states[1], RATE_MAIN),
            (ff_new, own_down, ff_states[2], RATE_DOWN),
            (pack_new, own_pack[:, :qkv_width], pack_states[0], RATE_MAIN),
            (pack_new, own_pack[:, OUT_AT:].T, pack_states[1], RATE_OUT),
        ):
            three = adamw(state[0], grad, state[1], state[2], rate, MATRIX_DECAY)
            new += [*three, three[0].astype(BF)]
    ff_new = [*ff_new[:8], *turned(*ff_new[8:])]
    grad_tokens = total_grad(n_keep, near_came, from_far)
    residual_rms = jnp.sqrt(squares / all_cells)
    result = jnp.concatenate(results, axis=0)
    return (result, grad_tokens, residual_rms, *pack_new, *ff_new, *new_norm)


def solution(mesh):
    tokens, wide, tall, full = P(("row", "col"), None), P("row", "col"), P("col", "row"), P()
    return jax.shard_map(
        on_device,
        mesh=mesh,
        in_specs=(tokens, tokens, P("row"), wide, tall, wide, wide, tall, full)
        + (wide, wide, tall, tall, wide, wide, wide, wide, tall, tall, full, full),
        out_specs=(tokens, tokens, full)
        + (wide,) * 4 + (tall,) * 4 + (wide,) * 8 + (tall,) * 4 + (full,) * 3,
        check_vma=False,
    )
```

```python
import functools
import math

import jax
import jax.numpy as jnp
import numpy as np
from jax import lax
from jax.experimental import pallas as pl
from jax.experimental.pallas import tpu as pltpu
from jax.sharding import PartitionSpec as P

D = 768
HD = 64
FF = 3072
SEQ = 2048
STEP = 10

FIRST_DECAY = 0.9
SECOND_DECAY = 0.999
ADAM_EPSILON = 1e-08
NORM_EPSILON = 1e-05
ROPE_BASE = 1000.0
MATRIX_DECAY = 0.01
NORM_RATE = 0.4
SCALE = 1.0 / math.sqrt(HD)
MASKED = -1e30
SAFE_SCORE = 60.0

BF = jnp.bfloat16
F32 = jnp.float32
NN = (((1,), (0,)), ((), ()))
NT = (((1,), (1,)), ((), ()))
VAUG = 80
ROWS = 8
BLOCK = D // ROWS

LINKS = {"c": ("col", 1), "y": ("col", 2), "x": ("row", 1), "0": ("row", 2), "1": ("row", 4)}
ORDER_QA, ORDER_QB = "1x0", "10x"
ORDER_A, ORDER_B = "1x0", "10x"
BACK_A, BACK_B = "1x0", "01x"
OUT_AT = 640


def mm(a, b, dims):
    return lax.dot_general(a, b, dims, preferred_element_type=F32)


def params(mib=10):
    return pltpu.CompilerParams(vmem_limit_bytes=mib << 20)


def cost(flops, nbytes, trans=0):
    return pl.CostEstimate(flops=int(flops) // 10, bytes_accessed=int(nbytes) // 10, transcendentals=int(trans))


def swap(value, step):
    axis, bit = LINKS[step]
    return lax.ppermute(value, axis, [(i, i ^ bit) for i in range(lax.axis_size(axis))])


def tie(*values):
    return lax.optimization_barrier(values)


def row_mask(order, j):
    return sum(LINKS[s][1] for k, s in enumerate(order) if (j >> k) & 1)


def doubled(held, step):
    return jnp.concatenate([held, swap(held, step)], axis=0)


RIDE = 16


def ride(sums):
    return jnp.concatenate([*split3(sums[:5]), jnp.zeros((1, D), F32)], axis=0).astype(BF)


def unride(rows):
    rows = rows.astype(F32)
    return jnp.concatenate([rows[:5] + rows[5:10] + rows[10:15], jnp.zeros((3, D), F32)], axis=0)


def fold_sums_kernel(a, b, a_came, b_came, sums, a_keep, b_keep, a_send, b_send, sums_out):
    half, rows = a_keep.shape[0], a_keep.shape[1]
    n = 2 * half
    total = sums[...] + unride(a_came[n * rows :, :D])
    sums_out[...] = total
    for j in range(n):
        ta = (a[j].astype(F32) + a_came[j * rows : (j + 1) * rows].astype(F32)).astype(BF)
        tb = (b[j].astype(F32) + b_came[j].astype(F32)).astype(BF)
        if j < half:
            a_keep[j] = ta
            b_keep[j] = tb
        else:
            a_send[(j - half) * rows : (j - half + 1) * rows, :] = ta
            b_send[j - half] = tb
    a_send[half * rows :, :D] = ride(total)
    a_send[half * rows :, D:] = jnp.zeros((RIDE, a_send.shape[1] - D), BF)


def fold_sums(a, b, a_came, b_came, sums):
    half = jax.ShapeDtypeStruct((a.shape[0] // 2,) + a.shape[1:], BF)
    send = jax.ShapeDtypeStruct((half.shape[0] * a.shape[1] + RIDE, a.shape[2]), BF)
    sums_out = jax.ShapeDtypeStruct(sums.shape, F32)
    outs = [half, half, send, half, sums_out]
    return vmem_call(fold_sums_kernel, outs, [], 2 * math.prod(a.shape), "fold_sums", (), a, b, a_came, b_came, sums)


def fold_kernel(*refs):
    n = len(refs) // 4
    for keep, came, out_keep, out_send in zip(refs[:n], refs[n : 2 * n], refs[2 * n : 3 * n], refs[3 * n :]):
        half = out_keep.shape[0]
        for j in range(2 * half):
            total = (keep[j].astype(F32) + came[j].astype(F32)).astype(BF)
            if j < half:
                out_keep[j] = total
            else:
                out_send[j - half] = total


def fold(keeps, cames):
    halves = [jax.ShapeDtypeStruct((k.shape[0] // 2,) + k.shape[1:], BF) for k in keeps]
    size = sum(math.prod(k.shape) for k in keeps)
    out = vmem_call(fold_kernel, halves * 2, [], size, "fold", (), *keeps, *cames)
    return out[: len(keeps)], out[len(keeps) :]


def gather_plain(shard, order, start, rows):
    full = lax.all_gather(shard, "row", axis=0, tiled=True)
    places = [row_mask(order, j) * BLOCK + start for j in range(ROWS)]
    return jnp.stack([full[at : at + rows] for at in places])


def ungather_plain(pieces):
    rows = []
    for r in range(ROWS):
        parts = []
        for order, blocks in pieces:
            j = [row_mask(order, i) for i in range(ROWS)].index(r)
            parts.append(blocks[j])
        rows.append(jnp.concatenate(parts, axis=0))
    return lax.psum_scatter(
        jnp.concatenate(rows, axis=0).astype(F32), "row", scatter_dimension=0, tiled=True
    )


def pack_kernel(w_qkv, w_out, w_gate, w_up, w_down, out, ffn_a, ffn_b):
    width = w_qkv.shape[1]
    gap = jnp.zeros((out.shape[0], OUT_AT - width), F32)
    out[...] = jnp.concatenate([w_qkv[...], gap, w_out[...].T], axis=1).astype(BF)
    half = BLOCK // 2
    ffn_a[:BLOCK] = w_gate[...].astype(BF)
    ffn_a[BLOCK:] = w_down[:half].astype(BF)
    ffn_b[:BLOCK] = w_up[...].astype(BF)
    ffn_b[BLOCK:] = w_down[half:].astype(BF)


def fill(dst, src, pos, start, rows, at, lanes, to, cols=slice(None), first=0):
    for j in range(src.shape[0]):
        place = pl.multiple_of(pos[first + j] * BLOCK + start, 16)
        dst[pl.ds(place, rows), to : to + lanes] = src[j, at : at + rows, cols]


def spill(src, keep, send, pos, start, rows, at, lanes, to, column=0):
    half = keep.shape[0]
    for j in range(ROWS):
        place = pl.multiple_of(pos[j] * BLOCK + start, 16)
        piece = src[pl.ds(place, rows), to : to + lanes].astype(BF)
        if j < half:
            keep[j, at : at + rows, column : column + lanes] = piece
        else:
            send[j - half, at : at + rows, column : column + lanes] = piece


def fill_qkv(w, packs, pos_a, pos_b):
    width = w.shape[1]
    for k, src in enumerate(packs):
        part, pos = k // 2, (pos_a, pos_b)[k // 2]
        fill(w, src, pos, part * BLOCK // 2, BLOCK // 2, 0, width, 0, slice(0, width), k % 2 * (ROWS // 2))


def project_kernel(col, pos_a, pos_b, lens, *refs):
    xs, packs, (cos, sin, q_t, k_t, v_t, k_n, v_n, qn, kn, w, w_t) = refs[:4], refs[4:8], refs[8:]
    heads = q_t.shape[0]
    rows = xs[0].shape[0]
    fill_qkv(w, packs, pos_a, pos_b)
    w_t[...] = w[...].T
    line = lax.broadcasted_iota(jnp.int32, (16, rows), 0)
    ones_q = jnp.where(line == 0, 1.0, 0.0).astype(BF)
    tail_v = jnp.where(line < 3, 1.0, 0.0).astype(BF)
    blank = jnp.zeros((48, rows), BF)
    for i, x in enumerate(xs):
        at = slice(i * rows, (i + 1) * rows)
        start = pl.multiple_of((i ^ col[0]) * rows, 128)
        c, s = cos[:, pl.ds(start, rows)], sin[:, pl.ds(start, rows)]
        mixed = mm(w_t[...], x[...], NT)
        position = start + lax.broadcasted_iota(jnp.int32, (16, rows), 1)
        bias = jnp.where(position < lens[0], 0.0, MASKED)
        tail_k = jnp.where(line == 0, bias, jnp.where(line < 4, 1.0, 0.0)).astype(BF)

        def turned(block):
            a, b = block[: HD // 2], block[HD // 2 :]
            return jnp.concatenate([a * c - b * s, b * c + a * s], axis=0).astype(BF)

        for h in range(heads):
            top = h * 3 * HD
            q = turned(mixed[top : top + HD]).astype(F32) * SCALE
            k = turned(mixed[top + HD : top + 2 * HD])
            v = mixed[top + 2 * HD : top + 3 * HD].astype(BF)
            kf = k.astype(F32)
            q_t[h, :, at] = jnp.concatenate([q.astype(BF), ones_q, blank], axis=0)
            k_t[h, :, at] = k
            v_t[h, :, at] = jnp.concatenate([v, ones_q], axis=0)
            k_n[h, at, :] = jnp.concatenate([k, tail_k, blank], axis=0).T
            v_n[h, at, :] = jnp.concatenate([v, tail_v, blank], axis=0).T
            qn[h, :, at] = jnp.broadcast_to(jnp.sum(q * q, axis=0, keepdims=True), (8, rows))
            kn[h, :, at] = jnp.broadcast_to(jnp.sum(kf * kf, axis=0, keepdims=True), (8, rows))


def project(col, pos_a, pos_b, lengths, xs, packs, cos, sin, width):
    t = 4 * xs[0].shape[0]
    heads = width // (3 * HD)
    made = lambda n, dt=BF: jax.ShapeDtypeStruct((heads, n, t), dt)
    natural = jax.ShapeDtypeStruct((heads, t, 128), BF)
    return vmem_call(
        project_kernel,
        [made(128), made(HD), made(VAUG), natural, natural, made(8, F32), made(8, F32)],
        [pltpu.VMEM((D, width), BF), pltpu.VMEM((width, D), BF)],
        4 * t * D * width,
        "project",
        (col, pos_a, pos_b, lengths),
        *xs, *packs, in_hbm(cos), in_hbm(sin),
        mib=14,
    )


def attend_kernel(q_t, k_n, v_t, qn, kn, out, inverse, kept, q_s):
    n = k_n.shape[1]
    chunk = min(1024, n)
    bq = q_t.shape[2]
    q_s[...] = q_t[0]

    @pl.when(jnp.max(qn[0]) * jnp.max(kn[0]) > SAFE_SCORE * SAFE_SCORE)
    def _():
        best = jnp.full((1, bq), -jnp.inf, F32)
        for i in range(n // 256):
            s = mm(k_n[0, i * 256 : (i + 1) * 256, :], q_t[0], NN)
            best = jnp.maximum(best, jnp.max(s, axis=0, keepdims=True))
        high = best.astype(BF).astype(F32)
        low = (best - high).astype(BF).astype(F32)
        line = lax.broadcasted_iota(jnp.int32, (16, bq), 0)
        tail = jnp.where(line == 0, 1.0, jnp.where(line == 1, -high, jnp.where(line == 2, -low, 0.0)))
        q_s[HD : HD + 16, :] = tail.astype(BF)

    q = q_s[...]
    total = None
    for i in range(n // chunk):
        at = slice(i * chunk, (i + 1) * chunk)
        p = jnp.exp(mm(k_n[0, at, :], q, NN)).astype(BF)
        kept[0, at, :] = p
        part = mm(v_t[0, :, at], p, NN)
        total = part if total is None else total + part
    scale = 1.0 / total[HD : HD + 1]
    out[0] = (total[:HD] * scale).astype(BF)
    inverse[0] = jnp.broadcast_to(scale, inverse.shape[1:])


def attend(q_t, k_n, v_t, qn, kn, half):
    heads, _, t = q_t.shape
    bq = t // 2
    lane = lambda rows, at=half: pl.BlockSpec((1, rows, bq), lambda h: (h, 0, at))
    return pl.pallas_call(
        attend_kernel,
        grid=(heads,),
        in_specs=[
            lane(128),
            pl.BlockSpec((1, t, 128), lambda h: (h, 0, 0)),
            pl.BlockSpec((1, VAUG, t), lambda h: (h, 0, 0)),
            lane(8),
            pl.BlockSpec((1, 8, t), lambda h: (h, 0, 0)),
        ],
        out_specs=[lane(HD, 0), lane(8, 0), pl.BlockSpec((1, t, bq), lambda h: (h, 0, 0))],
        out_shape=[
            jax.ShapeDtypeStruct((heads, HD, bq), BF),
            jax.ShapeDtypeStruct((heads, 8, bq), F32),
            pltpu.HBM((heads, t, bq), BF),
        ],
        scratch_shapes=[pltpu.VMEM((128, bq), BF)],
        compiler_params=params(24),
        cost_estimate=cost(0, 0),
        name="attend",
    )(q_t, k_n, v_t, qn, kn)


def split3(value):
    a = value.astype(BF).astype(F32)
    b = (value - a).astype(BF).astype(F32)
    return a, b, value - a - b


def turn_back(grad, c, s):
    a, b = grad[: HD // 2], grad[HD // 2 :]
    return jnp.concatenate([a * c + b * s, b * c - a * s], axis=0)


def relative(table, col, first, count):
    rows = table.shape[1] // 4
    starts = [pl.multiple_of((i ^ col[0]) * rows, 128) for i in range(first, first + count)]
    return jnp.concatenate([table[:, pl.ds(at, rows)] for at in starts], axis=1)


def attend_back_kernel(first, col, kept, inverse, q_t, o_t, do_t, k_t, v_n, cos, sin, *refs):
    if first:
        dq, dk, dv, do_s = refs
    else:
        dk_in, dv_in, dq, dk, dv, do_s, dk_s = refs
    n = v_n.shape[1]
    chunk = min(512, n)
    bq = q_t.shape[2]
    line = lax.broadcasted_iota(jnp.int32, (16, bq), 0)
    do = do_t[0].astype(F32) * inverse[0, :1]
    a, b, c = split3(-jnp.sum(do * o_t[0].astype(F32), axis=0, keepdims=True))
    tail = jnp.where(line == 0, a, jnp.where(line == 1, b, jnp.where(line == 2, c, 0.0)))
    do_s[:HD, :] = do.astype(BF)
    do_s[HD : HD + 16, :] = tail.astype(BF)
    do_s[HD + 16 :, :] = jnp.zeros((48, bq), BF)
    do = do_s[...]
    do64, q64 = do_s[:HD, :], q_t[0, :HD, :]
    total = None
    for i in range(n // chunk):
        at = slice(i * chunk, (i + 1) * chunk)
        p = kept[0, at, :]
        gs = (p.astype(F32) * mm(v_n[0, at, :], do, NN)).astype(BF)
        part = mm(k_t[0, :, at], gs, NN)
        total = part if total is None else total + part
        gv = mm(do64, p, NT)
        gk = mm(q64, gs, NT)
        if first:
            dv[0, :, at] = gv
            dk[0, :, at] = gk
        else:
            dv[0, :, at] = (gv + dv_in[0, :, at]).astype(BF)
            dk_s[:, at] = gk + dk_in[0, :, at]
    near = 0 if first else 2
    dq[0] = turn_back(total * SCALE, relative(cos, col, near, 2), relative(sin, col, near, 2)).astype(BF)
    if not first:
        dk[0] = turn_back(dk_s[...], relative(cos, col, 0, 4), relative(sin, col, 0, 4)).astype(BF)


def attend_back(col, q_t, kept, inverse, o_t, do_t, k_t, v_n, cos, sin, half, sums=None):
    heads, _, t = q_t.shape
    bq = t // 2
    first = sums is None
    lane = lambda rows, at=0: pl.BlockSpec((1, rows, bq), lambda h, *_: (h, 0, at))
    full = lambda rows: pl.BlockSpec((1, rows, t), lambda h, *_: (h, 0, 0))
    tall = lambda lanes: pl.BlockSpec((1, t, lanes), lambda h, *_: (h, 0, 0))
    table = const_spec(cos)
    made = F32 if first else BF
    more = () if first else tuple(sums)
    return pl.pallas_call(
        functools.partial(attend_back_kernel, first),
        grid_spec=pltpu.PrefetchScalarGridSpec(
            num_scalar_prefetch=1,
            grid=(heads,),
            in_specs=[tall(bq), lane(8), lane(128, half), lane(HD), lane(HD), full(HD), tall(128), table, table]
            + ([] if first else [full(HD), full(HD)]),
            out_specs=[lane(HD), full(HD), full(HD)],
            scratch_shapes=[pltpu.VMEM((128, bq), BF)]
            + ([] if first else [pltpu.VMEM((HD, t), F32)]),
        ),
        out_shape=[
            jax.ShapeDtypeStruct((heads, HD, bq), BF),
            jax.ShapeDtypeStruct((heads, HD, t), made),
            jax.ShapeDtypeStruct((heads, HD, t), made),
        ],
        compiler_params=params(28),
        cost_estimate=cost(heads * 4 * 2 * bq * t * 256, heads * t * 2048),
        name="attend_back",
    )(col, in_hbm(kept), inverse, q_t, o_t, do_t, k_t, v_n, in_hbm(cos), in_hbm(sin), *more)


def fill_out(w, packs, other, pos_a, pos_b):
    width = w.shape[2]
    half = BLOCK // 2
    for k, src in enumerate(packs):
        part, pos, first = k // 2, (pos_a, pos_b)[k // 2], k % 2 * (ROWS // 2)
        fill(w.at[0], src, pos, part * half, half, 0, width, 0, slice(OUT_AT, OUT_AT + width), first)
        fill(w.at[1], other.at[pl.ds(part * ROWS + first, ROWS // 2)], pos, part * half, half, 0, width, 0, first=first)


def out_kernel(pos_a, pos_b, h_own, h_other, wa, wa2, wb, wb2, other, keep, send, w):
    fill_out(w, (wa, wa2, wb, wb2), other, pos_a, pos_b)
    rows = keep.shape[0]
    for part, out in ((1, send), (0, keep)):
        at = slice(part * rows, (part + 1) * rows)
        total = mm(h_own[:, at].T, w[0], NT) + mm(h_other[:, at].T, w[1], NT)
        out[...] = total.astype(out.dtype)


def out_back_kernel(
    pos_a, pos_b, ga_own, ga_own2, ga_near, ga_near2, sums, h_own, h_other, wa, wa2, wb, wb2, other,
    gh_own, gh_other, keep, send, sums_out, w, ga,
):
    fill_out(w, (wa, wa2, wb, wb2), other, pos_a, pos_b)
    rows = ga_own.shape[0]
    for k, ref in enumerate((ga_own, ga_own2, ga_near, ga_near2)):
        ga[k * rows : (k + 1) * rows] = ref[:rows]
    total = sums[...] + unride(ga_near2[rows:])
    sums_out[...] = total
    send[h_own.shape[0] :, :] = ride(total)
    for half, (h, gh, g) in enumerate(((h_own, gh_own, keep), (h_other, gh_other, send))):
        gh[...] = mm(w[half].T, ga[...], NT).astype(BF)
        g[: h.shape[0], :] = mm(h[...], ga[...], NN).astype(BF)


def const_spec(a):
    return pl.BlockSpec(a.shape, lambda i, *_: (0,) * len(a.shape))


def in_hbm(x):
    return pltpu.with_memory_space_constraint(x, pltpu.HBM)


def vmem_call(kernel, out_shape, scratch, work, name, scalars, *args, mib=10, hbm_out=()):
    out_shape = [pltpu.HBM(o.shape, o.dtype) if k in hbm_out else o for k, o in enumerate(out_shape)]
    nbytes = sum(math.prod(a.shape) * a.dtype.itemsize for a in list(args) + list(out_shape))
    return pl.pallas_call(
        kernel,
        grid_spec=pltpu.PrefetchScalarGridSpec(
            num_scalar_prefetch=len(scalars),
            grid=(1,),
            in_specs=[const_spec(a) for a in args],
            out_specs=[const_spec(a) for a in out_shape],
            scratch_shapes=scratch,
        ),
        out_shape=out_shape,
        compiler_params=params(mib),
        cost_estimate=cost(work, nbytes),
        name=name,
    )(*scalars, *args)


def out_project(pos_a, pos_b, h_own, h_other, packs, other):
    rows = h_own.shape[1] // 2
    width = h_own.shape[0]
    return vmem_call(
        out_kernel,
        [jax.ShapeDtypeStruct((rows, D), F32), jax.ShapeDtypeStruct((rows, D), BF)],
        [pltpu.VMEM((2, D, width), BF)],
        2 * 2 * rows * D * 2 * width,
        "out_project",
        (pos_a, pos_b),
        h_own, h_other, *packs, other,
    )


def out_back(pos_a, pos_b, gas, sums, h_own, h_other, packs, other):
    t = 4 * gas[0].shape[0]
    width = h_own.shape[0]
    gh = jax.ShapeDtypeStruct((width, t), BF)
    grad = jax.ShapeDtypeStruct((width, D), BF)
    return vmem_call(
        out_back_kernel,
        [gh, gh, grad, jax.ShapeDtypeStruct((width + RIDE, D), BF), jax.ShapeDtypeStruct((8, D), F32)],
        [pltpu.VMEM((2, D, width), BF), pltpu.VMEM((t, D), BF)],
        2 * 2 * t * D * 2 * width,
        "out_back",
        (pos_a, pos_b),
        *gas, sums, h_own, h_other, *packs, other,
    )


FF_STEPS = 3


def assemble_kernel(pos, *refs):
    a, b, (g, u, d) = refs[:4], refs[4:8], refs[8:]
    lanes = a[0].shape[2]
    half = BLOCK // 2
    for k in range(4):
        to, first = k // 2 * lanes, k % 2 * (ROWS // 2)
        fill(g, a[k], pos.at[0], 0, BLOCK, 0, lanes, to, first=first)
        fill(u, b[k], pos.at[1], 0, BLOCK, 0, lanes, to, first=first)
        fill(d, a[k], pos.at[0], 0, half, BLOCK, lanes, to, first=first)
        fill(d, b[k], pos.at[1], half, half, BLOCK, lanes, to, first=first)


def assemble(pos, a_own, a_near, b_own, b_near):
    made = jax.ShapeDtypeStruct((D, 2 * a_own[0].shape[2]), BF)
    refs = [in_hbm(x) for x in (*a_own, *a_near, *b_own, *b_near)]
    return vmem_call(
        assemble_kernel, [made] * 3, [], 6 * D * made.shape[1], "assemble", (pos,), *refs, mib=24
    )


def place_call(kernel, pos, given, base, outs, scratch, work, name):
    in_vmem = pl.BlockSpec(memory_space=pltpu.VMEM)
    nbytes = sum(math.prod(o.shape) * 4 for o in outs)
    return list(pl.pallas_call(
        kernel,
        in_specs=[pl.BlockSpec(memory_space=pltpu.SMEM)] + [in_vmem] * (len(given) + len(base)),
        out_specs=[in_vmem] * len(outs),
        out_shape=outs,
        scratch_shapes=scratch,
        input_output_aliases={1 + len(given) + k: k for k in range(len(base))},
        compiler_params=params(),
        cost_estimate=cost(work, nbytes),
        name=name,
    )(pos, *given, *base))


def steps(units):
    width = units // FF_STEPS
    return [slice(k * width, (k + 1) * width) for k in range(FF_STEPS)]


def ffn_kernel(x_own, x_far, wg, wu, wd, gate, up, keep, send, x):
    rows = x_own.shape[0]
    x[:rows] = x_own[...]
    x[rows:] = x_far[...]
    total = None
    for at in steps(wg.shape[1]):
        g = mm(x[...], wg[:, at], NN)
        u = mm(x[...], wu[:, at], NN)
        gate[:, at] = g.astype(BF)
        up[:, at] = u.astype(BF)
        part = mm((g * jax.nn.sigmoid(g) * u).astype(BF), wd[:, at], NT)
        total = part if total is None else total + part
    keep[...] = total[:rows].astype(BF)
    send[...] = total[rows:].astype(BF)


def ffn_back_kernel(gb_own, gb_far, wg, wu, wd, gate, up, hid, ggate, gup, keep, send, gb):
    rows = gb_own.shape[0]
    gb[:rows] = gb_own[...]
    gb[rows:] = gb_far[...]
    total = None
    for at in steps(wg.shape[1]):
        gh = mm(gb[...], wd[:, at], NN)
        g, u = gate[:, at].astype(F32), up[:, at].astype(F32)
        sig = jax.nn.sigmoid(g)
        silu = g * sig
        hid[:, at] = (silu * u).astype(BF)
        gga = (gh * u * sig * (1.0 + g * (1.0 - sig))).astype(BF)
        gua = (gh * silu).astype(BF)
        ggate[:, at] = gga
        gup[:, at] = gua
        part = mm(gga, wg[:, at], NT) + mm(gua, wu[:, at], NT)
        total = part if total is None else total + part
    keep[...] = total[:rows].astype(BF)
    send[...] = total[rows:].astype(BF)


def ffn_grad_kernel(n, which, pos, *refs):
    xs, acts = refs[: 2 * n], refs[2 * n : 3 * n]
    outs, (x_t, grad) = refs[-6 if which is None else -4 : -2], refs[-2:]
    rows = xs[0].shape[0]
    for k in range(2 * n):
        x_t[:, k * rows : (k + 1) * rows] = xs[k][...].T
    lanes = outs[0].shape[2]
    half = BLOCK // 2
    wide = grad.shape[1]

    def product(right, at):
        total = None
        for k in range(n):
            part = mm(x_t[:, 2 * k * rows : 2 * (k + 1) * rows], right[k][:, at], NN)
            total = part if total is None else total + part
        grad[...] = total

    def out(src_pos, dst, start, count, to, cols):
        for j in range(ROWS):
            place = pl.multiple_of(src_pos[j] * BLOCK + start, 16)
            dst[j, to : to + count, cols] = grad[pl.ds(place, count), :].astype(BF)

    for part in range(2):
        for lo in range(0, lanes, wide):
            cols, at = slice(lo, lo + wide), slice(part * lanes + lo, part * lanes + lo + wide)
            product(acts, at)
            if which is None:
                out(pos.at[0], outs[2 * part], 0, half, BLOCK, cols)
                out(pos.at[1], outs[2 * part + 1], half, half, BLOCK, cols)
            else:
                out(pos.at[which], outs[part], 0, BLOCK, 0, cols)


def ffn_grad(pos, xs, acts, which, lanes, base=()):
    n = len(acts)
    rows = xs[0].shape[0]
    blocks = jax.ShapeDtypeStruct((ROWS, BLOCK * 3 // 2, lanes), BF)
    kernel = functools.partial(ffn_grad_kernel, n, which)
    scratch = [pltpu.VMEM((D, 2 * n * rows), BF), pltpu.VMEM((D, lanes // 3), F32)]
    work = n * rows * D * lanes
    outs = [blocks] * (4 if which is None else 2)
    return place_call(kernel, pos, list(xs) + acts, base, outs, scratch, work, "ffn_grad")


def ffn(x_own, x_far, weights):
    rows = x_own.shape[0]
    units = weights[0].shape[1]
    acts = jax.ShapeDtypeStruct((2 * rows, units), BF)
    ends = [jax.ShapeDtypeStruct((rows, D), BF)] * 2
    scratch = [pltpu.VMEM((2 * rows, D), BF)]
    work = 12 * rows * D * units
    return vmem_call(
        ffn_kernel, [acts, acts] + ends, scratch, work, "ffn", (), x_own, x_far, *weights,
        hbm_out=(0, 1),
    )


def ffn_back(gb_own, gb_far, weights, gate, up):
    rows = gb_own.shape[0]
    units = weights[0].shape[1]
    acts = jax.ShapeDtypeStruct((2 * rows, units), BF)
    ends = [jax.ShapeDtypeStruct((rows, D), BF)] * 2
    scratch = [pltpu.VMEM((2 * rows, D), BF)]
    work = 12 * rows * D * units
    return vmem_call(
        ffn_back_kernel, [acts] * 3 + ends, scratch, work, "ffn_back", (), gb_own, gb_far, *weights, in_hbm(gate), in_hbm(up),
        mib=20,
    )


def units_of(h):
    centre = jnp.mean(h, axis=1, keepdims=True)
    away = h - centre
    scale = lax.rsqrt(jnp.mean(away * away, axis=1, keepdims=True) + NORM_EPSILON)
    return away * scale, scale


def back_through(grad, unit, scale, gain):
    scaled = grad * gain
    mean = jnp.mean(scaled, axis=1, keepdims=True)
    crossed = jnp.mean(scaled * unit, axis=1, keepdims=True)
    return scale * (scaled - mean - unit * crossed)


def columns(value):
    return jnp.sum(value, axis=0, keepdims=True)


def first_kernel(tokens, keep, came, norm, first, *refs):
    h = tokens[...].astype(F32) + keep[...] + came[...].astype(F32)
    first[...] = h
    unit, _ = units_of(h)
    normed = (unit * norm[0:1] + norm[1:2]).astype(BF)
    rows = refs[0].shape[0]
    for k, low in enumerate(refs):
        k = k % (len(refs) // 2)
        low[...] = normed[k * rows : (k + 1) * rows]


def norm_one(tokens, keep, came, norm, chunks):
    rows = tokens.shape[0]
    return vmem_call(
        first_kernel,
        [jax.ShapeDtypeStruct((rows, D), F32)] + [jax.ShapeDtypeStruct((rows // chunks, D), BF)] * 2 * chunks,
        [], 12 * rows * D, "first_norm", (), tokens, keep, came, norm, hbm_out=[0, *range(1 + chunks, 1 + 2 * chunks)],
    )


def second_kernel(place, first, cotangent, keep, came, norm, result, low, low_too, sums):
    rows = result.shape[0]
    i = pl.program_id(0)
    unit, _ = units_of(first[...])
    normed = unit * norm[0:1] + norm[1:2]
    unit, scale = units_of(normed + keep[...].astype(F32) + came[...].astype(F32))
    out = unit * norm[2:3] + norm[3:4]
    result[...] = out.astype(BF)
    position = place[0] + i * rows + lax.broadcasted_iota(jnp.int32, (rows, 1), 0)
    weight = (position < place[1]).astype(F32)
    g = cotangent[...].astype(F32) * weight
    back = back_through(g, unit, scale, norm[2:3]).astype(BF)
    low[...] = back
    low_too[...] = back
    part = jnp.concatenate(
        [jnp.zeros((2, D), F32), columns(g * unit), columns(g), columns(out * out * weight), jnp.zeros((3, D), F32)],
        axis=0,
    )

    @pl.when(i == 0)
    def _():
        sums[...] = part

    @pl.when(i > 0)
    def _():
        sums[...] += part


def norm_two(k, place, first, keep, came, cotangent, norm):
    rows = keep.shape[0]
    n = 2
    part = lambda at: pl.BlockSpec((rows // n, D), lambda i, *_: (at * n + i, 0))
    sums = jax.ShapeDtypeStruct((8, D), F32)
    return pl.pallas_call(
        second_kernel,
        grid_spec=pltpu.PrefetchScalarGridSpec(
            num_scalar_prefetch=1,
            grid=(n,),
            in_specs=[part(k), part(k), part(0), part(0), const_spec(norm)],
            out_specs=[part(0)] * 3 + [const_spec(sums)],
        ),
        out_shape=[pltpu.HBM((rows, D), BF), jax.ShapeDtypeStruct((rows, D), BF), pltpu.HBM((rows, D), BF), sums],
        compiler_params=params(),
        cost_estimate=cost(30 * rows * D, 12 * rows * D),
        name="second_norm",
    )(place, in_hbm(first), in_hbm(cotangent), keep, came, norm)


def chunk_call(kernel, k, chunked, whole, out_shape, name, work):
    rows = out_shape[0].shape[0]
    part = pl.BlockSpec((rows, D), lambda i: (k, 0))
    return pl.pallas_call(
        kernel,
        grid=(1,),
        in_specs=[part] * len(chunked) + [const_spec(a) for a in whole],
        out_specs=[const_spec(a) for a in out_shape],
        out_shape=out_shape,
        compiler_params=params(),
        cost_estimate=cost(work, 20 * rows * D),
        name=name,
    )(*chunked, *whole)


def first_back_kernel(n, first, second, keep, came, norm, *refs):
    prior, (grad, low, sums) = refs[:n], refs[n:]
    rows = grad.shape[0]
    unit, scale = units_of(first[...])
    g = second[...].astype(F32) + keep[...].astype(F32) + came[...].astype(F32)
    back = back_through(g, unit, scale, norm[0:1])
    grad[...] = back
    low[:rows] = back.astype(BF)
    total = jnp.concatenate([columns(g * unit), columns(g), jnp.zeros((6, D), F32)], axis=0)
    for ref in prior:
        total = total + ref[...]
    sums[...] = total
    if n:
        low[rows:] = ride(total)


def norm_one_back(k, first, second, keep, came, norm, prior=()):
    rows = keep.shape[0]
    more = RIDE if prior else 0
    outs = [
        jax.ShapeDtypeStruct((rows, D), F32),
        jax.ShapeDtypeStruct((rows + more, D), BF),
        jax.ShapeDtypeStruct((8, D), F32),
    ]
    return chunk_call(
        functools.partial(first_back_kernel, len(prior)), k, (first,), (second, keep, came, norm, *prior),
        outs, "first_norm_back", 20 * rows * D,
    )


def token_kernel(n, pos_a, pos_b, *refs):
    groups, refs = [refs[3 * k : 3 * k + 3] for k in range(n)], refs[3 * n :]
    packs, base, (near, far, w) = refs[:4], refs[4:-3], refs[-3:]
    fill_qkv(w, packs, pos_a, pos_b)
    rows = near.shape[0]
    for part, out in ((1, far), (0, near)):
        at = slice(part * rows, (part + 1) * rows)
        mixed = [ref[h, :, at] for group in groups for h in range(group[0].shape[0]) for ref in group]
        total = mm(jnp.concatenate(mixed, axis=0).T, w[...], NT)
        if part == 0 and base:
            total = total + jnp.concatenate([ref[...] for ref in base], axis=0)
        out[...] = total.astype(out.dtype)


def token_terms(pos_a, pos_b, groups, packs, half, base=()):
    bq = groups[0][0].shape[2]
    width = sum(g[0].shape[0] for g in groups) * 3 * HD
    lane = lambda a, at: pl.BlockSpec((a.shape[0], HD, bq), lambda i, *_: (0, 0, at))
    flat = [a for g in groups for a in g]
    out = [jax.ShapeDtypeStruct((bq // 2, D), kind) for kind in (F32, BF)]
    return pl.pallas_call(
        functools.partial(token_kernel, len(groups)),
        grid_spec=pltpu.PrefetchScalarGridSpec(
            num_scalar_prefetch=2,
            grid=(1,),
            in_specs=[lane(a, half if k % 3 else 0) for k, a in enumerate(flat)]
            + [const_spec(a) for a in (*packs, *base)],
            out_specs=[const_spec(a) for a in out],
            scratch_shapes=[pltpu.VMEM((D, width), BF)],
        ),
        out_shape=out,
        compiler_params=params(),
        cost_estimate=cost(2 * bq * D * width, bq * (D + width) * 4),
        name="token_terms",
    )(pos_a, pos_b, *flat, *packs, *base)


def total_kernel(keep, near, far, out):
    out[...] = keep[...] + near[...].astype(F32) + far[...].astype(F32)


def total_grad(keep, near, far):
    rows = keep.shape[0]
    part = pl.BlockSpec((rows // 4, D), lambda i: (i, 0))
    return pl.pallas_call(
        total_kernel,
        grid=(4,),
        in_specs=[part] * 3,
        out_specs=part,
        out_shape=jax.ShapeDtypeStruct((rows, D), F32),
        compiler_params=params(),
        cost_estimate=cost(2 * rows * D, 12 * rows * D),
        name="total_grad",
    )(keep, near, far)


def qkv_grad_kernel(n, pos_a, pos_b, *refs):
    groups, refs = [refs[4 * k : 4 * k + 4] for k in range(n)], refs[4 * n :]
    x0, x1, x2, x3, out_own, out_came, sums, a_k, b_k, a_s, b_s, sums_out, g, go = refs
    rows = x0.shape[0]
    total = None
    for k, x in enumerate((x0, x1, x2, x3)):
        at, to = slice(k * rows, (k + 1) * rows), slice(k % 2 * rows, (k % 2 + 1) * rows)
        mixed = []
        for *dqs, dk, dv in groups:
            for h in range(dk.shape[0]):
                mixed += [dqs[k // 2][h, :, to], dk[h, :, at], dv[h, :, at]]
        part = mm(jnp.concatenate(mixed, axis=0), x[...], NN)
        total = part if total is None else total + part
    g[...] = total.T
    half = BLOCK // 2
    width, out_width = g.shape[1], go.shape[1]
    go[...] = (out_own[...].astype(F32) + out_came[:out_width].astype(F32)).T
    total = sums[...] + unride(out_came[out_width:])
    sums_out[...] = total
    gap = jnp.zeros((half, OUT_AT - width), BF)
    for part, (pos, k, s) in enumerate(((pos_a, a_k, a_s), (pos_b, b_k, b_s))):
        for j in range(ROWS):
            at = pl.ds(pl.multiple_of(pos[j] * BLOCK + part * half, 16), half)
            piece = jnp.concatenate([g[at, :].astype(BF), gap, go[at, :].astype(BF)], axis=1)
            if j < ROWS // 2:
                k[j] = piece
            elif part:
                s[j - ROWS // 2] = piece
            else:
                s[(j - ROWS // 2) * half : (j - ROWS // 2 + 1) * half, :] = piece
    a_s[ROWS // 2 * half :, :D] = ride(total)
    a_s[ROWS // 2 * half :, D:] = jnp.zeros((RIDE, a_s.shape[1] - D), BF)


def qkv_grad(pos_a, pos_b, groups, xs, out_own, out_came, sums):
    out_width = out_own.shape[0]
    blocks = jax.ShapeDtypeStruct((ROWS // 2, BLOCK // 2, OUT_AT + out_width), BF)
    send = jax.ShapeDtypeStruct((ROWS // 2 * (BLOCK // 2) + RIDE, OUT_AT + out_width), BF)
    width = 3 * HD * sum(g[0].shape[0] for g in groups)
    return vmem_call(
        functools.partial(qkv_grad_kernel, len(groups)),
        [blocks, blocks, send, blocks, jax.ShapeDtypeStruct((8, D), F32)],
        [pltpu.VMEM((D, width), F32), pltpu.VMEM((D, out_width), F32)],
        8 * xs[0].shape[0] * D * width,
        "qkv_grad",
        (pos_a, pos_b),
        *[a for g in groups for a in g], *xs, out_own, out_came, sums,
    )


def adamw(weight, gradient, first_state, second_state, step_rate, decay_rate):
    first_new = FIRST_DECAY * first_state + (1.0 - FIRST_DECAY) * gradient
    second_new = SECOND_DECAY * second_state + (1.0 - SECOND_DECAY) * gradient * gradient
    first_hat = first_new / (1.0 - FIRST_DECAY**STEP)
    second_hat = second_new / (1.0 - SECOND_DECAY**STEP)
    weight_new = weight - step_rate * (
        first_hat / (jnp.sqrt(second_hat) + ADAM_EPSILON) + decay_rate * weight
    )
    return (weight_new, first_new, second_new)


RATE_MAIN = 2.0 / math.sqrt(D)
RATE_OUT = 2.0 / math.sqrt(D * 16 // SEQ)
RATE_DOWN = 2.0 / math.sqrt(FF)


def update(grad, states, outs, rate):
    w, m, v = (ref[...] for ref in states)
    new, first, second = adamw(w, grad, m, v, rate, MATRIX_DECAY)
    for ref, value in zip(outs, (new, first, second, new.astype(BF))):
        ref[...] = value


def ffn_update_kernel(a, b, a_came, b_came, *refs):
    states, outs = refs[:9], refs[9:]
    ga = a[0].astype(F32) + a_came[0].astype(F32)
    gb = b[0].astype(F32) + b_came[0].astype(F32)
    rows = states[0].shape[0]
    update(ga[:rows], states[:3], outs[:4], RATE_MAIN)
    update(gb[:rows], states[3:6], outs[4:8], RATE_MAIN)
    update(jnp.concatenate([ga[rows:], gb[rows:]], axis=0), states[6:], outs[8:], RATE_DOWN)


def pack_update_kernel(a, b, came, sums, *refs):
    states, outs = refs[:9], refs[9:]
    rows = a.shape[1]
    ga = a[0].astype(F32) + came[:rows].astype(F32)
    gb = b[0].astype(F32) + came[rows + RIDE :].astype(F32)
    grad = jnp.concatenate([ga, gb], axis=0)
    width = states[0].shape[1]
    update(grad[:, :width], states[:3], outs[:4], RATE_MAIN)
    update(grad[:, OUT_AT:].T, states[3:6], outs[4:8], RATE_OUT)
    total = sums[...] + unride(came[rows : rows + RIDE, :D])
    w, m, v = (ref[...] for ref in states[6:])
    for ref, value in zip(outs[8:], adamw(w, total[:4], m, v, NORM_RATE, 0.0)):
        ref[...] = value
    outs[11][...] = jnp.broadcast_to(jnp.sum(total[4:5], axis=1, keepdims=True), outs[11].shape)


def updated(kernel, given, states, name, more=()):
    outs = []
    for w, _, _ in states:
        outs += [pltpu.HBM(w.shape, F32)] * 3 + [pltpu.HBM(w.shape, BF)]
    flat = [in_hbm(x) for state in states for x in state]
    work = sum(20 * math.prod(w.shape) for w, _, _ in states)
    rest = [x for state in more for x in state]
    for w, _, _ in more:
        outs += [jax.ShapeDtypeStruct(w.shape, F32)] * 3 + [jax.ShapeDtypeStruct((8, 128), F32)]
    return vmem_call(kernel, outs, [], work, name, (), *given, *flat, *rest)


def rope_tables(length):
    position = np.arange(length, dtype=np.float32)
    inverse = np.exp(np.arange(HD // 2, dtype=np.float32) * np.float32(-2.0 * math.log(ROPE_BASE) / HD))
    angle = (inverse.astype(np.float32)[:, None] * position[None, :]).astype(np.float64)
    return np.cos(angle).astype(np.float32), np.sin(angle).astype(np.float32)


def on_device(
    tokens, cotangent, lengths, w_qkv, w_out, w_gate, w_up, w_down, norm_params,
    m_qkv, v_qkv, m_out, v_out, m_gate, v_gate, m_up, v_up, m_down, v_down, m_norm, v_norm,
):
    own_rows = tokens.shape[0]
    seq_rows = own_rows * lax.axis_size("col")
    col = lax.axis_index("col").astype(jnp.int32)
    row = lax.axis_index("row").astype(jnp.int32)
    small = lax.axis_size("row") == ROWS
    me = row if small else row * 0
    qkv_width = w_qkv.shape[1]
    head_width = qkv_width // 3
    heads = head_width // HD
    half = BLOCK // 2
    chunks = 2

    places = lambda order: jnp.stack([me ^ row_mask(order, j) for j in range(ROWS)])
    pos_a, pos_b = places(ORDER_QA), places(ORDER_QB)
    pos_f = jnp.stack([places(ORDER_A), places(ORDER_B)])
    pos_r = jnp.stack([places(BACK_A), places(BACK_B)])

    near = swap(tokens, "c")
    far = swap(tokens, "y")
    if small:
        part = (BLOCK + half, w_gate.shape[1])
        shapes = [jax.ShapeDtypeStruct(n, BF) for n in ((BLOCK, OUT_AT + head_width), part, part)]
        given = [in_hbm(w) for w in (w_qkv, w_out, w_gate, w_up, w_down.T)]
        pack, fa, fb = vmem_call(pack_kernel, shapes, [], 0, "pack", (), *given)
        pack, fa, fb = pack[None], fa[None], fb[None]
        pack_came, fa, fb = tie(swap(pack, "1"), fa, fb)
        ff_came = swap(fa, "1"), swap(fb, "1")
        both = jnp.concatenate([pack, pack_came], axis=0)
        qa, qb = both[:, :half], both[:, half:]
        came = swap(qa, "x"), swap(qb, "0")
        qa_came, qb_came, near, far = tie(*came, near, far)
        qa, qb = jnp.concatenate([qa, qa_came], axis=0), jnp.concatenate([qb, qb_came], axis=0)
        came = swap(qa, "0"), swap(qb, "x")
        fa, fb = jnp.concatenate([fa, ff_came[0]], axis=0), jnp.concatenate([fb, ff_came[1]], axis=0)
        fa, fb, *came = tie(fa, fb, *came)
        packs = (qa, came[0], qb, came[1])
        ff_came = swap(fa, "x"), swap(fb, "0")
    else:
        gap = jnp.zeros((w_qkv.shape[0], OUT_AT - qkv_width), BF)
        pack = jnp.concatenate([w_qkv.astype(BF), gap, w_out.T.astype(BF)], axis=1)
        low_down = w_down.T.astype(BF)
        low_gate, low_up = w_gate.astype(BF), w_up.astype(BF)
        wa = gather_plain(pack, ORDER_QA, 0, half)
        wb = gather_plain(pack, ORDER_QB, half, half)
        packs = (wa[: ROWS // 2], wa[ROWS // 2 :], wb[: ROWS // 2], wb[ROWS // 2 :])
        join = lambda w, order, start: jnp.concatenate(
            [gather_plain(w, order, 0, BLOCK), gather_plain(low_down, order, start, half)], axis=1
        )
        fa, fb = join(low_gate, ORDER_A, 0), join(low_up, ORDER_B, half)
        fa, fb, fa2, fb2 = fa[: ROWS // 2], fb[: ROWS // 2], fa[ROWS // 2 :], fb[ROWS // 2 :]
    far_near = swap(far, "c")
    blocks = (tokens, near, far, far_near)

    cos_np, sin_np = rope_tables(seq_rows)
    cos, sin = jnp.asarray(cos_np), jnp.asarray(sin_np)
    q_t, k_t, v_t, k_n, v_n, qn, kn = project(
        col[None], pos_a, pos_b, lengths, blocks, packs, cos, sin, qkv_width
    )
    wo_far = swap(jnp.concatenate([p[:, :, OUT_AT:] for p in packs], axis=0), "y")
    if small:
        fa_came, fb_came, q_t = tie(*ff_came, q_t)
        fa, fb = jnp.concatenate([fa, fa_came], axis=0), jnp.concatenate([fb, fb_came], axis=0)
        fa, fb, q_t = tie(fa, fb, q_t)
        fa2, fb2 = swap(fa, "0"), swap(fb, "x")
    far_heads, far_inv, far_kept = attend(q_t, k_n, v_t, qn, kn, 1)
    if small:
        far_heads, q_t = tie(far_heads, q_t)
    fa_c, fb_c = swap(fa, "c"), swap(fb, "c")
    if small:
        far_heads, wo_far = tie(far_heads, wo_far)
    other_heads = swap(far_heads.reshape(head_width, seq_rows // 2), "y")
    own_heads, own_inv, own_kept = attend(q_t, k_n, v_t, qn, kn, 0)
    flat_heads = own_heads.reshape(head_width, seq_rows // 2)
    if small:
        flat_heads, other_heads, fa2, fb2 = tie(flat_heads, other_heads, fa2, fb2)

    keep, send = out_project(pos_a, pos_b, flat_heads, other_heads, packs, wo_far)
    first, *normed = norm_one(tokens, keep, swap(send, "c"), norm_params, chunks)
    fa2_c, fb2_c = swap(fa2, "c"), swap(fb2, "c")
    weights = assemble(pos_f, (fa, fa2), (fa_c, fa2_c), (fb, fb2), (fb_c, fb2_c))
    weights = list(weights)
    normed_far = [swap(normed[0], "y")]
    for k in range(1, chunks):
        normed_far[-1], normed[k], weights[0] = tie(normed_far[-1], normed[k], weights[0])
        normed_far.append(swap(normed[k], "y"))
    normed = normed[chunks:]
    place = lambda k: jnp.stack([col * own_rows + k * (own_rows // chunks), lengths[0]])
    fwd, sums, results, lows, lows_far = [], [], [], [], []
    for k in range(chunks):
        fwd.append(ffn(normed[k], normed_far[k], weights))
    came = [swap(f[3], "y") for f in fwd]
    for k in range(chunks):
        result, low_send, low, part = norm_two(
            k, place(k), first, fwd[k][2], came[k], cotangent, norm_params
        )
        results.append(result)
        lows.append(low)
        lows_far.append(swap(low_send, "y"))
        sums.append(part)
    back = [ffn_back(lows[k], lows_far[k], weights, fwd[k][0], fwd[k][1]) for k in range(chunks)]
    came = [swap(b[4], "y") for b in back]
    pairs = lambda a, b: [v for ab in zip(a, b) for v in ab]
    spread = lambda t: [back[k][t] for k in range(chunks)]
    down = ffn_grad(pos_r, pairs(lows, lows_far), spread(0), None, w_gate.shape[1])
    xs = pairs(normed, normed_far)
    if small:
        came[0], xs[0] = tie(came[0], xs[0])
    gate_grad = ffn_grad(pos_r, xs, spread(1), 0, w_gate.shape[1], down[::2])
    if small:
        came[1], xs[0] = tie(came[1], xs[0])
    up_grad = ffn_grad(pos_r, xs, spread(2), 1, w_gate.shape[1], down[1::2])
    (ak, as_), (bk, bs) = gate_grad, up_grad
    firsts, ga = [], []
    (ak, bk), (as_, bs) = fold((ak, bk), (swap(as_, "c"), swap(bs, "c")))
    for k in range(chunks):
        if small and k == chunks - 1:
            ak, bk, as_, bs, came[k] = tie(ak, bk, as_, bs, came[k])
        prior = sums if k == chunks - 1 else ()
        grad, low, part = norm_one_back(k, first, lows[k], back[k][3], came[k], norm_params, prior)
        firsts.append(grad)
        ga.append(low)
        sums = sums + [part]
    own_sums = sums[-1]
    ga += [swap(low, "c") for low in ga]
    gh_own, gh_other, go_own, go_other, sums = out_back(
        pos_a, pos_b, ga, own_sums, flat_heads, other_heads, packs, wo_far
    )
    gh_far = swap(gh_other, "y")
    go_came = swap(go_other, "y")
    shaped = lambda a: a.reshape(heads, HD, seq_rows // 2)
    back = lambda rows, half, sums=None: attend_back(col[None], q_t, *rows, k_t, v_n, cos, sin, half, sums)
    if small:
        came = swap(as_, "0"), swap(bs, "x")
    dq0, dk, dv = back((own_kept, own_inv, own_heads, shaped(gh_own)), 0)
    if small:
        *came, dq0 = tie(*came, dq0)
        (ak, bk), (as_, bs) = fold((ak, bk), came)
        as_, bs, dk = tie(as_, bs, dk)
        ff_came = swap(as_, "x"), swap(bs, "1")
    dq0, dk, go_came, gh_far = tie(dq0, dk, go_came, gh_far)
    dq1, dk, dv = back((far_kept, far_inv, far_heads, shaped(gh_far)), 1, (dk, dv))
    groups = ((dq0, dq1, dk, dv),)
    qa, qb, qa_s, qb_s, sums = qkv_grad(pos_a, pos_b, groups, blocks, go_own, go_came, sums)
    qa_s, qb_s, dq1 = tie(qa_s, qb_s, dq1)
    if small:
        came = swap(qa_s, "0"), swap(qb_s, "x")
        *ff_came, dq1 = tie(*ff_came, dq1)
        (ak, bk), (as_, bs) = fold((ak, bk), ff_came)
        as_, bs, dq1 = tie(as_, bs, dq1)
        ff_came = swap(as_, "1"), swap(bs, "0")
    f_keep, f_send = token_terms(pos_a, pos_b, ((dq1, dk, dv),), packs, 1)
    f_came = swap(f_send, "c")
    from_far = swap((f_keep + f_came.astype(F32)).astype(BF), "y")
    n_keep, n_send = token_terms(pos_a, pos_b, ((dq0, dk, dv),), packs, 0, firsts)
    near_came = swap(n_send, "c")
    turned = lambda *arrays: tuple(x.T for x in arrays)
    ff_states = ((w_gate, m_gate, v_gate), (w_up, m_up, v_up), turned(w_down, m_down, v_down))
    pack_states = ((w_qkv, m_qkv, v_qkv), (w_out, m_out, v_out))
    norm_states = (norm_params, m_norm, v_norm)
    all_cells = float(own_rows * lax.axis_size("row") * lax.axis_size("col") * D)
    if small:
        qa, qb, qa_s, qb_s, sums = fold_sums(qa, qb, *came, sums)
        came = swap(qa_s, "x"), swap(qb_s, "0")
        qa, qb, qa_s, qb_s, sums = fold_sums(qa, qb, *came, sums)
        came = swap(jnp.concatenate([qa_s, qb_s[0]], axis=0), "1")
        ff_new = updated(ffn_update_kernel, (ak, bk, *ff_came), ff_states, "ffn_update")
        grad_tokens = total_grad(n_keep, near_came, from_far)
        came, grad_tokens = tie(came, grad_tokens)
        *pack_new, squares = updated(
            pack_update_kernel, (qa, qb, came, sums), pack_states, "pack_update", (norm_states,)
        )
        pack_new, new_norm = pack_new[:8], pack_new[8:]
        squares = squares[0, 0]
    else:
        sums = lax.psum(own_sums, ("row", "col"))
        new_norm = adamw(norm_params, sums[:4], m_norm, v_norm, NORM_RATE, 0.0)
        squares = jnp.sum(sums[4])
        ga, gb = jnp.concatenate([ak, as_]), jnp.concatenate([bk, bs])
        own_down = ungather_plain([(BACK_A, ga[:, BLOCK:]), (BACK_B, gb[:, BLOCK:])])
        own_pack = ungather_plain([
            (ORDER_QA, jnp.concatenate([qa, qa_s[: ROWS // 2 * half].reshape(qa.shape)])),
            (ORDER_QB, jnp.concatenate([qb, qb_s])),
        ])
        ff_new, pack_new = [], []
        for new, grad, state, rate in (
            (ff_new, ungather_plain([(BACK_A, ga[:, :BLOCK])]), ff_states[0], RATE_MAIN),
            (ff_new, ungather_plain([(BACK_B, gb[:, :BLOCK])]), ff_states[1], RATE_MAIN),
            (ff_new, own_down, ff_states[2], RATE_DOWN),
            (pack_new, own_pack[:, :qkv_width], pack_states[0], RATE_MAIN),
            (pack_new, own_pack[:, OUT_AT:].T, pack_states[1], RATE_OUT),
        ):
            three = adamw(state[0], grad, state[1], state[2], rate, MATRIX_DECAY)
            new += [*three, three[0].astype(BF)]
    ff_new = [*ff_new[:8], *turned(*ff_new[8:])]
    if not small:
        grad_tokens = total_grad(n_keep, near_came, from_far)
    residual_rms = jnp.sqrt(squares / all_cells)
    result = jnp.concatenate(results, axis=0)
    return (result, grad_tokens, residual_rms, *pack_new, *ff_new, *new_norm)


def solution(mesh):
    tokens, wide, tall, full = P(("row", "col"), None), P("row", "col"), P("col", "row"), P()
    return jax.shard_map(
        on_device,
        mesh=mesh,
        in_specs=(tokens, tokens, P("row"), wide, tall, wide, wide, tall, full)
        + (wide, wide, tall, tall, wide, wide, wide, wide, tall, tall, full, full),
        out_specs=(tokens, tokens, full)
        + (wide,) * 4 + (tall,) * 4 + (wide,) * 8 + (tall,) * 4 + (full,) * 3,
        check_vma=False,
    )
```

```python
import functools
import math

import jax
import jax.numpy as jnp
import numpy as np
from jax import lax
from jax.experimental import pallas as pl
from jax.experimental.pallas import tpu as pltpu
from jax.sharding import PartitionSpec as P

D = 768
HD = 64
FF = 3072
SEQ = 2048
STEP = 10

FIRST_DECAY = 0.9
SECOND_DECAY = 0.999
ADAM_EPSILON = 1e-08
NORM_EPSILON = 1e-05
ROPE_BASE = 1000.0
MATRIX_DECAY = 0.01
NORM_RATE = 0.4
SCALE = 1.0 / math.sqrt(HD)
MASKED = -1e30
SAFE_SCORE = 60.0

BF = jnp.bfloat16
F32 = jnp.float32
NN = (((1,), (0,)), ((), ()))
NT = (((1,), (1,)), ((), ()))
VAUG = 80
ROWS = 8
BLOCK = D // ROWS

LINKS = {"c": ("col", 1), "y": ("col", 2), "x": ("row", 1), "0": ("row", 2), "1": ("row", 4)}
ORDER_QA, ORDER_QB = "1x0", "10x"
ORDER_A, ORDER_B = "1x0", "10x"
BACK_A, BACK_B = "1x0", "01x"
OUT_AT = 640


def mm(a, b, dims):
    return lax.dot_general(a, b, dims, preferred_element_type=F32)


def params(mib=10):
    return pltpu.CompilerParams(vmem_limit_bytes=mib << 20)


def cost(flops, nbytes, trans=0):
    return pl.CostEstimate(flops=int(flops) // 10, bytes_accessed=int(nbytes) // 10, transcendentals=int(trans))


def swap(value, step):
    axis, bit = LINKS[step]
    return lax.ppermute(value, axis, [(i, i ^ bit) for i in range(lax.axis_size(axis))])


def tie(*values):
    return lax.optimization_barrier(values)


def row_mask(order, j):
    return sum(LINKS[s][1] for k, s in enumerate(order) if (j >> k) & 1)


def doubled(held, step):
    return jnp.concatenate([held, swap(held, step)], axis=0)


RIDE = 16


def ride(sums):
    return jnp.concatenate([*split3(sums[:5]), jnp.zeros((1, D), F32)], axis=0).astype(BF)


def unride(rows):
    rows = rows.astype(F32)
    return jnp.concatenate([rows[:5] + rows[5:10] + rows[10:15], jnp.zeros((3, D), F32)], axis=0)


def fold_sums_kernel(a, b, a_came, b_came, sums, a_keep, b_keep, a_send, b_send, sums_out):
    half, rows = a_keep.shape[0], a_keep.shape[1]
    n = 2 * half
    total = sums[...] + unride(a_came[n * rows :, :D])
    sums_out[...] = total
    for j in range(n):
        ta = (a[j].astype(F32) + a_came[j * rows : (j + 1) * rows].astype(F32)).astype(BF)
        tb = (b[j].astype(F32) + b_came[j].astype(F32)).astype(BF)
        if j < half:
            a_keep[j] = ta
            b_keep[j] = tb
        else:
            a_send[(j - half) * rows : (j - half + 1) * rows, :] = ta
            b_send[j - half] = tb
    a_send[half * rows :, :D] = ride(total)
    a_send[half * rows :, D:] = jnp.zeros((RIDE, a_send.shape[1] - D), BF)


def fold_sums(a, b, a_came, b_came, sums):
    half = jax.ShapeDtypeStruct((a.shape[0] // 2,) + a.shape[1:], BF)
    send = jax.ShapeDtypeStruct((half.shape[0] * a.shape[1] + RIDE, a.shape[2]), BF)
    sums_out = jax.ShapeDtypeStruct(sums.shape, F32)
    outs = [half, half, send, half, sums_out]
    return vmem_call(fold_sums_kernel, outs, [], 2 * math.prod(a.shape), "fold_sums", (), a, b, a_came, b_came, sums)


def fold_kernel(*refs):
    n = len(refs) // 4
    for keep, came, out_keep, out_send in zip(refs[:n], refs[n : 2 * n], refs[2 * n : 3 * n], refs[3 * n :]):
        half = out_keep.shape[0]
        for j in range(2 * half):
            total = (keep[j].astype(F32) + came[j].astype(F32)).astype(BF)
            if j < half:
                out_keep[j] = total
            else:
                out_send[j - half] = total


def fold(keeps, cames):
    halves = [jax.ShapeDtypeStruct((k.shape[0] // 2,) + k.shape[1:], BF) for k in keeps]
    size = sum(math.prod(k.shape) for k in keeps)
    out = vmem_call(fold_kernel, halves * 2, [], size, "fold", (), *keeps, *cames)
    return out[: len(keeps)], out[len(keeps) :]


def gather_plain(shard, order, start, rows):
    full = lax.all_gather(shard, "row", axis=0, tiled=True)
    places = [row_mask(order, j) * BLOCK + start for j in range(ROWS)]
    return jnp.stack([full[at : at + rows] for at in places])


def ungather_plain(pieces):
    rows = []
    for r in range(ROWS):
        parts = []
        for order, blocks in pieces:
            j = [row_mask(order, i) for i in range(ROWS)].index(r)
            parts.append(blocks[j])
        rows.append(jnp.concatenate(parts, axis=0))
    return lax.psum_scatter(
        jnp.concatenate(rows, axis=0).astype(F32), "row", scatter_dimension=0, tiled=True
    )


def pack_kernel(w_qkv, w_out, w_gate, w_up, w_down, out, ffn_a, ffn_b):
    width = w_qkv.shape[1]
    gap = jnp.zeros((out.shape[0], OUT_AT - width), F32)
    out[...] = jnp.concatenate([w_qkv[...], gap, w_out[...].T], axis=1).astype(BF)
    half = BLOCK // 2
    ffn_a[:BLOCK] = w_gate[...].astype(BF)
    ffn_a[BLOCK:] = w_down[:half].astype(BF)
    ffn_b[:BLOCK] = w_up[...].astype(BF)
    ffn_b[BLOCK:] = w_down[half:].astype(BF)


def fill(dst, src, pos, start, rows, at, lanes, to, cols=slice(None), first=0):
    for j in range(src.shape[0]):
        place = pl.multiple_of(pos[first + j] * BLOCK + start, 16)
        dst[pl.ds(place, rows), to : to + lanes] = src[j, at : at + rows, cols]


def spill(src, keep, send, pos, start, rows, at, lanes, to, column=0):
    half = keep.shape[0]
    for j in range(ROWS):
        place = pl.multiple_of(pos[j] * BLOCK + start, 16)
        piece = src[pl.ds(place, rows), to : to + lanes].astype(BF)
        if j < half:
            keep[j, at : at + rows, column : column + lanes] = piece
        else:
            send[j - half, at : at + rows, column : column + lanes] = piece


def fill_qkv(w, packs, pos_a, pos_b):
    width = w.shape[1]
    for k, src in enumerate(packs):
        part, pos = k // 2, (pos_a, pos_b)[k // 2]
        fill(w, src, pos, part * BLOCK // 2, BLOCK // 2, 0, width, 0, slice(0, width), k % 2 * (ROWS // 2))


def project_kernel(col, pos_a, pos_b, lens, *refs):
    xs, packs, (cos, sin, q_t, k_t, v_t, k_n, v_n, qn, kn, w, w_t) = refs[:4], refs[4:8], refs[8:]
    heads = q_t.shape[0]
    rows = xs[0].shape[0]
    fill_qkv(w, packs, pos_a, pos_b)
    w_t[...] = w[...].T
    line = lax.broadcasted_iota(jnp.int32, (16, rows), 0)
    ones_q = jnp.where(line == 0, 1.0, 0.0).astype(BF)
    tail_v = jnp.where(line < 3, 1.0, 0.0).astype(BF)
    blank = jnp.zeros((48, rows), BF)
    for i, x in enumerate(xs):
        at = slice(i * rows, (i + 1) * rows)
        start = pl.multiple_of((i ^ col[0]) * rows, 128)
        c, s = cos[:, pl.ds(start, rows)], sin[:, pl.ds(start, rows)]
        mixed = mm(w_t[...], x[...], NT)
        position = start + lax.broadcasted_iota(jnp.int32, (16, rows), 1)
        bias = jnp.where(position < lens[0], 0.0, MASKED)
        tail_k = jnp.where(line == 0, bias, jnp.where(line < 4, 1.0, 0.0)).astype(BF)

        def turned(block):
            a, b = block[: HD // 2], block[HD // 2 :]
            return jnp.concatenate([a * c - b * s, b * c + a * s], axis=0).astype(BF)

        for h in range(heads):
            top = h * 3 * HD
            q = turned(mixed[top : top + HD]).astype(F32) * SCALE
            k = turned(mixed[top + HD : top + 2 * HD])
            v = mixed[top + 2 * HD : top + 3 * HD].astype(BF)
            kf = k.astype(F32)
            q_t[h, :, at] = jnp.concatenate([q.astype(BF), ones_q, blank], axis=0)
            k_t[h, :, at] = k
            v_t[h, :, at] = jnp.concatenate([v, ones_q], axis=0)
            k_n[h, at, :] = jnp.concatenate([k, tail_k, blank], axis=0).T
            v_n[h, at, :] = jnp.concatenate([v, tail_v, blank], axis=0).T
            qn[h, :, at] = jnp.broadcast_to(jnp.sum(q * q, axis=0, keepdims=True), (8, rows))
            kn[h, :, at] = jnp.broadcast_to(jnp.sum(kf * kf, axis=0, keepdims=True), (8, rows))


def project(col, pos_a, pos_b, lengths, xs, packs, cos, sin, width):
    t = 4 * xs[0].shape[0]
    heads = width // (3 * HD)
    made = lambda n, dt=BF: jax.ShapeDtypeStruct((heads, n, t), dt)
    natural = jax.ShapeDtypeStruct((heads, t, 128), BF)
    return vmem_call(
        project_kernel,
        [made(128), made(HD), made(VAUG), natural, natural, made(8, F32), made(8, F32)],
        [pltpu.VMEM((D, width), BF), pltpu.VMEM((width, D), BF)],
        4 * t * D * width,
        "project",
        (col, pos_a, pos_b, lengths),
        *xs, *packs, in_hbm(cos), in_hbm(sin),
        mib=14,
    )


def attend_kernel(q_t, k_n, v_t, qn, kn, out, inverse, kept, q_s):
    n = k_n.shape[1]
    chunk = min(1024, n)
    bq = q_t.shape[2]
    q_s[...] = q_t[0]

    @pl.when(jnp.max(qn[0]) * jnp.max(kn[0]) > SAFE_SCORE * SAFE_SCORE)
    def _():
        best = jnp.full((1, bq), -jnp.inf, F32)
        for i in range(n // 256):
            s = mm(k_n[0, i * 256 : (i + 1) * 256, :], q_t[0], NN)
            best = jnp.maximum(best, jnp.max(s, axis=0, keepdims=True))
        high = best.astype(BF).astype(F32)
        low = (best - high).astype(BF).astype(F32)
        line = lax.broadcasted_iota(jnp.int32, (16, bq), 0)
        tail = jnp.where(line == 0, 1.0, jnp.where(line == 1, -high, jnp.where(line == 2, -low, 0.0)))
        q_s[HD : HD + 16, :] = tail.astype(BF)

    q = q_s[...]
    total = None
    for i in range(n // chunk):
        at = slice(i * chunk, (i + 1) * chunk)
        p = jnp.exp(mm(k_n[0, at, :], q, NN)).astype(BF)
        kept[0, at, :] = p
        part = mm(v_t[0, :, at], p, NN)
        total = part if total is None else total + part
    scale = 1.0 / total[HD : HD + 1]
    out[0] = (total[:HD] * scale).astype(BF)
    inverse[0] = jnp.broadcast_to(scale, inverse.shape[1:])


def attend(q_t, k_n, v_t, qn, kn, half):
    heads, _, t = q_t.shape
    bq = t // 2
    lane = lambda rows, at=half: pl.BlockSpec((1, rows, bq), lambda h: (h, 0, at))
    return pl.pallas_call(
        attend_kernel,
        grid=(heads,),
        in_specs=[
            lane(128),
            pl.BlockSpec((1, t, 128), lambda h: (h, 0, 0)),
            pl.BlockSpec((1, VAUG, t), lambda h: (h, 0, 0)),
            lane(8),
            pl.BlockSpec((1, 8, t), lambda h: (h, 0, 0)),
        ],
        out_specs=[lane(HD, 0), lane(8, 0), pl.BlockSpec((1, t, bq), lambda h: (h, 0, 0))],
        out_shape=[
            jax.ShapeDtypeStruct((heads, HD, bq), BF),
            jax.ShapeDtypeStruct((heads, 8, bq), F32),
            pltpu.HBM((heads, t, bq), BF),
        ],
        scratch_shapes=[pltpu.VMEM((128, bq), BF)],
        compiler_params=params(24),
        cost_estimate=cost(0, 0),
        name="attend",
    )(q_t, k_n, v_t, qn, kn)


def split3(value):
    a = value.astype(BF).astype(F32)
    b = (value - a).astype(BF).astype(F32)
    return a, b, value - a - b


def turn_back(grad, c, s):
    a, b = grad[: HD // 2], grad[HD // 2 :]
    return jnp.concatenate([a * c + b * s, b * c - a * s], axis=0)


def relative(table, col, first, count):
    rows = table.shape[1] // 4
    starts = [pl.multiple_of((i ^ col[0]) * rows, 128) for i in range(first, first + count)]
    return jnp.concatenate([table[:, pl.ds(at, rows)] for at in starts], axis=1)


def attend_back_kernel(first, col, kept, inverse, q_t, o_t, do_t, k_t, v_n, cos, sin, *refs):
    if first:
        dq, dk, dv, do_s = refs
    else:
        dk_in, dv_in, dq, dk, dv, do_s, dk_s = refs
    n = v_n.shape[1]
    chunk = min(512, n)
    bq = q_t.shape[2]
    line = lax.broadcasted_iota(jnp.int32, (16, bq), 0)
    do = do_t[0].astype(F32) * inverse[0, :1]
    a, b, c = split3(-jnp.sum(do * o_t[0].astype(F32), axis=0, keepdims=True))
    tail = jnp.where(line == 0, a, jnp.where(line == 1, b, jnp.where(line == 2, c, 0.0)))
    do_s[:HD, :] = do.astype(BF)
    do_s[HD : HD + 16, :] = tail.astype(BF)
    do_s[HD + 16 :, :] = jnp.zeros((48, bq), BF)
    do = do_s[...]
    do64, q64 = do_s[:HD, :], q_t[0, :HD, :]
    total = None
    for i in range(n // chunk):
        at = slice(i * chunk, (i + 1) * chunk)
        p = kept[0, at, :]
        gs = (p.astype(F32) * mm(v_n[0, at, :], do, NN)).astype(BF)
        part = mm(k_t[0, :, at], gs, NN)
        total = part if total is None else total + part
        gv = mm(do64, p, NT)
        gk = mm(q64, gs, NT)
        if first:
            dv[0, :, at] = gv
            dk[0, :, at] = gk
        else:
            dv[0, :, at] = (gv + dv_in[0, :, at]).astype(BF)
            dk_s[:, at] = gk + dk_in[0, :, at]
    near = 0 if first else 2
    dq[0] = turn_back(total * SCALE, relative(cos, col, near, 2), relative(sin, col, near, 2)).astype(BF)
    if not first:
        dk[0] = turn_back(dk_s[...], relative(cos, col, 0, 4), relative(sin, col, 0, 4)).astype(BF)


def attend_back(col, q_t, kept, inverse, o_t, do_t, k_t, v_n, cos, sin, half, sums=None):
    heads, _, t = q_t.shape
    bq = t // 2
    first = sums is None
    lane = lambda rows, at=0: pl.BlockSpec((1, rows, bq), lambda h, *_: (h, 0, at))
    full = lambda rows: pl.BlockSpec((1, rows, t), lambda h, *_: (h, 0, 0))
    tall = lambda lanes: pl.BlockSpec((1, t, lanes), lambda h, *_: (h, 0, 0))
    table = const_spec(cos)
    made = F32 if first else BF
    more = () if first else tuple(sums)
    return pl.pallas_call(
        functools.partial(attend_back_kernel, first),
        grid_spec=pltpu.PrefetchScalarGridSpec(
            num_scalar_prefetch=1,
            grid=(heads,),
            in_specs=[tall(bq), lane(8), lane(128, half), lane(HD), lane(HD), full(HD), tall(128), table, table]
            + ([] if first else [full(HD), full(HD)]),
            out_specs=[lane(HD), full(HD), full(HD)],
            scratch_shapes=[pltpu.VMEM((128, bq), BF)]
            + ([] if first else [pltpu.VMEM((HD, t), F32)]),
        ),
        out_shape=[
            jax.ShapeDtypeStruct((heads, HD, bq), BF),
            jax.ShapeDtypeStruct((heads, HD, t), made),
            jax.ShapeDtypeStruct((heads, HD, t), made),
        ],
        compiler_params=params(28),
        cost_estimate=cost(heads * 4 * 2 * bq * t * 256, heads * t * 2048),
        name="attend_back",
    )(col, in_hbm(kept), inverse, q_t, o_t, do_t, k_t, v_n, in_hbm(cos), in_hbm(sin), *more)


def fill_out(w, packs, other, pos_a, pos_b):
    width = w.shape[2]
    half = BLOCK // 2
    for k, src in enumerate(packs):
        part, pos, first = k // 2, (pos_a, pos_b)[k // 2], k % 2 * (ROWS // 2)
        fill(w.at[0], src, pos, part * half, half, 0, width, 0, slice(OUT_AT, OUT_AT + width), first)
        fill(w.at[1], other.at[pl.ds(part * ROWS + first, ROWS // 2)], pos, part * half, half, 0, width, 0, first=first)


def out_kernel(pos_a, pos_b, h_own, h_other, wa, wa2, wb, wb2, other, keep, send, w):
    fill_out(w, (wa, wa2, wb, wb2), other, pos_a, pos_b)
    rows = keep.shape[0]
    for part, out in ((1, send), (0, keep)):
        at = slice(part * rows, (part + 1) * rows)
        total = mm(h_own[:, at].T, w[0], NT) + mm(h_other[:, at].T, w[1], NT)
        out[...] = total.astype(out.dtype)


def out_back_kernel(
    pos_a, pos_b, ga_own, ga_own2, ga_near, ga_near2, sums, h_own, h_other, wa, wa2, wb, wb2, other,
    gh_own, gh_other, keep, send, sums_out, w, ga,
):
    fill_out(w, (wa, wa2, wb, wb2), other, pos_a, pos_b)
    rows = ga_own.shape[0]
    for k, ref in enumerate((ga_own, ga_own2, ga_near, ga_near2)):
        ga[k * rows : (k + 1) * rows] = ref[:rows]
    total = sums[...] + unride(ga_near2[rows:])
    sums_out[...] = total
    send[h_own.shape[0] :, :] = ride(total)
    for half, (h, gh, g) in enumerate(((h_own, gh_own, keep), (h_other, gh_other, send))):
        gh[...] = mm(w[half].T, ga[...], NT).astype(BF)
        g[: h.shape[0], :] = mm(h[...], ga[...], NN).astype(BF)


def const_spec(a):
    return pl.BlockSpec(a.shape, lambda i, *_: (0,) * len(a.shape))


def in_hbm(x):
    return pltpu.with_memory_space_constraint(x, pltpu.HBM)


def vmem_call(kernel, out_shape, scratch, work, name, scalars, *args, mib=10, hbm_out=()):
    out_shape = [pltpu.HBM(o.shape, o.dtype) if k in hbm_out else o for k, o in enumerate(out_shape)]
    nbytes = sum(math.prod(a.shape) * a.dtype.itemsize for a in list(args) + list(out_shape))
    return pl.pallas_call(
        kernel,
        grid_spec=pltpu.PrefetchScalarGridSpec(
            num_scalar_prefetch=len(scalars),
            grid=(1,),
            in_specs=[const_spec(a) for a in args],
            out_specs=[const_spec(a) for a in out_shape],
            scratch_shapes=scratch,
        ),
        out_shape=out_shape,
        compiler_params=params(mib),
        cost_estimate=cost(work, nbytes),
        name=name,
    )(*scalars, *args)


def out_project(pos_a, pos_b, h_own, h_other, packs, other):
    rows = h_own.shape[1] // 2
    width = h_own.shape[0]
    return vmem_call(
        out_kernel,
        [jax.ShapeDtypeStruct((rows, D), F32), jax.ShapeDtypeStruct((rows, D), BF)],
        [pltpu.VMEM((2, D, width), BF)],
        2 * 2 * rows * D * 2 * width,
        "out_project",
        (pos_a, pos_b),
        h_own, h_other, *packs, other,
    )


def out_back(pos_a, pos_b, gas, sums, h_own, h_other, packs, other):
    t = 4 * gas[0].shape[0]
    width = h_own.shape[0]
    gh = jax.ShapeDtypeStruct((width, t), BF)
    grad = jax.ShapeDtypeStruct((width, D), BF)
    return vmem_call(
        out_back_kernel,
        [gh, gh, grad, jax.ShapeDtypeStruct((width + RIDE, D), BF), jax.ShapeDtypeStruct((8, D), F32)],
        [pltpu.VMEM((2, D, width), BF), pltpu.VMEM((t, D), BF)],
        2 * 2 * t * D * 2 * width,
        "out_back",
        (pos_a, pos_b),
        *gas, sums, h_own, h_other, *packs, other,
    )


FF_STEPS = 3


def assemble_kernel(pos, *refs):
    a, b, (g, u, d) = refs[:4], refs[4:8], refs[8:]
    lanes = a[0].shape[2]
    half = BLOCK // 2
    for k in range(4):
        to, first = k // 2 * lanes, k % 2 * (ROWS // 2)
        fill(g, a[k], pos.at[0], 0, BLOCK, 0, lanes, to, first=first)
        fill(u, b[k], pos.at[1], 0, BLOCK, 0, lanes, to, first=first)
        fill(d, a[k], pos.at[0], 0, half, BLOCK, lanes, to, first=first)
        fill(d, b[k], pos.at[1], half, half, BLOCK, lanes, to, first=first)


def assemble(pos, a_own, a_near, b_own, b_near):
    made = jax.ShapeDtypeStruct((D, 2 * a_own[0].shape[2]), BF)
    refs = [in_hbm(x) for x in (*a_own, *a_near, *b_own, *b_near)]
    return vmem_call(
        assemble_kernel, [made] * 3, [], 6 * D * made.shape[1], "assemble", (pos,), *refs, mib=24
    )


def place_call(kernel, pos, given, base, outs, scratch, work, name):
    in_vmem = pl.BlockSpec(memory_space=pltpu.VMEM)
    nbytes = sum(math.prod(o.shape) * 4 for o in outs)
    return list(pl.pallas_call(
        kernel,
        in_specs=[pl.BlockSpec(memory_space=pltpu.SMEM)] + [in_vmem] * (len(given) + len(base)),
        out_specs=[in_vmem] * len(outs),
        out_shape=outs,
        scratch_shapes=scratch,
        input_output_aliases={1 + len(given) + k: k for k in range(len(base))},
        compiler_params=params(),
        cost_estimate=cost(work, nbytes),
        name=name,
    )(pos, *given, *base))


def steps(units):
    width = units // FF_STEPS
    return [slice(k * width, (k + 1) * width) for k in range(FF_STEPS)]


def ffn_kernel(x_own, x_far, wg, wu, wd, gate, up, keep, send, x):
    rows = x_own.shape[0]
    x[:rows] = x_own[...]
    x[rows:] = x_far[...]
    total = None
    for at in steps(wg.shape[1]):
        g = mm(x[...], wg[:, at], NN)
        u = mm(x[...], wu[:, at], NN)
        gate[:, at] = g.astype(BF)
        up[:, at] = u.astype(BF)
        part = mm((g * jax.nn.sigmoid(g) * u).astype(BF), wd[:, at], NT)
        total = part if total is None else total + part
    keep[...] = total[:rows].astype(BF)
    send[...] = total[rows:].astype(BF)


def ffn_back_kernel(gb_own, gb_far, wg, wu, wd, gate, up, hid, ggate, gup, keep, send, gb):
    rows = gb_own.shape[0]
    gb[:rows] = gb_own[...]
    gb[rows:] = gb_far[...]
    total = None
    for at in steps(wg.shape[1]):
        gh = mm(gb[...], wd[:, at], NN)
        g, u = gate[:, at].astype(F32), up[:, at].astype(F32)
        sig = jax.nn.sigmoid(g)
        silu = g * sig
        hid[:, at] = (silu * u).astype(BF)
        gga = (gh * u * sig * (1.0 + g * (1.0 - sig))).astype(BF)
        gua = (gh * silu).astype(BF)
        ggate[:, at] = gga
        gup[:, at] = gua
        part = mm(gga, wg[:, at], NT) + mm(gua, wu[:, at], NT)
        total = part if total is None else total + part
    keep[...] = total[:rows].astype(BF)
    send[...] = total[rows:].astype(BF)


def ffn_grad_kernel(n, which, pos, *refs):
    xs, acts = refs[: 2 * n], refs[2 * n : 3 * n]
    outs, (x_t, grad) = refs[-6 if which is None else -4 : -2], refs[-2:]
    rows = xs[0].shape[0]
    for k in range(2 * n):
        x_t[:, k * rows : (k + 1) * rows] = xs[k][...].T
    lanes = outs[0].shape[2]
    half = BLOCK // 2
    wide = grad.shape[1]

    def product(right, at):
        total = None
        for k in range(n):
            part = mm(x_t[:, 2 * k * rows : 2 * (k + 1) * rows], right[k][:, at], NN)
            total = part if total is None else total + part
        grad[...] = total

    def out(src_pos, dst, start, count, to, cols):
        for j in range(ROWS):
            place = pl.multiple_of(src_pos[j] * BLOCK + start, 16)
            dst[j, to : to + count, cols] = grad[pl.ds(place, count), :].astype(BF)

    for part in range(2):
        for lo in range(0, lanes, wide):
            cols, at = slice(lo, lo + wide), slice(part * lanes + lo, part * lanes + lo + wide)
            product(acts, at)
            if which is None:
                out(pos.at[0], outs[2 * part], 0, half, BLOCK, cols)
                out(pos.at[1], outs[2 * part + 1], half, half, BLOCK, cols)
            else:
                out(pos.at[which], outs[part], 0, BLOCK, 0, cols)


def ffn_grad(pos, xs, acts, which, lanes, base=()):
    n = len(acts)
    rows = xs[0].shape[0]
    blocks = jax.ShapeDtypeStruct((ROWS, BLOCK * 3 // 2, lanes), BF)
    kernel = functools.partial(ffn_grad_kernel, n, which)
    scratch = [pltpu.VMEM((D, 2 * n * rows), BF), pltpu.VMEM((D, lanes // 3), F32)]
    work = n * rows * D * lanes
    outs = [blocks] * (4 if which is None else 2)
    return place_call(kernel, pos, list(xs) + acts, base, outs, scratch, work, "ffn_grad")


def ffn(x_own, x_far, weights):
    rows = x_own.shape[0]
    units = weights[0].shape[1]
    acts = jax.ShapeDtypeStruct((2 * rows, units), BF)
    ends = [jax.ShapeDtypeStruct((rows, D), BF)] * 2
    scratch = [pltpu.VMEM((2 * rows, D), BF)]
    work = 12 * rows * D * units
    return vmem_call(
        ffn_kernel, [acts, acts] + ends, scratch, work, "ffn", (), x_own, x_far, *weights,
        hbm_out=(0, 1),
    )


def ffn_back(gb_own, gb_far, weights, gate, up):
    rows = gb_own.shape[0]
    units = weights[0].shape[1]
    acts = jax.ShapeDtypeStruct((2 * rows, units), BF)
    ends = [jax.ShapeDtypeStruct((rows, D), BF)] * 2
    scratch = [pltpu.VMEM((2 * rows, D), BF)]
    work = 12 * rows * D * units
    return vmem_call(
        ffn_back_kernel, [acts] * 3 + ends, scratch, work, "ffn_back", (), gb_own, gb_far, *weights, in_hbm(gate), in_hbm(up),
        mib=20,
    )


def units_of(h):
    centre = jnp.mean(h, axis=1, keepdims=True)
    away = h - centre
    scale = lax.rsqrt(jnp.mean(away * away, axis=1, keepdims=True) + NORM_EPSILON)
    return away * scale, scale


def back_through(grad, unit, scale, gain):
    scaled = grad * gain
    mean = jnp.mean(scaled, axis=1, keepdims=True)
    crossed = jnp.mean(scaled * unit, axis=1, keepdims=True)
    return scale * (scaled - mean - unit * crossed)


def columns(value):
    return jnp.sum(value, axis=0, keepdims=True)


def first_kernel(tokens, keep, came, norm, first, *refs):
    h = tokens[...].astype(F32) + keep[...] + came[...].astype(F32)
    first[...] = h
    unit, _ = units_of(h)
    normed = (unit * norm[0:1] + norm[1:2]).astype(BF)
    rows = refs[0].shape[0]
    for k, low in enumerate(refs):
        k = k % (len(refs) // 2)
        low[...] = normed[k * rows : (k + 1) * rows]


def norm_one(tokens, keep, came, norm, chunks):
    rows = tokens.shape[0]
    return vmem_call(
        first_kernel,
        [jax.ShapeDtypeStruct((rows, D), F32)] + [jax.ShapeDtypeStruct((rows // chunks, D), BF)] * 2 * chunks,
        [], 12 * rows * D, "first_norm", (), tokens, keep, came, norm, hbm_out=[0, *range(1 + chunks, 1 + 2 * chunks)],
    )


def second_kernel(place, first, cotangent, keep, came, norm, result, low, low_too, sums):
    rows = result.shape[0]
    i = pl.program_id(0)
    unit, _ = units_of(first[...])
    normed = unit * norm[0:1] + norm[1:2]
    unit, scale = units_of(normed + keep[...].astype(F32) + came[...].astype(F32))
    out = unit * norm[2:3] + norm[3:4]
    result[...] = out.astype(BF)
    position = place[0] + i * rows + lax.broadcasted_iota(jnp.int32, (rows, 1), 0)
    weight = (position < place[1]).astype(F32)
    g = cotangent[...].astype(F32) * weight
    back = back_through(g, unit, scale, norm[2:3]).astype(BF)
    low[...] = back
    low_too[...] = back
    part = jnp.concatenate(
        [jnp.zeros((2, D), F32), columns(g * unit), columns(g), columns(out * out * weight), jnp.zeros((3, D), F32)],
        axis=0,
    )

    @pl.when(i == 0)
    def _():
        sums[...] = part

    @pl.when(i > 0)
    def _():
        sums[...] += part


def norm_two(k, place, first, keep, came, cotangent, norm):
    rows = keep.shape[0]
    n = 2
    part = lambda at: pl.BlockSpec((rows // n, D), lambda i, *_: (at * n + i, 0))
    sums = jax.ShapeDtypeStruct((8, D), F32)
    return pl.pallas_call(
        second_kernel,
        grid_spec=pltpu.PrefetchScalarGridSpec(
            num_scalar_prefetch=1,
            grid=(n,),
            in_specs=[part(k), part(k), part(0), part(0), const_spec(norm)],
            out_specs=[part(0)] * 3 + [const_spec(sums)],
        ),
        out_shape=[pltpu.HBM((rows, D), BF), jax.ShapeDtypeStruct((rows, D), BF), pltpu.HBM((rows, D), BF), sums],
        compiler_params=params(),
        cost_estimate=cost(30 * rows * D, 12 * rows * D),
        name="second_norm",
    )(place, in_hbm(first), in_hbm(cotangent), keep, came, norm)


def chunk_call(kernel, k, chunked, whole, out_shape, name, work):
    rows = out_shape[0].shape[0]
    part = pl.BlockSpec((rows, D), lambda i: (k, 0))
    return pl.pallas_call(
        kernel,
        grid=(1,),
        in_specs=[part] * len(chunked) + [const_spec(a) for a in whole],
        out_specs=[const_spec(a) for a in out_shape],
        out_shape=out_shape,
        compiler_params=params(),
        cost_estimate=cost(work, 20 * rows * D),
        name=name,
    )(*chunked, *whole)


def first_back_kernel(n, first, second, keep, came, norm, *refs):
    prior, (grad, low, sums) = refs[:n], refs[n:]
    rows = grad.shape[0]
    unit, scale = units_of(first[...])
    g = second[...].astype(F32) + keep[...].astype(F32) + came[...].astype(F32)
    back = back_through(g, unit, scale, norm[0:1])
    grad[...] = back
    low[:rows] = back.astype(BF)
    total = jnp.concatenate([columns(g * unit), columns(g), jnp.zeros((6, D), F32)], axis=0)
    for ref in prior:
        total = total + ref[...]
    sums[...] = total
    if n:
        low[rows:] = ride(total)


def norm_one_back(k, first, second, keep, came, norm, prior=()):
    rows = keep.shape[0]
    more = RIDE if prior else 0
    outs = [
        jax.ShapeDtypeStruct((rows, D), F32),
        jax.ShapeDtypeStruct((rows + more, D), BF),
        jax.ShapeDtypeStruct((8, D), F32),
    ]
    return chunk_call(
        functools.partial(first_back_kernel, len(prior)), k, (first,), (second, keep, came, norm, *prior),
        outs, "first_norm_back", 20 * rows * D,
    )


def token_kernel(n, pos_a, pos_b, *refs):
    groups, refs = [refs[3 * k : 3 * k + 3] for k in range(n)], refs[3 * n :]
    packs, base, (near, far, w) = refs[:4], refs[4:-3], refs[-3:]
    fill_qkv(w, packs, pos_a, pos_b)
    rows = near.shape[0]
    for part, out in ((1, far), (0, near)):
        at = slice(part * rows, (part + 1) * rows)
        mixed = [ref[h, :, at] for group in groups for h in range(group[0].shape[0]) for ref in group]
        total = mm(jnp.concatenate(mixed, axis=0).T, w[...], NT)
        if part == 0 and base:
            total = total + jnp.concatenate([ref[...] for ref in base], axis=0)
        out[...] = total.astype(out.dtype)


def token_terms(pos_a, pos_b, groups, packs, half, base=()):
    bq = groups[0][0].shape[2]
    width = sum(g[0].shape[0] for g in groups) * 3 * HD
    lane = lambda a, at: pl.BlockSpec((a.shape[0], HD, bq), lambda i, *_: (0, 0, at))
    flat = [a for g in groups for a in g]
    out = [jax.ShapeDtypeStruct((bq // 2, D), kind) for kind in (F32, BF)]
    return pl.pallas_call(
        functools.partial(token_kernel, len(groups)),
        grid_spec=pltpu.PrefetchScalarGridSpec(
            num_scalar_prefetch=2,
            grid=(1,),
            in_specs=[lane(a, half if k % 3 else 0) for k, a in enumerate(flat)]
            + [const_spec(a) for a in (*packs, *base)],
            out_specs=[const_spec(a) for a in out],
            scratch_shapes=[pltpu.VMEM((D, width), BF)],
        ),
        out_shape=out,
        compiler_params=params(),
        cost_estimate=cost(2 * bq * D * width, bq * (D + width) * 4),
        name="token_terms",
    )(pos_a, pos_b, *flat, *packs, *base)


def total_kernel(keep, near, far, out):
    out[...] = keep[...] + near[...].astype(F32) + far[...].astype(F32)


def total_grad(keep, near, far):
    rows = keep.shape[0]
    part = pl.BlockSpec((rows // 4, D), lambda i: (i, 0))
    return pl.pallas_call(
        total_kernel,
        grid=(4,),
        in_specs=[part] * 3,
        out_specs=part,
        out_shape=jax.ShapeDtypeStruct((rows, D), F32),
        compiler_params=params(),
        cost_estimate=cost(2 * rows * D, 12 * rows * D),
        name="total_grad",
    )(keep, near, far)


def qkv_grad_kernel(n, pos_a, pos_b, *refs):
    groups, refs = [refs[4 * k : 4 * k + 4] for k in range(n)], refs[4 * n :]
    x0, x1, x2, x3, out_own, out_came, sums, a_k, b_k, a_s, b_s, sums_out, g, go = refs
    rows = x0.shape[0]
    total = None
    for k, x in enumerate((x0, x1, x2, x3)):
        at, to = slice(k * rows, (k + 1) * rows), slice(k % 2 * rows, (k % 2 + 1) * rows)
        mixed = []
        for *dqs, dk, dv in groups:
            for h in range(dk.shape[0]):
                mixed += [dqs[k // 2][h, :, to], dk[h, :, at], dv[h, :, at]]
        part = mm(jnp.concatenate(mixed, axis=0), x[...], NN)
        total = part if total is None else total + part
    g[...] = total.T
    half = BLOCK // 2
    width, out_width = g.shape[1], go.shape[1]
    go[...] = (out_own[...].astype(F32) + out_came[:out_width].astype(F32)).T
    total = sums[...] + unride(out_came[out_width:])
    sums_out[...] = total
    gap = jnp.zeros((half, OUT_AT - width), BF)
    for part, (pos, k, s) in enumerate(((pos_a, a_k, a_s), (pos_b, b_k, b_s))):
        for j in range(ROWS):
            at = pl.ds(pl.multiple_of(pos[j] * BLOCK + part * half, 16), half)
            piece = jnp.concatenate([g[at, :].astype(BF), gap, go[at, :].astype(BF)], axis=1)
            if j < ROWS // 2:
                k[j] = piece
            elif part:
                s[j - ROWS // 2] = piece
            else:
                s[(j - ROWS // 2) * half : (j - ROWS // 2 + 1) * half, :] = piece
    a_s[ROWS // 2 * half :, :D] = ride(total)
    a_s[ROWS // 2 * half :, D:] = jnp.zeros((RIDE, a_s.shape[1] - D), BF)


def qkv_grad(pos_a, pos_b, groups, xs, out_own, out_came, sums):
    out_width = out_own.shape[0]
    blocks = jax.ShapeDtypeStruct((ROWS // 2, BLOCK // 2, OUT_AT + out_width), BF)
    send = jax.ShapeDtypeStruct((ROWS // 2 * (BLOCK // 2) + RIDE, OUT_AT + out_width), BF)
    width = 3 * HD * sum(g[0].shape[0] for g in groups)
    return vmem_call(
        functools.partial(qkv_grad_kernel, len(groups)),
        [blocks, blocks, send, blocks, jax.ShapeDtypeStruct((8, D), F32)],
        [pltpu.VMEM((D, width), F32), pltpu.VMEM((D, out_width), F32)],
        8 * xs[0].shape[0] * D * width,
        "qkv_grad",
        (pos_a, pos_b),
        *[a for g in groups for a in g], *xs, out_own, out_came, sums,
    )


def adamw(weight, gradient, first_state, second_state, step_rate, decay_rate):
    first_new = FIRST_DECAY * first_state + (1.0 - FIRST_DECAY) * gradient
    second_new = SECOND_DECAY * second_state + (1.0 - SECOND_DECAY) * gradient * gradient
    first_hat = first_new / (1.0 - FIRST_DECAY**STEP)
    second_hat = second_new / (1.0 - SECOND_DECAY**STEP)
    weight_new = weight - step_rate * (
        first_hat / (jnp.sqrt(second_hat) + ADAM_EPSILON) + decay_rate * weight
    )
    return (weight_new, first_new, second_new)


RATE_MAIN = 2.0 / math.sqrt(D)
RATE_OUT = 2.0 / math.sqrt(D * 16 // SEQ)
RATE_DOWN = 2.0 / math.sqrt(FF)


def update(grad, states, outs, rate):
    w, m, v = (ref[...] for ref in states)
    new, first, second = adamw(w, grad, m, v, rate, MATRIX_DECAY)
    for ref, value in zip(outs, (new, first, second, new.astype(BF))):
        ref[...] = value


def gate_update_kernel(a, came, *refs):
    rows = refs[0].shape[0]
    update(a[0, :rows].astype(F32) + came[0, :rows].astype(F32), refs[:3], refs[3:], RATE_MAIN)


def ffn_update_kernel(a, b, a_came, b_came, *refs):
    states, outs = refs[:6], refs[6:]
    rows = states[0].shape[0]
    gb = b[0].astype(F32) + b_came[0].astype(F32)
    down = a[0, rows:].astype(F32) + a_came[0, rows:].astype(F32)
    update(gb[:rows], states[:3], outs[:4], RATE_MAIN)
    update(jnp.concatenate([down, gb[rows:]], axis=0), states[3:], outs[4:], RATE_DOWN)


def pack_update_kernel(a, b, came, sums, *refs):
    states, outs = refs[:9], refs[9:]
    rows = a.shape[1]
    ga = a[0].astype(F32) + came[:rows].astype(F32)
    gb = b[0].astype(F32) + came[rows + RIDE :].astype(F32)
    grad = jnp.concatenate([ga, gb], axis=0)
    width = states[0].shape[1]
    update(grad[:, :width], states[:3], outs[:4], RATE_MAIN)
    update(grad[:, OUT_AT:].T, states[3:6], outs[4:8], RATE_OUT)
    total = sums[...] + unride(came[rows : rows + RIDE, :D])
    w, m, v = (ref[...] for ref in states[6:])
    for ref, value in zip(outs[8:], adamw(w, total[:4], m, v, NORM_RATE, 0.0)):
        ref[...] = value
    outs[11][...] = jnp.broadcast_to(jnp.sum(total[4:5], axis=1, keepdims=True), outs[11].shape)


def updated(kernel, given, states, name, more=()):
    outs = []
    for w, _, _ in states:
        outs += [pltpu.HBM(w.shape, F32)] * 3 + [pltpu.HBM(w.shape, BF)]
    flat = [in_hbm(x) for state in states for x in state]
    work = sum(20 * math.prod(w.shape) for w, _, _ in states)
    rest = [x for state in more for x in state]
    for w, _, _ in more:
        outs += [jax.ShapeDtypeStruct(w.shape, F32)] * 3 + [jax.ShapeDtypeStruct((8, 128), F32)]
    return list(vmem_call(kernel, outs, [], work, name, (), *given, *flat, *rest))


def rope_tables(length):
    position = np.arange(length, dtype=np.float32)
    inverse = np.exp(np.arange(HD // 2, dtype=np.float32) * np.float32(-2.0 * math.log(ROPE_BASE) / HD))
    angle = (inverse.astype(np.float32)[:, None] * position[None, :]).astype(np.float64)
    return np.cos(angle).astype(np.float32), np.sin(angle).astype(np.float32)


def on_device(
    tokens, cotangent, lengths, w_qkv, w_out, w_gate, w_up, w_down, norm_params,
    m_qkv, v_qkv, m_out, v_out, m_gate, v_gate, m_up, v_up, m_down, v_down, m_norm, v_norm,
):
    own_rows = tokens.shape[0]
    seq_rows = own_rows * lax.axis_size("col")
    col = lax.axis_index("col").astype(jnp.int32)
    row = lax.axis_index("row").astype(jnp.int32)
    small = lax.axis_size("row") == ROWS
    me = row if small else row * 0
    qkv_width = w_qkv.shape[1]
    head_width = qkv_width // 3
    heads = head_width // HD
    half = BLOCK // 2
    chunks = 2

    places = lambda order: jnp.stack([me ^ row_mask(order, j) for j in range(ROWS)])
    pos_a, pos_b = places(ORDER_QA), places(ORDER_QB)
    pos_f = jnp.stack([places(ORDER_A), places(ORDER_B)])
    pos_r = jnp.stack([places(BACK_A), places(BACK_B)])

    near = swap(tokens, "c")
    far = swap(tokens, "y")
    if small:
        part = (BLOCK + half, w_gate.shape[1])
        shapes = [jax.ShapeDtypeStruct(n, BF) for n in ((BLOCK, OUT_AT + head_width), part, part)]
        given = [in_hbm(w) for w in (w_qkv, w_out, w_gate, w_up, w_down.T)]
        pack, fa, fb = vmem_call(pack_kernel, shapes, [], 0, "pack", (), *given)
        pack, fa, fb = pack[None], fa[None], fb[None]
        pack_came, fa, fb = tie(swap(pack, "1"), fa, fb)
        ff_came = swap(fa, "1"), swap(fb, "1")
        both = jnp.concatenate([pack, pack_came], axis=0)
        qa, qb = both[:, :half], both[:, half:]
        came = swap(qa, "x"), swap(qb, "0")
        qa_came, qb_came, near, far = tie(*came, near, far)
        qa, qb = jnp.concatenate([qa, qa_came], axis=0), jnp.concatenate([qb, qb_came], axis=0)
        came = swap(qa, "0"), swap(qb, "x")
        fa, fb = jnp.concatenate([fa, ff_came[0]], axis=0), jnp.concatenate([fb, ff_came[1]], axis=0)
        fa, fb, *came = tie(fa, fb, *came)
        packs = (qa, came[0], qb, came[1])
        ff_came = swap(fa, "x"), swap(fb, "0")
    else:
        gap = jnp.zeros((w_qkv.shape[0], OUT_AT - qkv_width), BF)
        pack = jnp.concatenate([w_qkv.astype(BF), gap, w_out.T.astype(BF)], axis=1)
        low_down = w_down.T.astype(BF)
        low_gate, low_up = w_gate.astype(BF), w_up.astype(BF)
        wa = gather_plain(pack, ORDER_QA, 0, half)
        wb = gather_plain(pack, ORDER_QB, half, half)
        packs = (wa[: ROWS // 2], wa[ROWS // 2 :], wb[: ROWS // 2], wb[ROWS // 2 :])
        join = lambda w, order, start: jnp.concatenate(
            [gather_plain(w, order, 0, BLOCK), gather_plain(low_down, order, start, half)], axis=1
        )
        fa, fb = join(low_gate, ORDER_A, 0), join(low_up, ORDER_B, half)
        fa, fb, fa2, fb2 = fa[: ROWS // 2], fb[: ROWS // 2], fa[ROWS // 2 :], fb[ROWS // 2 :]
    far_near = swap(far, "c")
    blocks = (tokens, near, far, far_near)

    cos_np, sin_np = rope_tables(seq_rows)
    cos, sin = jnp.asarray(cos_np), jnp.asarray(sin_np)
    q_t, k_t, v_t, k_n, v_n, qn, kn = project(
        col[None], pos_a, pos_b, lengths, blocks, packs, cos, sin, qkv_width
    )
    wo_far = swap(jnp.concatenate([p[:, :, OUT_AT:] for p in packs], axis=0), "y")
    if small:
        fa_came, fb_came, q_t = tie(*ff_came, q_t)
        fa, fb = jnp.concatenate([fa, fa_came], axis=0), jnp.concatenate([fb, fb_came], axis=0)
        fa, fb, q_t = tie(fa, fb, q_t)
        fa2, fb2 = swap(fa, "0"), swap(fb, "x")
    far_heads, far_inv, far_kept = attend(q_t, k_n, v_t, qn, kn, 1)
    if small:
        far_heads, q_t = tie(far_heads, q_t)
    fa_c, fb_c = swap(fa, "c"), swap(fb, "c")
    if small:
        far_heads, wo_far = tie(far_heads, wo_far)
    other_heads = swap(far_heads.reshape(head_width, seq_rows // 2), "y")
    own_heads, own_inv, own_kept = attend(q_t, k_n, v_t, qn, kn, 0)
    flat_heads = own_heads.reshape(head_width, seq_rows // 2)
    if small:
        flat_heads, other_heads, fa2, fb2 = tie(flat_heads, other_heads, fa2, fb2)

    keep, send = out_project(pos_a, pos_b, flat_heads, other_heads, packs, wo_far)
    first, *normed = norm_one(tokens, keep, swap(send, "c"), norm_params, chunks)
    fa2_c, fb2_c = swap(fa2, "c"), swap(fb2, "c")
    weights = assemble(pos_f, (fa, fa2), (fa_c, fa2_c), (fb, fb2), (fb_c, fb2_c))
    weights = list(weights)
    normed_far = [swap(normed[0], "y")]
    for k in range(1, chunks):
        normed_far[-1], normed[k], weights[0] = tie(normed_far[-1], normed[k], weights[0])
        normed_far.append(swap(normed[k], "y"))
    normed = normed[chunks:]
    place = lambda k: jnp.stack([col * own_rows + k * (own_rows // chunks), lengths[0]])
    fwd, sums, results, lows, lows_far = [], [], [], [], []
    for k in range(chunks):
        fwd.append(ffn(normed[k], normed_far[k], weights))
    came = [swap(f[3], "y") for f in fwd]
    for k in range(chunks):
        result, low_send, low, part = norm_two(
            k, place(k), first, fwd[k][2], came[k], cotangent, norm_params
        )
        results.append(result)
        lows.append(low)
        lows_far.append(swap(low_send, "y"))
        sums.append(part)
    back = [ffn_back(lows[k], lows_far[k], weights, fwd[k][0], fwd[k][1]) for k in range(chunks)]
    came = [swap(b[4], "y") for b in back]
    pairs = lambda a, b: [v for ab in zip(a, b) for v in ab]
    spread = lambda t: [back[k][t] for k in range(chunks)]
    down = ffn_grad(pos_r, pairs(lows, lows_far), spread(0), None, w_gate.shape[1])
    xs = pairs(normed, normed_far)
    if small:
        came[0], xs[0] = tie(came[0], xs[0])
    gate_grad = ffn_grad(pos_r, xs, spread(1), 0, w_gate.shape[1], down[::2])
    if small:
        came[1], xs[0] = tie(came[1], xs[0])
    up_grad = ffn_grad(pos_r, xs, spread(2), 1, w_gate.shape[1], down[1::2])
    (ak, as_), (bk, bs) = gate_grad, up_grad
    firsts, ga = [], []
    (ak, bk), (as_, bs) = fold((ak, bk), (swap(as_, "c"), swap(bs, "c")))
    for k in range(chunks):
        if small and k == chunks - 1:
            ak, bk, as_, bs, came[k] = tie(ak, bk, as_, bs, came[k])
        prior = sums if k == chunks - 1 else ()
        grad, low, part = norm_one_back(k, first, lows[k], back[k][3], came[k], norm_params, prior)
        firsts.append(grad)
        ga.append(low)
        sums = sums + [part]
    own_sums = sums[-1]
    ga += [swap(low, "c") for low in ga]
    gh_own, gh_other, go_own, go_other, sums = out_back(
        pos_a, pos_b, ga, own_sums, flat_heads, other_heads, packs, wo_far
    )
    gh_far = swap(gh_other, "y")
    go_came = swap(go_other, "y")
    shaped = lambda a: a.reshape(heads, HD, seq_rows // 2)
    back = lambda rows, half, sums=None: attend_back(col[None], q_t, *rows, k_t, v_n, cos, sin, half, sums)
    if small:
        came = swap(as_, "0"), swap(bs, "x")
    dq0, dk, dv = back((own_kept, own_inv, own_heads, shaped(gh_own)), 0)
    if small:
        *came, dq0 = tie(*came, dq0)
        (ak, bk), (as_, bs) = fold((ak, bk), came)
        as_, bs, dk = tie(as_, bs, dk)
        ff_came = swap(as_, "x"), swap(bs, "1")
    dq0, dk, go_came, gh_far = tie(dq0, dk, go_came, gh_far)
    dq1, dk, dv = back((far_kept, far_inv, far_heads, shaped(gh_far)), 1, (dk, dv))
    groups = ((dq0, dq1, dk, dv),)
    qa, qb, qa_s, qb_s, sums = qkv_grad(pos_a, pos_b, groups, blocks, go_own, go_came, sums)
    qa_s, qb_s, dq1 = tie(qa_s, qb_s, dq1)
    if small:
        came = swap(qa_s, "0"), swap(qb_s, "x")
        *ff_came, dq1 = tie(*ff_came, dq1)
        (ak, bk), (as_, bs) = fold((ak, bk), ff_came)
        as_, bs, dq1 = tie(as_, bs, dq1)
        ff_came = swap(as_, "1"), swap(bs, "0")
    f_keep, f_send = token_terms(pos_a, pos_b, ((dq1, dk, dv),), packs, 1)
    f_came = swap(f_send, "c")
    f_came, dq0 = tie(f_came, dq0)
    from_far = swap((f_keep + f_came.astype(F32)).astype(BF), "y")
    n_keep, n_send = token_terms(pos_a, pos_b, ((dq0, dk, dv),), packs, 0, firsts)
    near_came = swap(n_send, "c")
    turned = lambda *arrays: tuple(x.T for x in arrays)
    ff_states = ((w_gate, m_gate, v_gate), (w_up, m_up, v_up), turned(w_down, m_down, v_down))
    pack_states = ((w_qkv, m_qkv, v_qkv), (w_out, m_out, v_out))
    norm_states = (norm_params, m_norm, v_norm)
    all_cells = float(own_rows * lax.axis_size("row") * lax.axis_size("col") * D)
    if small:
        qa, qb, qa_s, qb_s, sums = fold_sums(qa, qb, *came, sums)
        came = swap(qa_s, "x"), swap(qb_s, "0")
        qa, qb, qa_s, qb_s, sums = fold_sums(qa, qb, *came, sums)
        came = swap(jnp.concatenate([qa_s, qb_s[0]], axis=0), "1")
        grad_tokens = total_grad(n_keep, near_came, from_far)
        a_came, grad_tokens = tie(ff_came[0], grad_tokens)
        ff_new = updated(gate_update_kernel, (ak, a_came), ff_states[:1], "gate_update")
        b_came, ff_new[0] = tie(ff_came[1], ff_new[0])
        ff_new += updated(ffn_update_kernel, (ak, bk, a_came, b_came), ff_states[1:], "ffn_update")
        came, grad_tokens, ff_new[4] = tie(came, grad_tokens, ff_new[4])
        *pack_new, squares = updated(
            pack_update_kernel, (qa, qb, came, sums), pack_states, "pack_update", (norm_states,)
        )
        pack_new, new_norm = pack_new[:8], pack_new[8:]
        squares = squares[0, 0]
    else:
        sums = lax.psum(own_sums, ("row", "col"))
        new_norm = adamw(norm_params, sums[:4], m_norm, v_norm, NORM_RATE, 0.0)
        squares = jnp.sum(sums[4])
        ga, gb = jnp.concatenate([ak, as_]), jnp.concatenate([bk, bs])
        own_down = ungather_plain([(BACK_A, ga[:, BLOCK:]), (BACK_B, gb[:, BLOCK:])])
        own_pack = ungather_plain([
            (ORDER_QA, jnp.concatenate([qa, qa_s[: ROWS // 2 * half].reshape(qa.shape)])),
            (ORDER_QB, jnp.concatenate([qb, qb_s])),
        ])
        ff_new, pack_new = [], []
        for new, grad, state, rate in (
            (ff_new, ungather_plain([(BACK_A, ga[:, :BLOCK])]), ff_states[0], RATE_MAIN),
            (ff_new, ungather_plain([(BACK_B, gb[:, :BLOCK])]), ff_states[1], RATE_MAIN),
            (ff_new, own_down, ff_states[2], RATE_DOWN),
            (pack_new, own_pack[:, :qkv_width], pack_states[0], RATE_MAIN),
            (pack_new, own_pack[:, OUT_AT:].T, pack_states[1], RATE_OUT),
        ):
            three = adamw(state[0], grad, state[1], state[2], rate, MATRIX_DECAY)
            new += [*three, three[0].astype(BF)]
    ff_new = [*ff_new[:8], *turned(*ff_new[8:])]
    if not small:
        grad_tokens = total_grad(n_keep, near_came, from_far)
    residual_rms = jnp.sqrt(squares / all_cells)
    result = jnp.concatenate(results, axis=0)
    return (result, grad_tokens, residual_rms, *pack_new, *ff_new, *new_norm)


def solution(mesh):
    tokens, wide, tall, full = P(("row", "col"), None), P("row", "col"), P("col", "row"), P()
    return jax.shard_map(
        on_device,
        mesh=mesh,
        in_specs=(tokens, tokens, P("row"), wide, tall, wide, wide, tall, full)
        + (wide, wide, tall, tall, wide, wide, wide, wide, tall, tall, full, full),
        out_specs=(tokens, tokens, full)
        + (wide,) * 4 + (tall,) * 4 + (wide,) * 8 + (tall,) * 4 + (full,) * 3,
        check_vma=False,
    )
```
